32 devices in a mesh: loc: 32 (over z, y, x, core).
Axes of the slice: x: 2, y: 2, z: 4, core: 2. Of those that a mesh axis runs over, the one named last changes fastest.
Arguments:
- points: float32 [3, 32768], P(None, 'loc'), may hold values from -1 to 1, as said below
- right_sides: float32 [16, 32768], P(None, 'loc')
- skeleton: int32 [4, 8192], P(None, 'loc'), may hold values from 0 to 1023, as said below
- lengthscale: float32 [1], replicated, may hold values from 0.10606602 to 0.26516503
- far_length: float32 [1], replicated, may hold values from 0.4 to 1
- signal: float32 [1], replicated, may hold values from 0.00024414062 to 0.0009765625
- noise_var: float32 [1], replicated, may hold values from 0.5 to 2
Outputs:
- solution: float32 [16, 32768], P(None, 'loc')
- residual: float32 [16, 32768], P(None, 'loc')
- slope_image: float32 [16, 32768], P(None, 'loc')
- trace_terms: float32 [16], replicated
The draws below stay inside these ranges and needn't reach their ends.
Inputs may be any that keep to these rules, and one draw needn't show every extreme that they name: `points`: unit vectors. `skeleton`: each leaf's 256 entries of a level rise, the j-th in the range j*1024/256 to (j+1)*1024/256 - 1.
All inputs are finite; a program needn't handle non-finite values.
Results may differ from the reference program's by a relative error of at most 0.002.
Values may be sent and summed in bfloat16 or wider, within the bound.
No kernel may reach another device: no remote copies, remote signals or barrier semaphores. Data moves between devices by JAX's collectives and lax.ppermute only.
A program may use at most 64 MiB of HBM per device.

```python
import math
import jax
import jax.numpy as jnp
from jax import lax

ROWS = 1024
R = 256
PROBES = 16
ITERS = 2
NPTS = 32768
LEVELS = 4


def hilbert_cells(cell_ids, curve_order):
    column = jnp.zeros_like(cell_ids)
    row_pos = jnp.zeros_like(cell_ids)
    remain = cell_ids
    for level_id in range(curve_order):
        extent = 2 ** level_id
        flip_x = remain // 2 & 1
        flip_y = (remain ^ flip_x) & 1
        rotate = flip_y == 0
        mirror = rotate & (flip_x == 1)
        column_m = jnp.where(mirror, extent - 1 - column, column)
        row_m = jnp.where(mirror, extent - 1 - row_pos, row_pos)
        column = jnp.where(rotate, row_m, column_m) + extent * flip_x
        row_pos = jnp.where(rotate, column_m, row_m) + extent * flip_y
        remain = remain // 4
    return (column, row_pos)


def sphere_points(key):
    total_bits = NPTS.bit_length() - 1
    curve_order = (total_bits - 3) // 2
    side_cells = 2 ** curve_order
    point_ids = jnp.arange(NPTS, dtype=jnp.int32)
    cell_ids = point_ids // 2 ** (total_bits - 2 * curve_order)
    column, row_pos = hilbert_cells(cell_ids, curve_order)
    jitter = jax.random.uniform(key, (2, NPTS), jnp.float32)
    longitude = 2.0 * math.pi * (column.astype(jnp.float32) + jitter[0]) / side_cells - math.pi
    height = 2.0 * (row_pos.astype(jnp.float32) + jitter[1]) / side_cells - 1.0
    planar = jnp.sqrt(jnp.maximum(1.0 - height * height, 0.0))
    return jnp.stack([planar * jnp.cos(longitude), planar * jnp.sin(longitude), height])


def draw_points(key, part):
    return sphere_points(jax.random.fold_in(key, 11))


def draw_right_sides(key, part):
    locations = sphere_points(jax.random.fold_in(key, 11))
    keys_list = jax.random.split(jax.random.fold_in(key, 23), 4)
    rough = jnp.clip(jax.random.normal(keys_list[0], (PROBES, NPTS), jnp.float32), -4.0, 4.0)
    probe_scale = jnp.exp(jax.random.uniform(keys_list[1], (PROBES, 1), jnp.float32, 0.0, math.log(3.0)))
    smooth_weight = 2.0
    cell_scale = jnp.exp(jax.random.uniform(keys_list[2], (1, NPTS), jnp.float32, math.log(0.3), math.log(3.0)))
    tilts = jax.random.uniform(keys_list[3], (PROBES, 3), jnp.float32, -0.5, 0.5)
    smooth = 1.5 + tilts[:, 0:1] * locations[0][None, :] + tilts[:, 1:2] * locations[1][None, :] + tilts[:, 2:3] * locations[2][None, :]
    return probe_scale * (0.5 * cell_scale * rough + smooth_weight * smooth)


def draw_skeleton(key, part):
    stride = ROWS // R
    leaf_count = NPTS // ROWS
    offsets = jax.random.randint(key, (LEVELS, leaf_count, R), 0, stride, dtype=jnp.int32)
    starts = jnp.arange(R, dtype=jnp.int32) * stride
    return (starts[None, None, :] + offsets).reshape(LEVELS, leaf_count * R)


def setup_inputs(seed: int = 0) -> dict:
    streams_of = jax.random.split(jax.random.key(seed), 8)
    points = draw_points(jax.random.fold_in(streams_of[7], 71), 0)
    right_sides = draw_right_sides(jax.random.fold_in(streams_of[7], 71), 0)
    skeleton = draw_skeleton(jax.random.fold_in(streams_of[7], 71), 0)
    lengthscale = jnp.clip(jnp.exp(jax.random.uniform(streams_of[3], (1,), jnp.float32, math.log(0.10606602), math.log(0.26516503))), 0.10606602, 0.26516503)
    far_length = jnp.clip(jnp.exp(jax.random.uniform(streams_of[4], (1,), jnp.float32, math.log(0.4), math.log(1.0))), 0.4, 1.0)
    signal = jnp.clip(jnp.exp(jax.random.uniform(streams_of[5], (1,), jnp.float32, math.log(0.00024414062), math.log(0.0009765625))), 0.00024414062, 0.0009765625)
    noise_var = jnp.clip(jnp.exp(jax.random.uniform(streams_of[6], (1,), jnp.float32, math.log(0.5), math.log(2.0))), 0.5, 2.0)
    return {"points": points, "right_sides": right_sides, "skeleton": skeleton, "lengthscale": lengthscale, "far_length": far_length, "signal": signal, "noise_var": noise_var}


root_three = 1.7320508075688772

def kernel_pair(row_pts, col_pts, length):
    diff_a = row_pts[0][:, None] - col_pts[0][None, :]
    diff_b = row_pts[1][:, None] - col_pts[1][None, :]
    diff_c = row_pts[2][:, None] - col_pts[2][None, :]
    radius = jnp.sqrt(diff_a * diff_a + diff_b * diff_b + diff_c * diff_c)
    scaled = root_three * radius / length
    decay = jnp.exp(-scaled)
    return ((1.0 + scaled) * decay, scaled * scaled * decay)

def contract_rows(vectors, matrix):
    return lax.dot_general(vectors, matrix, (((1,), (1,)), ((), ())), preferred_element_type=jnp.float32)

def reference(points, right_sides, skeleton, lengthscale, far_length, signal, noise_var):
    length = lengthscale[0]
    far_len = far_length[0]
    signal_var = signal[0]
    nugget = noise_var[0]
    leaf_count = NPTS // ROWS
    leaf_pts = points.reshape(3, leaf_count, ROWS).transpose(1, 0, 2)
    blank_pts = jnp.zeros((1, 3, ROWS), jnp.float32)
    padded_pts = jnp.concatenate([blank_pts, leaf_pts, blank_pts], axis=0)
    skel_idx = skeleton.reshape(LEVELS, leaf_count, R)
    own_skel = []
    for level_id in range(LEVELS):
        picks = jnp.broadcast_to(skel_idx[level_id][:, None, :], (leaf_count, 3, R))
        own_skel.append(jnp.take_along_axis(leaf_pts, picks, axis=2))
    far_scale = 1.0 / (R * R * LEVELS)

    def apply_kernel(vectors, slope_rows):
        vec_count = vectors.shape[0]
        vec_half = vectors.astype(jnp.bfloat16)
        leaf_half = vec_half.reshape(vec_count, leaf_count, ROWS).transpose(1, 0, 2)
        blank_half = jnp.zeros((1, vec_count, ROWS), jnp.bfloat16)
        padded_half = jnp.concatenate([blank_half, leaf_half, blank_half], axis=0)

        def coef_leaf(leaf_id):
            coef_list = []
            for level_id in range(LEVELS):
                basis = kernel_pair(own_skel[level_id][leaf_id], leaf_pts[leaf_id], far_len)[0].astype(jnp.bfloat16)
                coef_list.append(contract_rows(leaf_half[leaf_id], basis))
            return jnp.stack(coef_list)
        coefs = lax.map(coef_leaf, jnp.arange(leaf_count, dtype=jnp.int32))

        def image_leaf(leaf_id):
            own_pts = leaf_pts[leaf_id]
            far_sum = jnp.zeros((vec_count, ROWS), jnp.float32)
            for level_id in range(LEVELS):
                partner_id = jnp.bitwise_xor(leaf_id, 1 << level_id + 1)
                basis = kernel_pair(own_skel[level_id][leaf_id], own_pts, far_len)[0].astype(jnp.bfloat16)
                coupling = kernel_pair(own_skel[level_id][partner_id], own_skel[level_id][leaf_id], far_len)[0]
                mixed_half = jnp.dot(coefs[partner_id, level_id], coupling, precision=lax.Precision.HIGHEST).astype(jnp.bfloat16)
                far_sum = far_sum + jnp.dot(mixed_half, basis, preferred_element_type=jnp.float32)
            near_sum = jnp.zeros((vec_count, ROWS), jnp.float32)
            slope_acc = jnp.zeros((max(slope_rows, 1), ROWS), jnp.float32)
            for offset in range(3):
                col_pts = padded_pts[leaf_id + offset]
                col_half = padded_half[leaf_id + offset]
                kernel_vals, slope_vals = kernel_pair(own_pts, col_pts, length)
                near_sum = near_sum + contract_rows(col_half, kernel_vals.astype(jnp.bfloat16))
                if slope_rows > 0:
                    slope_acc = slope_acc + contract_rows(col_half[:slope_rows], slope_vals.astype(jnp.bfloat16))
            return (near_sum + far_scale * far_sum, slope_acc)
        images, slopes = lax.map(image_leaf, jnp.arange(leaf_count, dtype=jnp.int32))
        images = images.transpose(1, 0, 2).reshape(vec_count, NPTS)
        slopes = slopes.transpose(1, 0, 2).reshape(slopes.shape[1], NPTS)
        return (images, slopes)
    ones_row = jnp.ones((1, NPTS), jnp.float32)
    first_out, slope_raw = apply_kernel(jnp.concatenate([right_sides, ones_row], axis=0), PROBES)
    row_sums = first_out[PROBES:]
    slope_image = signal_var * slope_raw

    def operate(vectors, kernel_part):
        return nugget * vectors + signal_var * (kernel_part + row_sums * vectors)
    image = operate(right_sides, first_out[:PROBES])
    solution = jnp.zeros_like(right_sides)
    residual = right_sides
    direction = right_sides
    norm_now = lax.optimization_barrier(jnp.sum(residual * residual, axis=1))
    for sweep in range(ITERS):
        if sweep > 0:
            image = operate(direction, apply_kernel(direction, 0)[0])
        alpha = norm_now / lax.optimization_barrier(jnp.sum(direction * image, axis=1))
        solution = solution + alpha[:, None] * direction
        residual = residual - alpha[:, None] * image
        norm_next = lax.optimization_barrier(jnp.sum(residual * residual, axis=1))
        direction = residual + (norm_next / norm_now)[:, None] * direction
        norm_now = norm_next
    trace_terms = lax.optimization_barrier(jnp.sum(solution * slope_image, axis=1)) / NPTS
    return (solution, residual, slope_image, trace_terms)
```

```python
import functools

import jax
import jax.numpy as jnp
from jax import lax
from jax.experimental import pallas as pl
from jax.experimental.pallas import tpu as pltpu
from jax.sharding import PartitionSpec as P

HALF = jnp.bfloat16
FULL = jnp.float32
LOG2_E = 1.4426950408889634
LN_2 = 0.6931471805599453
TINY = 1e-30
VEC_ROWS = 32
SRC_ROWS = 32
MSG_ROWS = 48
TILE = 256
VMEM = pltpu.VMEM
SMEM = pltpu.SMEM


def split_two(value):
    high = value.astype(HALF)
    low = (value - high.astype(FULL)).astype(HALF)
    return high, low


def split_three(value):
    first = value.astype(HALF).astype(FULL)
    rest = value - first
    second = rest.astype(HALF).astype(FULL)
    third = (rest - second).astype(HALF).astype(FULL)
    return first, second, third


def matern(squared):
    squared = jnp.maximum(squared, TINY)
    scaled = squared * lax.rsqrt(squared)
    decay = jnp.exp2(-scaled)
    return squared, decay, decay + (LN_2 * scaled) * decay


def source_rows(buf, base, pts):
    one, two, three = split_three(pts)
    for slot, piece in enumerate((one, one, two, two, one, three)):
        buf[base + 1 + 3 * slot : base + 4 + 3 * slot, :] = piece
    size = jnp.sum(pts * pts, axis=0, keepdims=True)
    one, two, three = split_three(size)
    for slot, piece in enumerate((one, one, two, two, one, three)):
        buf[base + 19 + slot : base + 20 + slot, :] = piece
    unit = jnp.ones_like(size)
    buf[base : base + 1, :] = unit
    buf[base + 25 : base + 26, :] = unit
    buf[base + 26 : base + 27, :] = unit
    buf[base + 27 : base + 32, :] = jnp.zeros((5, size.shape[1]), FULL)


def target_rows(buf, pts, length):
    size = jnp.sum(pts * pts, axis=0, keepdims=True)
    reach = jnp.full_like(size, length)
    scale = (3.0 * LOG2_E * LOG2_E) / (reach * reach)
    one, two, three = split_three(pts * (-2.0 * scale))
    for slot, piece in enumerate((one, two, one, two, three, one)):
        buf[1 + 3 * slot : 4 + 3 * slot, :] = piece
    one, two, three = split_three(scale)
    for slot, piece in enumerate((one, two, one, two, three, one)):
        buf[19 + slot : 20 + slot, :] = piece
    one, two, three = split_three(scale * size)
    buf[0:1, :] = one
    buf[25:26, :] = two
    buf[26:27, :] = three
    buf[27:32, :] = jnp.zeros((5, size.shape[1]), FULL)


def dot(a, b):
    return jnp.dot(a, b, preferred_element_type=FULL)


def dot_rows(a, b):
    return lax.dot_general(a, b, (((1,), (1,)), ((), ())), preferred_element_type=FULL)


def turned(value):
    return value.astype(FULL).T.astype(HALF)


def front_kernel(levels, *refs):
    length, far_length, pts, rhs, skel = refs[:5]
    msg, target, basis, skel_target = refs[5:9]
    lev = refs[9 : 9 + levels]
    buf, far_buf, pair_buf = refs[9 + levels :]
    points = pts[...]
    buf[0:16, :] = rhs[...]
    source_rows(buf, 16, points)
    msg[...] = buf[...].astype(HALF)
    target_rows(far_buf, points, length[0])
    target[...] = far_buf[...].astype(HALF)
    target_rows(far_buf, points, far_length[0])
    pair_buf[0:SRC_ROWS, :] = msg[16:48, :]
    pair_buf[SRC_ROWS:, :] = far_buf[...].astype(HALF)
    rows, rank = pts.shape[1], skel.shape[1]
    vecs = msg[0:VEC_ROWS, :]
    for level in range(levels):
        spot = lax.broadcasted_iota(jnp.int32, (rows, rank), 0)
        picks = jnp.where(spot == skel[level : level + 1, :], 1.0, 0.0).astype(HALF)
        both = dot(pair_buf[...], picks)
        skel_target[level] = both[SRC_ROWS:].astype(HALF)
        skel_source = both[:SRC_ROWS]
        squared = dot(skel_source.T.astype(HALF), pair_buf[SRC_ROWS:, :])
        block = matern(squared)[2].astype(HALF)
        basis[level] = block
        high, low = split_two(dot_rows(vecs, block))
        lev[level][0:32, :] = high
        lev[level][32:64, :] = low
        lev[level][64:96, :] = skel_source.astype(HALF)


def near_block(msg, target, turned_src, kept, image, slopes, first):
    rows = target.shape[1]
    turned_src[...] = turned(msg[16:48, :])

    def strip(index, carry):
        start = pl.multiple_of(index * TILE, TILE)
        vecs = msg[0:VEC_ROWS, pl.ds(start, TILE)]
        for col in range(0, rows, TILE):
            squared = dot(turned_src[pl.ds(start, TILE), :], target[:, col : col + TILE])
            squared, decay, value = matern(squared)
            value = value.astype(HALF)
            slope = (squared * decay).astype(HALF)
            kept[pl.ds(start, TILE), col : col + TILE] = value
            image[:, col : col + TILE] += dot(vecs, value)
            slopes[:, col : col + TILE] += dot(vecs[0:16], slope)
        return carry

    if first:
        image[...] = jnp.zeros_like(image)
        slopes[...] = jnp.zeros_like(slopes)
    lax.fori_loop(0, rows // TILE, strip, 0)


def own_kernel(msg, target, kept, image, slopes, turned_src):
    near_block(msg, target, turned_src, kept, image, slopes, True)


def side_kernel(levels, far_scale, *refs):
    signal, msg_a, msg_b, target, own_image, own_slopes, rhs, basis, skel_target = refs[:9]
    lev = refs[9 : 9 + levels]
    outs = refs[9 + levels :]
    kept_a, kept_b, coup_high, coup_low, row_sum, slope_image, first, wmsg = outs[:8]
    wlev = outs[8 : 8 + levels]
    turned_src, image, slopes = outs[8 + levels :]
    image[...] = own_image[...]
    slopes[...] = own_slopes[...]
    near_block(msg_a, target, turned_src, kept_a, image, slopes, False)
    near_block(msg_b, target, turned_src, kept_b, image, slopes, False)
    slope_image[...] = (signal[0] * (LN_2 * LN_2)) * slopes[...]
    far = jnp.zeros(image.shape, FULL)
    for level in range(levels):
        squared = dot(turned(lev[level][64:96, :]), skel_target[level])
        high, low = split_two(matern(squared)[2])
        coup_high[level] = high
        coup_low[level] = low
        coef = lev[level][0:32, :]
        mixed = dot(coef, high) + dot(lev[level][32:64, :], high) + dot(coef, low)
        far = far + dot(mixed.astype(HALF), basis[level])
    total = image[...] + far_scale * far
    sums = total[16:17, :]
    row_sum[...] = sums
    value = signal[0] * (total[0:16] + sums * rhs[...])
    first[...] = value
    high, low = split_two(value)
    wmsg[0:16, :] = high
    wmsg[16:32, :] = low
    for level in range(levels):
        both = dot_rows(wmsg[...], basis[level])
        high, low = split_two(both[0:16] + both[16:32])
        wlev[level][0:16, :] = high
        wlev[level][16:32, :] = low


def row_total(a, b):
    return jnp.sum(a * b, axis=1, keepdims=True)


def second_kernel(levels, far_scale, *refs):
    signal, wmsg, wmsg_a, wmsg_b, kept, kept_a, kept_b = refs[:7]
    basis, coup_high, coup_low, row_sum, first, rhs, slope_image = refs[7:14]
    wlev = refs[14 : 14 + levels]
    sums, first_rest, second_rest, shift_out = refs[14 + levels :]
    both = dot(wmsg[...], kept[...]) + dot(wmsg_a[...], kept_a[...]) + dot(wmsg_b[...], kept_b[...])
    far = jnp.zeros(both.shape, FULL)
    for level in range(levels):
        coef = wlev[level][...]
        mixed = dot(coef, coup_high[level])
        mixed = mixed[0:16] + mixed[16:32] + dot(coef[0:16], coup_low[level])
        high, low = split_two(mixed)
        far = far + dot(jnp.concatenate([high, low], axis=0), basis[level])
    both = both + far_scale * far
    base = rhs[...]
    value = first[...]
    image = signal[0] * (both[0:16] + both[16:32] + row_sum[...] * value)
    weight = row_total(base, base)
    shift = jnp.where(weight > 0.0, row_total(base, value) / jnp.where(weight > 0.0, weight, 1.0), 0.0)
    value = value - shift * base
    image = image - (2.0 * shift) * value - (shift * shift) * base
    first_rest[...] = value
    second_rest[...] = image
    shift_out[...] = jnp.broadcast_to(shift, shift_out.shape)
    slope = slope_image[...]
    parts = (
        shift,
        weight,
        row_total(value, value),
        row_total(value, image),
        row_total(base, image),
        row_total(base, value),
        row_total(base, slope),
        row_total(value, slope),
    )
    lane = lax.broadcasted_iota(jnp.int32, (16, 128), 1)
    row = lax.broadcasted_iota(jnp.int32, (16, 128), 0)
    packed = jnp.zeros((16, 128), FULL)
    for slot, part in enumerate(parts):
        packed = jnp.where(lane == row + 16 * slot, part, packed)
    sums[...] = jnp.broadcast_to(jnp.sum(packed, axis=0, keepdims=True), sums.shape)


def last_kernel(point_total, noise, table, shift_in, first_rest, second_rest, rhs, out, res, trace):
    gathered = table[...]
    shift = gathered

    def slot(index):
        return pltpu.roll(gathered, 128 - 16 * index, 1)

    weight, ww, wz, rz, rw, rs, ws = (slot(index) for index in range(1, 8))

    def total(value):
        return jnp.sum(value, axis=0, keepdims=True)

    norm = total(weight)
    center = total(shift * weight + rw) / norm
    off = shift - center
    cross = total(rw + off * weight)
    square = total(ww + 2.0 * off * rw + off * off * weight)
    mixed = total(rz + 2.0 * off * rw + off * off * weight)
    second = total(
        wz + 2.0 * off * ww + off * off * rw + off * rz + 2.0 * off * off * rw + off * off * off * weight
    )
    held = total(rs)
    along = total(ws + off * rs)
    level = noise[0] + center
    lead = level * norm + cross
    alpha = norm / lead
    part = cross / lead
    norm_next = part * part * norm - 2.0 * part * alpha * cross + alpha * alpha * square
    lean = part + norm_next / norm
    direction = lean * lean * norm - 2.0 * lean * alpha * cross + alpha * alpha * square
    bend = lean * lean * cross - lean * alpha * (mixed + square) + alpha * alpha * second
    beta = norm_next / (level * direction + bend)
    trace[...] = (((alpha + beta * lean) * held - beta * alpha * along) / point_total)[:, 0:16]

    lane = lax.broadcasted_iota(jnp.int32, (16, 128), 1)
    row = lax.broadcasted_iota(jnp.int32, (16, 128), 0)

    def column(value):
        return jnp.sum(jnp.where(lane == row, value, 0.0), axis=1, keepdims=True)

    own_off = shift_in[:, 0:1] - column(center)
    base = rhs[...]
    rest = first_rest[...]
    value = rest + own_off * base
    image = second_rest[...] + (2.0 * own_off) * rest + (own_off * own_off) * base
    out[...] = column(alpha + beta * lean) * base - column(beta * alpha) * value
    res[...] = (
        column(part - beta * level * lean) * base
        - column(alpha - beta * level * alpha + beta * lean) * value
        + column(beta * alpha) * image
    )


def call(kernel, outs, spaces, scratch=(), flops=0):
    params = pltpu.CompilerParams(vmem_limit_bytes=40 * 2**20)
    cost = pl.CostEstimate(flops=flops, bytes_accessed=2**20, transcendentals=0)
    return pl.pallas_call(
        kernel,
        out_shape=[jax.ShapeDtypeStruct(shape, kind) for shape, kind in outs],
        in_specs=[pl.BlockSpec(memory_space=space) for space in spaces],
        out_specs=[pl.BlockSpec(memory_space=VMEM) for _ in outs],
        scratch_shapes=list(scratch),
        compiler_params=params,
        cost_estimate=cost,
    )


def shards(points, right_sides, skeleton, lengthscale, far_length, signal, noise_var):
    probes, rows = right_sides.shape
    levels, rank = skeleton.shape
    count = lax.axis_size("loc")
    far_scale = 1.0 / (rank * rank * levels)
    beside = [(i, i ^ 1) for i in range(count)]
    across = [(i, i + 1) for i in range(1, count - 1, 2)]
    across = across + [(j, i) for i, j in across]

    def partner(value, level):
        return lax.ppermute(value, "loc", [(i, i ^ (2 << level)) for i in range(count)])

    def sides(value):
        return lax.ppermute(value, "loc", beside), lax.ppermute(value, "loc", across)

    msg, target, basis, skel_target, *lev = call(
        functools.partial(front_kernel, levels),
        [
            ((MSG_ROWS, rows), HALF),
            ((SRC_ROWS, rows), HALF),
            ((levels, rank, rows), HALF),
            ((levels, SRC_ROWS, rank), HALF),
        ]
        + [((96, rank), HALF)] * levels,
        [SMEM, SMEM] + [VMEM] * 3,
        [VMEM((MSG_ROWS, rows), FULL), VMEM((SRC_ROWS, rows), FULL), VMEM((2 * SRC_ROWS, rows), HALF)],
    )(lengthscale, far_length, points, right_sides, skeleton)
    msg_a, msg_b = sides(msg)
    lev = [partner(value, level) for level, value in enumerate(lev)]
    kept, image, slopes = call(
        own_kernel,
        [((rows, rows), HALF), ((VEC_ROWS, rows), FULL), ((probes, rows), FULL)],
        [VMEM] * 2,
        [VMEM((rows, SRC_ROWS), HALF)],
    )(msg, target)
    kept_a, kept_b, coup_high, coup_low, row_sum, slope_image, first, wmsg, *wlev = call(
        functools.partial(side_kernel, levels, far_scale),
        [
            ((rows, rows), HALF),
            ((rows, rows), HALF),
            ((levels, rank, rank), HALF),
            ((levels, rank, rank), HALF),
            ((1, rows), FULL),
            ((probes, rows), FULL),
            ((probes, rows), FULL),
            ((2 * probes, rows), HALF),
        ]
        + [((2 * probes, rank), HALF)] * levels,
        [SMEM] + [VMEM] * (8 + levels),
        [VMEM((rows, SRC_ROWS), HALF), VMEM((VEC_ROWS, rows), FULL), VMEM((probes, rows), FULL)],
    )(signal, msg_a, msg_b, target, image, slopes, right_sides, basis, skel_target, *lev)
    wmsg_a, wmsg_b = sides(wmsg)
    wlev = [partner(value, level) for level, value in enumerate(wlev)]
    sums, first_rest, second_rest, shift = call(
        functools.partial(second_kernel, levels, far_scale),
        [((count, 128), FULL), ((probes, rows), FULL), ((probes, rows), FULL), ((probes, 128), FULL)],
        [SMEM] + [VMEM] * (13 + levels),
    )(
        signal,
        wmsg,
        wmsg_a,
        wmsg_b,
        kept,
        kept_a,
        kept_b,
        basis,
        coup_high,
        coup_low,
        row_sum,
        first,
        right_sides,
        slope_image,
        *wlev,
    )
    table = lax.all_to_all(sums, "loc", 0, 0, tiled=True)
    solution, residual, trace = call(
        functools.partial(last_kernel, float(rows * count)),
        [((probes, rows), FULL), ((probes, rows), FULL), ((1, probes), FULL)],
        [SMEM] + [VMEM] * 5,
    )(noise_var, table, shift, first_rest, second_rest, right_sides)
    return (solution, residual, slope_image, trace.reshape(probes))


def solution(mesh):
    placed = (P(None, "loc"), P(None, "loc"), P(None, "loc"), P(), P(), P(), P())
    return jax.shard_map(
        shards,
        mesh=mesh,
        in_specs=placed,
        out_specs=(P(None, "loc"), P(None, "loc"), P(None, "loc"), P()),
        check_vma=False,
    )
```

```python
import functools

import jax
import jax.numpy as jnp
from jax import lax
from jax.experimental import pallas as pl
from jax.experimental.pallas import tpu as pltpu
from jax.sharding import PartitionSpec as P

HALF = jnp.bfloat16
FULL = jnp.float32
LOG2_E = 1.4426950408889634
ROOT_THREE = 1.7320508075688772
TINY = 1e-30
SRC_ROWS = 32
MSG_ROWS = 64
VEC_ROWS = 48
TILE = 128
VMEM = pltpu.VMEM
SMEM = pltpu.SMEM


def split_two(value):
    high = value.astype(HALF)
    low = (value - high.astype(FULL)).astype(HALF)
    return high, low


def split_three(value):
    first = value.astype(HALF).astype(FULL)
    rest = value - first
    second = rest.astype(HALF).astype(FULL)
    third = (rest - second).astype(HALF).astype(FULL)
    return first, second, third


def rate_of(length):
    return ROOT_THREE / length


def matern(squared, rate):
    squared = jnp.maximum(squared, TINY)
    radius = squared * lax.rsqrt(squared)
    decay = jnp.exp2(radius * (-LOG2_E * rate))
    falling = radius * decay
    return decay + rate * falling, radius * falling


def excess(pts):
    total = jnp.full((1, pts.shape[1]), -1.0, FULL)
    lost = jnp.zeros_like(total)
    small = jnp.zeros_like(total)
    for axis in range(3):
        value = pts[axis : axis + 1, :]
        head = value.astype(HALF).astype(FULL)
        tail = value - head
        small = small + tail * tail
        for term in (head * head, 2.0 * head * tail):
            grown = total + term
            back = grown - total
            lost = lost + ((total - (grown - back)) + (term - back))
            total = grown
    return total + (lost + small)


def write_rows(buf, base, pts, source):
    over = excess(pts)
    first = over.astype(HALF).astype(FULL)
    second = over - first
    unit = jnp.ones_like(over)
    if source:
        rows = (unit, unit, unit, first, second)
        order = (0, 0, 0, 1, 1, 1, 2, 2, 2)
        pieces = split_three(pts)
    else:
        rows = (unit + unit, first, second, unit, unit)
        order = (0, 1, 2, 0, 1, 2, 0, 1, 2)
        pieces = split_three(-2.0 * pts)
    for slot, row in enumerate(rows):
        buf[base + slot : base + slot + 1, :] = row
    for slot, index in enumerate(order):
        start = base + 5 + 3 * slot
        buf[start : start + 3, :] = pieces[index]


def dot(a, b):
    return jnp.dot(a, b, preferred_element_type=FULL)


def dot_rows(a, b):
    return lax.dot_general(a, b, (((1,), (1,)), ((), ())), preferred_element_type=FULL)


def turned(value):
    return value.astype(FULL).T.astype(HALF)


def merged(both):
    return jnp.concatenate([both[0:16] + both[16:32], both[32:48]], axis=0)


def front_kernel(levels, *refs):
    far_length, pts_in, rhs_in, skel_in = refs[:4]
    msg, target, basis, skel_target, rhs = refs[4:9]
    lev = refs[9 : 9 + levels]
    buf, pair_buf, turned_src, pts, skel, sems = refs[9 + levels :]
    copies = [
        pltpu.make_async_copy(source, dest, sems.at[index])
        for index, (source, dest) in enumerate(((pts_in, pts), (skel_in, skel), (rhs_in, rhs)))
    ]
    for copy in copies:
        copy.start()
    copies[0].wait()
    points = pts[...]
    write_rows(buf, 0, points, False)
    target[...] = buf[...].astype(HALF)
    pair_buf[SRC_ROWS:, :] = buf[...].astype(HALF)
    write_rows(buf, 0, points, True)
    pair_buf[0:SRC_ROWS, :] = buf[...].astype(HALF)
    msg[32:64, :] = buf[...].astype(HALF)
    rows, rank = pts.shape[1], skel.shape[1]
    copies[1].wait()
    for level in range(levels):
        spot = lax.broadcasted_iota(jnp.int32, (rows, rank), 0)
        picks = jnp.where(spot == skel[level : level + 1, :], 1.0, 0.0).astype(HALF)
        both = dot(pair_buf[...], picks)
        skel_target[level] = both[SRC_ROWS:].astype(HALF)
        skel_source = both[:SRC_ROWS]
        lev[level][64:96, :] = skel_source.astype(HALF)
        turned_src[level * rank : (level + 1) * rank, :] = skel_source.T.astype(HALF)
    rate = rate_of(far_length[0])
    for col in range(0, rows, TILE):
        squared = dot(turned_src[...], target[:, col : col + TILE])
        basis[:, col : col + TILE] = matern(squared, rate)[0].astype(HALF)
    copies[2].wait()
    high, low = split_two(rhs[...])
    msg[0:16, :] = low
    msg[16:32, :] = high
    coef = merged(dot_rows(msg[0:VEC_ROWS, :], basis[...]))
    for level in range(levels):
        high, low = split_two(coef[:, level * rank : (level + 1) * rank])
        lev[level][0:32, :] = high
        lev[level][32:64, :] = low


def near_block(msg, target, turned_src, rate, kept):
    rows = target.shape[1]
    turned_src[...] = turned(msg[32:64, :])
    for col in range(0, rows, TILE):
        squared = dot(turned_src[...], target[:, col : col + TILE])
        value, slope = matern(squared, rate)
        value = value.astype(HALF)
        kept[:, col : col + TILE] = value
        pair = jnp.concatenate([value, slope.astype(HALF)], axis=1)
        total = dot(msg[0:VEC_ROWS, :], pair)
        yield slice(col, col + TILE), merged(total[:, :TILE]), total[16:32, TILE:]


def own_kernel(length, msg, target, kept, image, slopes, turned_src):
    for span, part, slope in near_block(msg, target, turned_src, rate_of(length[0]), kept):
        image[:, span] = part
        slopes[:, span] = slope


def side_kernel(levels, far_scale, *refs):
    length, far_length, signal, msg_a, msg_b, target, image, slopes, rhs, basis, skel_target = refs[:11]
    lev = refs[11 : 11 + levels]
    outs = refs[11 + levels :]
    kept_a, kept_b, coup_high, coup_low, row_sum, slope_image, slope_copy, first, wmsg = outs[:9]
    wlev = outs[9 : 9 + levels]
    turned_a, turned_b = outs[9 + levels :]
    rank = skel_target.shape[2]
    far_rate = rate_of(far_length[0])
    rate = rate_of(length[0])
    mixed = []
    for level in range(levels):
        squared = dot(turned(lev[level][64:96, :]), skel_target[level])
        high, low = split_two(matern(squared, far_rate)[0])
        coup_high[level] = high
        coup_low[level] = low
        both = dot(lev[level][0:64, :], high)
        part = both[0:32] + both[32:64] + dot(lev[level][0:32, :], low)
        mixed.append(jnp.concatenate(split_two(part), axis=0))
    far = dot(jnp.concatenate(mixed, axis=1), basis[...])
    far = far_scale * (far[0:32] + far[32:64])
    factor = signal[0] * (rate * rate)
    side_a = near_block(msg_a, target, turned_a, rate, kept_a)
    side_b = near_block(msg_b, target, turned_b, rate, kept_b)
    for (span, image_a, slopes_a), (_, image_b, slopes_b) in zip(side_a, side_b):
        slope = factor * (slopes[:, span] + slopes_a + slopes_b)
        slope_image[:, span] = slope
        slope_copy[:, span] = slope
        total = image[:, span] + image_a + image_b + far[:, span]
        sums = total[16:17, :]
        row_sum[:, span] = sums
        value = signal[0] * (total[0:16] + sums * rhs[:, span])
        first[:, span] = value
        high, low = split_two(value)
        wmsg[0:16, span] = high
        wmsg[16:32, span] = low
    both = dot_rows(wmsg[...], basis[...])
    high, low = split_two(both[0:16] + both[16:32])
    for level in range(levels):
        span = slice(level * rank, (level + 1) * rank)
        wlev[level][0:16, :] = high[:, span]
        wlev[level][16:32, :] = low[:, span]


def row_total(a, b):
    return jnp.sum(a * b, axis=1, keepdims=True)


def second_kernel(levels, far_scale, *refs):
    signal, wmsg, wmsg_a, wmsg_b, kept, kept_a, kept_b = refs[:7]
    basis, coup_high, coup_low, row_sum, first, rhs, slope_image = refs[7:14]
    wlev = refs[14 : 14 + levels]
    sums, first_rest, second_rest, shift_out = refs[14 + levels :]
    both = dot(wmsg[...], kept[...]) + dot(wmsg_a[...], kept_a[...]) + dot(wmsg_b[...], kept_b[...])
    pieces = []
    for level in range(levels):
        coef = wlev[level][...]
        mixed = dot(coef, coup_high[level])
        mixed = mixed[0:16] + mixed[16:32] + dot(coef[0:16], coup_low[level])
        pieces.append(jnp.concatenate(split_two(mixed), axis=0))
    both = both + far_scale * dot(jnp.concatenate(pieces, axis=1), basis[...])
    base = rhs[...]
    value = first[...]
    image = signal[0] * (both[0:16] + both[16:32] + row_sum[...] * value)
    weight = row_total(base, base)
    shift = jnp.where(weight > 0.0, row_total(base, value) / jnp.where(weight > 0.0, weight, 1.0), 0.0)
    value = value - shift * base
    image = image - (2.0 * shift) * value - (shift * shift) * base
    first_rest[...] = value
    second_rest[...] = image
    shift_out[...] = jnp.broadcast_to(shift, shift_out.shape)
    slope = slope_image[...]
    parts = (
        shift,
        weight,
        row_total(value, value),
        row_total(value, image),
        row_total(base, image),
        row_total(base, value),
        row_total(base, slope),
        row_total(value, slope),
    )
    lane = lax.broadcasted_iota(jnp.int32, (16, 128), 1)
    row = lax.broadcasted_iota(jnp.int32, (16, 128), 0)
    packed = jnp.zeros((16, 128), FULL)
    for slot, part in enumerate(parts):
        packed = jnp.where(lane == row + 16 * slot, part, packed)
    sums[...] = jnp.broadcast_to(jnp.sum(packed, axis=0, keepdims=True), sums.shape)


def last_kernel(point_total, noise, table, shift_in, first_rest, second_rest, rhs, out, res, trace):
    gathered = table[...]
    shift = gathered

    def slot(index):
        return pltpu.roll(gathered, 128 - 16 * index, 1)

    weight, ww, wz, rz, rw, rs, ws = (slot(index) for index in range(1, 8))

    def total(value):
        return jnp.sum(value, axis=0, keepdims=True)

    norm = total(weight)
    center = total(shift * weight + rw) / norm
    off = shift - center
    cross = total(rw + off * weight)
    square = total(ww + 2.0 * off * rw + off * off * weight)
    mixed = total(rz + 2.0 * off * rw + off * off * weight)
    second = total(
        wz + 2.0 * off * ww + off * off * rw + off * rz + 2.0 * off * off * rw + off * off * off * weight
    )
    held = total(rs)
    along = total(ws + off * rs)
    level = noise[0] + center
    lead = level * norm + cross
    alpha = norm / lead
    part = cross / lead
    norm_next = part * part * norm - 2.0 * part * alpha * cross + alpha * alpha * square
    lean = part + norm_next / norm
    direction = lean * lean * norm - 2.0 * lean * alpha * cross + alpha * alpha * square
    bend = lean * lean * cross - lean * alpha * (mixed + square) + alpha * alpha * second
    beta = norm_next / (level * direction + bend)
    trace[...] = (((alpha + beta * lean) * held - beta * alpha * along) / point_total)[:, 0:16]

    lane = lax.broadcasted_iota(jnp.int32, (16, 128), 1)
    row = lax.broadcasted_iota(jnp.int32, (16, 128), 0)

    def column(value):
        return jnp.sum(jnp.where(lane == row, value, 0.0), axis=1, keepdims=True)

    own_off = shift_in[:, 0:1] - column(center)
    base = rhs[...]
    rest = first_rest[...]
    value = rest + own_off * base
    image = second_rest[...] + (2.0 * own_off) * rest + (own_off * own_off) * base
    out[...] = column(alpha + beta * lean) * base - column(beta * alpha) * value
    res[...] = (
        column(part - beta * level * lean) * base
        - column(alpha - beta * level * alpha + beta * lean) * value
        + column(beta * alpha) * image
    )


def call(kernel, outs, spaces, scratch=(), flops=0):
    params = pltpu.CompilerParams(vmem_limit_bytes=40 * 2**20)
    cost = pl.CostEstimate(flops=flops, bytes_accessed=2**20, transcendentals=0)
    return pl.pallas_call(
        kernel,
        out_shape=[jax.ShapeDtypeStruct(shape, kind) for shape, kind in outs],
        in_specs=[pl.BlockSpec(memory_space=space) for space in spaces],
        out_specs=[pl.BlockSpec(memory_space=VMEM) for _ in outs],
        scratch_shapes=list(scratch),
        compiler_params=params,
        cost_estimate=cost,
    )


def shards(points, right_sides, skeleton, lengthscale, far_length, signal, noise_var):
    probes, rows = right_sides.shape
    levels, rank = skeleton.shape
    count = lax.axis_size("loc")
    far_scale = 1.0 / (rank * rank * levels)
    beside = [(i, i ^ 1) for i in range(count)]
    across = [(i, i + 1) for i in range(1, count - 1, 2)]
    across = across + [(j, i) for i, j in across]

    def partner(value, level):
        return lax.ppermute(value, "loc", [(i, i ^ (2 << level)) for i in range(count)])

    def sides(value):
        return lax.ppermute(value, "loc", beside), lax.ppermute(value, "loc", across)

    msg, target, basis, skel_target, rhs, *lev = call(
        functools.partial(front_kernel, levels),
        [
            ((MSG_ROWS, rows), HALF),
            ((SRC_ROWS, rows), HALF),
            ((levels * rank, rows), HALF),
            ((levels, SRC_ROWS, rank), HALF),
            ((probes, rows), FULL),
        ]
        + [((96, rank), HALF)] * levels,
        [SMEM] + [pltpu.HBM] * 3,
        [
            VMEM((SRC_ROWS, rows), FULL),
            VMEM((2 * SRC_ROWS, rows), HALF),
            VMEM((levels * rank, SRC_ROWS), HALF),
            VMEM(points.shape, FULL),
            VMEM(skeleton.shape, jnp.int32),
            pltpu.SemaphoreType.DMA((3,)),
        ],
    )(far_length, points, right_sides, skeleton)
    msg_a, msg_b = sides(msg)
    lev = [partner(value, level) for level, value in enumerate(lev)]
    kept, image, slopes = call(
        own_kernel,
        [((rows, rows), HALF), ((32, rows), FULL), ((probes, rows), FULL)],
        [SMEM] + [VMEM] * 2,
        [VMEM((rows, SRC_ROWS), HALF)],
    )(lengthscale, msg, target)
    kept_a, kept_b, coup_high, coup_low, row_sum, slope_image, slope_copy, first, wmsg, *wlev = call(
        functools.partial(side_kernel, levels, far_scale),
        [
            ((rows, rows), HALF),
            ((rows, rows), HALF),
            ((levels, rank, rank), HALF),
            ((levels, rank, rank), HALF),
            ((1, rows), FULL),
            ((probes, rows), FULL),
            ((probes, rows), FULL),
            ((probes, rows), FULL),
            ((2 * probes, rows), HALF),
        ]
        + [((2 * probes, rank), HALF)] * levels,
        [SMEM] * 3 + [VMEM] * (8 + levels),
        [VMEM((rows, SRC_ROWS), HALF)] * 2,
    )(lengthscale, far_length, signal, msg_a, msg_b, target, image, slopes, rhs, basis, skel_target, *lev)
    wmsg_a, wmsg_b = sides(wmsg)
    wlev = [partner(value, level) for level, value in enumerate(wlev)]
    sums, first_rest, second_rest, shift = call(
        functools.partial(second_kernel, levels, far_scale),
        [((count, 128), FULL), ((probes, rows), FULL), ((probes, rows), FULL), ((probes, 128), FULL)],
        [SMEM] + [VMEM] * (13 + levels),
    )(
        signal,
        wmsg,
        wmsg_a,
        wmsg_b,
        kept,
        kept_a,
        kept_b,
        basis,
        coup_high,
        coup_low,
        row_sum,
        first,
        rhs,
        slope_copy,
        *wlev,
    )
    table = lax.all_to_all(sums, "loc", 0, 0, tiled=True)
    solution, residual, trace = call(
        functools.partial(last_kernel, float(rows * count)),
        [((probes, rows), FULL), ((probes, rows), FULL), ((1, probes), FULL)],
        [SMEM] + [VMEM] * 5,
    )(noise_var, table, shift, first_rest, second_rest, rhs)
    return (solution, residual, slope_image, trace.reshape(probes))


def solution(mesh):
    placed = (P(None, "loc"), P(None, "loc"), P(None, "loc"), P(), P(), P(), P())
    return jax.shard_map(
        shards,
        mesh=mesh,
        in_specs=placed,
        out_specs=(P(None, "loc"), P(None, "loc"), P(None, "loc"), P()),
        check_vma=False,
    )
```

```python
import functools

import jax
import jax.numpy as jnp
from jax import lax
from jax.experimental import pallas as pl
from jax.experimental.pallas import tpu as pltpu
from jax.sharding import PartitionSpec as P

HALF = jnp.bfloat16
FULL = jnp.float32
LOG2_E = 1.4426950408889634
ROOT_THREE = 1.7320508075688772
TINY = 1e-30
SCALE = 2.0**-10
SRC_ROWS = 32
MSG_ROWS = 64
VEC_ROWS = 48
TILE = 128
VMEM = pltpu.VMEM
SMEM = pltpu.SMEM


def split_two(value):
    high = value.astype(HALF)
    low = (value - high.astype(FULL)).astype(HALF)
    return high, low


def split_three(value):
    first = value.astype(HALF).astype(FULL)
    rest = value - first
    second = rest.astype(HALF).astype(FULL)
    third = (rest - second).astype(HALF).astype(FULL)
    return first, second, third


def matern(squared, rates):
    rate, falling_rate = rates
    squared = jnp.maximum(squared, TINY)
    radius = squared * lax.rsqrt(squared)
    decay = jnp.exp2(radius * falling_rate)
    falling = radius * decay
    return decay + rate * falling, radius * falling


def excess(pts):
    total = jnp.full((1, pts.shape[1]), -1.0, FULL)
    lost = jnp.zeros_like(total)
    small = jnp.zeros_like(total)
    for axis in range(3):
        value = pts[axis : axis + 1, :]
        head = value.astype(HALF).astype(FULL)
        tail = value - head
        small = small + tail * tail
        for term in (head * head, 2.0 * head * tail):
            grown = total + term
            back = grown - total
            lost = lost + ((total - (grown - back)) + (term - back))
            total = grown
    return total + (lost + small)


def write_rows(buf, base, pts, source):
    over = excess(pts)
    first = over.astype(HALF).astype(FULL)
    second = over - first
    unit = jnp.ones_like(over)
    if source:
        rows = (unit, unit, unit, first, second)
        order = (0, 0, 0, 1, 1, 1, 2, 2, 2)
        pieces = split_three(pts)
    else:
        rows = (unit + unit, first, second, unit, unit)
        order = (0, 1, 2, 0, 1, 2, 0, 1, 2)
        pieces = split_three(-2.0 * pts)
    for slot, row in enumerate(rows):
        buf[base + slot : base + slot + 1, :] = row
    for slot, index in enumerate(order):
        start = base + 5 + 3 * slot
        buf[start : start + 3, :] = pieces[index]


def dot(a, b):
    return jnp.dot(a, b, preferred_element_type=FULL)


def dot_rows(a, b):
    return lax.dot_general(a, b, (((1,), (1,)), ((), ())), preferred_element_type=FULL)


def turned(value):
    return value.astype(FULL).T.astype(HALF)


def merged(both):
    return jnp.concatenate([both[0:16] + both[16:32], both[32:48]], axis=0)


def front_kernel(levels, *refs):
    length, far_length, given = refs[:3]
    msg, target, basis, skel_target, numbers = refs[3:8]
    lev = refs[8 : 8 + levels]
    buf, pair_buf, turned_src = refs[8 + levels :]
    points = given[16:19, :]
    for slot, value in enumerate((length[0], far_length[0])):
        lengths = jnp.full((1, 128), value, FULL)
        numbers[slot : slot + 1, :] = ROOT_THREE / lengths
        numbers[slot + 2 : slot + 3, :] = (-LOG2_E * ROOT_THREE) / lengths
    write_rows(buf, 0, points, False)
    target[...] = buf[...].astype(HALF)
    pair_buf[SRC_ROWS:, :] = buf[...].astype(HALF)
    write_rows(buf, 0, points, True)
    pair_buf[0:SRC_ROWS, :] = buf[...].astype(HALF)
    msg[32:64, :] = buf[...].astype(HALF)
    rows, rank = points.shape[1], skel_target.shape[2]
    for level in range(levels):
        spot = lax.broadcasted_iota(jnp.int32, (rows, rank), 0).astype(FULL)
        picks = jnp.where(spot == given[24 + level : 25 + level, 0:rank], 1.0, 0.0).astype(HALF)
        both = dot(pair_buf[...], picks)
        skel_target[level] = both[SRC_ROWS:].astype(HALF)
        skel_source = both[:SRC_ROWS]
        lev[level][64:96, :] = skel_source.astype(HALF)
        turned_src[level * rank : (level + 1) * rank, :] = skel_source.T.astype(HALF)
    rates = numbers[1:2, :], numbers[3:4, :]
    for col in range(0, rows, TILE):
        squared = dot(turned_src[...], target[:, col : col + TILE])
        basis[:, col : col + TILE] = matern(squared, rates)[0].astype(HALF)
    high, low = split_two(given[0:16, :])
    msg[0:16, :] = low
    msg[16:32, :] = high
    coef = merged(dot_rows(msg[0:VEC_ROWS, :], basis[...]))
    for level in range(levels):
        high, low = split_two(coef[:, level * rank : (level + 1) * rank])
        lev[level][0:32, :] = high
        lev[level][32:64, :] = low


def near_block(msg, target, turned_src, rates, kept):
    rows = target.shape[1]
    turned_src[...] = turned(msg[32:64, :])
    for col in range(0, rows, TILE):
        squared = dot(turned_src[...], target[:, col : col + TILE])
        value, slope = matern(squared, rates)
        value = value.astype(HALF)
        kept[:, col : col + TILE] = value
        pair = jnp.concatenate([value, slope.astype(HALF)], axis=1)
        total = dot(msg[0:VEC_ROWS, :], pair)
        yield slice(col, col + TILE), merged(total[:, :TILE]), total[16:32, TILE:]


def own_kernel(numbers, msg, target, kept, image, slopes, turned_src):
    rates = numbers[0:1, :], numbers[2:3, :]
    for span, part, slope in near_block(msg, target, turned_src, rates, kept):
        image[:, span] = part
        slopes[:, span] = slope


def side_kernel(levels, far_scale, *refs):
    numbers, msg_a, msg_b, target, image, slopes, given, basis, skel_target = refs[:9]
    lev = refs[9 : 9 + levels]
    outs = refs[9 + levels :]
    kept_a, kept_b, coup_high, coup_low, row_sum, slope_sum, first, wmsg = outs[:8]
    wlev = outs[8 : 8 + levels]
    turned_a, turned_b = outs[8 + levels :]
    rank = skel_target.shape[2]
    rates = numbers[0:1, :], numbers[2:3, :]
    far_rates = [jnp.concatenate([numbers[row : row + 1, :]] * (rank // 128), axis=1) for row in (1, 3)]
    mixed = []
    for level in range(levels):
        squared = dot(turned(lev[level][64:96, :]), skel_target[level])
        high, low = split_two(matern(squared, far_rates)[0])
        coup_high[level] = high
        coup_low[level] = low
        both = dot(lev[level][0:64, :], high)
        part = both[0:32] + both[32:64] + dot(lev[level][0:32, :], low)
        mixed.append(jnp.concatenate(split_two(part), axis=0))
    far = dot(jnp.concatenate(mixed, axis=1), basis[...])
    far = far_scale * (far[0:32] + far[32:64])
    side_a = near_block(msg_a, target, turned_a, rates, kept_a)
    side_b = near_block(msg_b, target, turned_b, rates, kept_b)
    for (span, image_a, slopes_a), (_, image_b, slopes_b) in zip(side_a, side_b):
        slope_sum[:, span] = slopes[:, span] + slopes_a + slopes_b
        total = image[:, span] + image_a + image_b + far[:, span]
        sums = total[16:17, :]
        row_sum[:, span] = sums
        value = SCALE * (total[0:16] + sums * given[0:16, span])
        first[:, span] = value
        high, low = split_two(value)
        wmsg[0:16, span] = high
        wmsg[16:32, span] = low
    both = dot_rows(wmsg[...], basis[...])
    high, low = split_two(both[0:16] + both[16:32])
    for level in range(levels):
        span = slice(level * rank, (level + 1) * rank)
        wlev[level][0:16, :] = high[:, span]
        wlev[level][16:32, :] = low[:, span]


def row_total(a, b):
    return jnp.sum(a * b, axis=1, keepdims=True)


def second_kernel(levels, far_scale, *refs):
    wmsg, wmsg_a, wmsg_b, kept, kept_a, kept_b = refs[:6]
    basis, coup_high, coup_low, row_sum, first, given, slope_sum = refs[6:13]
    wlev = refs[13 : 13 + levels]
    sums, first_rest, second_rest, shift_out = refs[13 + levels :]
    both = dot(wmsg[...], kept[...]) + dot(wmsg_a[...], kept_a[...]) + dot(wmsg_b[...], kept_b[...])
    pieces = []
    for level in range(levels):
        coef = wlev[level][...]
        mixed = dot(coef, coup_high[level])
        mixed = mixed[0:16] + mixed[16:32] + dot(coef[0:16], coup_low[level])
        pieces.append(jnp.concatenate(split_two(mixed), axis=0))
    both = both + far_scale * dot(jnp.concatenate(pieces, axis=1), basis[...])
    base = given[0:16, :]
    value = first[...]
    image = SCALE * (both[0:16] + both[16:32] + row_sum[...] * value)
    weight = row_total(base, base)
    shift = jnp.where(weight > 0.0, row_total(base, value) / jnp.where(weight > 0.0, weight, 1.0), 0.0)
    value = value - shift * base
    image = image - (2.0 * shift) * value - (shift * shift) * base
    first_rest[...] = value
    second_rest[...] = image
    shift_out[...] = jnp.broadcast_to(shift, shift_out.shape)
    slope = slope_sum[...]
    parts = (
        shift,
        weight,
        row_total(value, value),
        row_total(value, image),
        row_total(base, image),
        row_total(base, value),
        row_total(base, slope),
        row_total(value, slope),
    )
    lane = lax.broadcasted_iota(jnp.int32, (16, 128), 1)
    row = lax.broadcasted_iota(jnp.int32, (16, 128), 0)
    packed = jnp.zeros((16, 128), FULL)
    for slot, part in enumerate(parts):
        packed = jnp.where(lane == row + 16 * slot, part, packed)
    sums[...] = jnp.broadcast_to(jnp.sum(packed, axis=0, keepdims=True), sums.shape)


def last_kernel(point_total, signal, noise, numbers, table, shift_in, first_rest, second_rest, given, out, res, trace):
    gathered = table[...]
    shift = gathered

    def slot(index):
        return pltpu.roll(gathered, 128 - 16 * index, 1)

    weight, ww, wz, rz, rw, rs, ws = (slot(index) for index in range(1, 8))

    def total(value):
        return jnp.sum(value, axis=0, keepdims=True)

    gain = signal[0] / SCALE
    rate = numbers[0:1, :]
    norm = total(weight)
    center = total(shift * weight + rw) / norm
    off = shift - center
    cross = total(rw + off * weight)
    square = total(ww + 2.0 * off * rw + off * off * weight)
    mixed = total(rz + 2.0 * off * rw + off * off * weight)
    second = total(
        wz + 2.0 * off * ww + off * off * rw + off * rz + 2.0 * off * off * rw + off * off * off * weight
    )
    held = total(rs)
    along = total(ws + off * rs)
    cross = gain * cross
    square = (gain * gain) * square
    mixed = (gain * gain) * mixed
    second = (gain * gain) * gain * second
    level = noise[0] + gain * center
    lead = level * norm + cross
    alpha = norm / lead
    part = cross / lead
    norm_next = part * part * norm - 2.0 * part * alpha * cross + alpha * alpha * square
    lean = part + norm_next / norm
    direction = lean * lean * norm - 2.0 * lean * alpha * cross + alpha * alpha * square
    bend = lean * lean * cross - lean * alpha * (mixed + square) + alpha * alpha * second
    beta = norm_next / (level * direction + bend)
    factor = signal[0] * (rate * rate)
    trace[...] = (((alpha + beta * lean) * held - beta * alpha * gain * along) * factor / point_total)[:, 0:16]

    lane = lax.broadcasted_iota(jnp.int32, (16, 128), 1)
    row = lax.broadcasted_iota(jnp.int32, (16, 128), 0)

    def column(value):
        return jnp.sum(jnp.where(lane == row, value, 0.0), axis=1, keepdims=True)

    own_off = shift_in[:, 0:1] - column(center)
    base = given[0:16, :]
    rest = first_rest[...]
    value = rest + own_off * base
    image = second_rest[...] + (2.0 * own_off) * rest + (own_off * own_off) * base
    out[...] = column(alpha + beta * lean) * base - column(beta * alpha * gain) * value
    res[...] = (
        column(part - beta * level * lean) * base
        - column((alpha - beta * level * alpha + beta * lean) * gain) * value
        + column(beta * alpha * gain * gain) * image
    )


def slope_kernel(signal, numbers, source, dest):
    rate = numbers[0:1, 0:1]
    dest[...] = (signal[0] * rate * rate) * source[...]


def call(kernel, outs, spaces, scratch=(), flops=0):
    params = pltpu.CompilerParams(vmem_limit_bytes=40 * 2**20)
    cost = pl.CostEstimate(flops=flops, bytes_accessed=2**20, transcendentals=0)
    return pl.pallas_call(
        kernel,
        out_shape=[jax.ShapeDtypeStruct(shape, kind) for shape, kind in outs],
        in_specs=[pl.BlockSpec(memory_space=space) for space in spaces],
        out_specs=[pl.BlockSpec(memory_space=VMEM) for _ in outs],
        scratch_shapes=list(scratch),
        compiler_params=params,
        cost_estimate=cost,
    )


def shards(points, right_sides, skeleton, lengthscale, far_length, signal, noise_var):
    probes, rows = right_sides.shape
    levels, rank = skeleton.shape
    count = lax.axis_size("loc")
    far_scale = 1.0 / (rank * rank * levels)
    beside = [(i, i ^ 1) for i in range(count)]
    across = [(i, i + 1) for i in range(1, count - 1, 2)]
    across = across + [(j, i) for i, j in across]

    def partner(value, level):
        return lax.ppermute(value, "loc", [(i, i ^ (2 << level)) for i in range(count)])

    def sides(value):
        return lax.ppermute(value, "loc", beside), lax.ppermute(value, "loc", across)

    height = -(-(24 + levels) // 8) * 8
    given = jnp.pad(right_sides, ((0, height - probes), (0, 0)))
    given += jnp.pad(points, ((16, height - 19), (0, 0)))
    given += jnp.pad(skeleton, ((24, height - 24 - levels), (0, rows - rank))).astype(FULL)
    msg, target, basis, skel_target, numbers, *lev = call(
        functools.partial(front_kernel, levels),
        [
            ((MSG_ROWS, rows), HALF),
            ((SRC_ROWS, rows), HALF),
            ((levels * rank, rows), HALF),
            ((levels, SRC_ROWS, rank), HALF),
            ((8, 128), FULL),
        ]
        + [((96, rank), HALF)] * levels,
        [SMEM, SMEM, VMEM],
        [
            VMEM((SRC_ROWS, rows), FULL),
            VMEM((2 * SRC_ROWS, rows), HALF),
            VMEM((levels * rank, SRC_ROWS), HALF),
        ],
    )(lengthscale, far_length, given)
    msg_a, msg_b = sides(msg)
    lev = [partner(value, level) for level, value in enumerate(lev)]
    kept, image, slopes = call(
        own_kernel,
        [((rows, rows), HALF), ((32, rows), FULL), ((probes, rows), FULL)],
        [VMEM] * 3,
        [VMEM((rows, SRC_ROWS), HALF)],
    )(numbers, msg, target)
    kept_a, kept_b, coup_high, coup_low, row_sum, slope_sum, first, wmsg, *wlev = call(
        functools.partial(side_kernel, levels, far_scale),
        [
            ((rows, rows), HALF),
            ((rows, rows), HALF),
            ((levels, rank, rank), HALF),
            ((levels, rank, rank), HALF),
            ((1, rows), FULL),
            ((probes, rows), FULL),
            ((probes, rows), FULL),
            ((2 * probes, rows), HALF),
        ]
        + [((2 * probes, rank), HALF)] * levels,
        [VMEM] * (9 + levels),
        [VMEM((rows, SRC_ROWS), HALF)] * 2,
    )(numbers, msg_a, msg_b, target, image, slopes, given, basis, skel_target, *lev)
    wmsg_a, wmsg_b = sides(wmsg)
    wlev = [partner(value, level) for level, value in enumerate(wlev)]
    sums, first_rest, second_rest, shift = call(
        functools.partial(second_kernel, levels, far_scale),
        [((count, 128), FULL), ((probes, rows), FULL), ((probes, rows), FULL), ((probes, 128), FULL)],
        [VMEM] * (13 + levels),
    )(
        wmsg,
        wmsg_a,
        wmsg_b,
        kept,
        kept_a,
        kept_b,
        basis,
        coup_high,
        coup_low,
        row_sum,
        first,
        given,
        slope_sum,
        *wlev,
    )
    table = lax.all_to_all(sums, "loc", 0, 0, tiled=True)
    (slope_image,) = call(slope_kernel, [((probes, rows), FULL)], [SMEM, VMEM, VMEM])(signal, numbers, slope_sum)
    solution, residual, trace = call(
        functools.partial(last_kernel, float(rows * count)),
        [((probes, rows), FULL), ((probes, rows), FULL), ((1, probes), FULL)],
        [SMEM, SMEM] + [VMEM] * 6,
    )(signal, noise_var, numbers, table, shift, first_rest, second_rest, given)
    return (solution, residual, slope_image, trace.reshape(probes))


def solution(mesh):
    placed = (P(None, "loc"), P(None, "loc"), P(None, "loc"), P(), P(), P(), P())
    return jax.shard_map(
        shards,
        mesh=mesh,
        in_specs=placed,
        out_specs=(P(None, "loc"), P(None, "loc"), P(None, "loc"), P()),
        check_vma=False,
    )
```

```python
import functools

import jax
import jax.numpy as jnp
from jax import lax
from jax.experimental import pallas as pl
from jax.experimental.pallas import tpu as pltpu
from jax.sharding import PartitionSpec as P

HALF = jnp.bfloat16
FULL = jnp.float32
LOG2_E = 1.4426950408889634
ROOT_THREE = 1.7320508075688772
TINY = 1e-30
SCALE = 2.0**-10
SRC_ROWS = 32
MSG_ROWS = 64
VEC_ROWS = 48
TILE = 128
VMEM = pltpu.VMEM
SMEM = pltpu.SMEM


def split_two(value):
    high = value.astype(HALF)
    low = (value - high.astype(FULL)).astype(HALF)
    return high, low


def split_three(value):
    first = value.astype(HALF).astype(FULL)
    rest = value - first
    second = rest.astype(HALF).astype(FULL)
    third = (rest - second).astype(HALF).astype(FULL)
    return first, second, third


def matern(squared, rates):
    rate, falling_rate = rates
    squared = jnp.maximum(squared, TINY)
    radius = squared * lax.rsqrt(squared)
    decay = jnp.exp2(radius * falling_rate)
    falling = radius * decay
    return decay + rate * falling, radius * falling


def excess(pts):
    total = jnp.full((1, pts.shape[1]), -1.0, FULL)
    lost = jnp.zeros_like(total)
    small = jnp.zeros_like(total)
    for axis in range(3):
        value = pts[axis : axis + 1, :]
        head = value.astype(HALF).astype(FULL)
        tail = value - head
        small = small + tail * tail
        for term in (head * head, 2.0 * head * tail):
            grown = total + term
            back = grown - total
            lost = lost + ((total - (grown - back)) + (term - back))
            total = grown
    return total + (lost + small)


def write_rows(buf, base, pts, source):
    over = excess(pts)
    first = over.astype(HALF).astype(FULL)
    second = over - first
    unit = jnp.ones_like(over)
    if source:
        rows = (unit, unit, unit, first, second)
        order = (0, 0, 0, 1, 1, 1, 2, 2, 2)
        pieces = split_three(pts)
    else:
        rows = (unit + unit, first, second, unit, unit)
        order = (0, 1, 2, 0, 1, 2, 0, 1, 2)
        pieces = split_three(-2.0 * pts)
    for slot, row in enumerate(rows):
        buf[base + slot : base + slot + 1, :] = row
    for slot, index in enumerate(order):
        start = base + 5 + 3 * slot
        buf[start : start + 3, :] = pieces[index]


def dot(a, b):
    return jnp.dot(a, b, preferred_element_type=FULL)


def dot_rows(a, b):
    return lax.dot_general(a, b, (((1,), (1,)), ((), ())), preferred_element_type=FULL)


def turned(value):
    return value.astype(FULL).T.astype(HALF)


def merged(both):
    return jnp.concatenate([both[0:16] + both[16:32], both[32:48]], axis=0)


def on_first_core():
    return lax.rem(lax.axis_index("loc"), 2) == 0


def share(values, keep, give):
    first = on_first_core()
    for slot in range(len(values) // 2):
        even, odd = values[2 * slot], values[2 * slot + 1]
        keep[slot] = jnp.where(first, even, odd)
        give[slot] = jnp.where(first, odd, even)


def gather_share(keep, got, packs):
    first = on_first_core()
    for slot, pack in enumerate(packs):
        pack[0] = jnp.where(first, keep[slot], got[slot])
        pack[1] = jnp.where(first, got[slot], keep[slot])


def level_values(cross, other):
    first = on_first_core()
    values = []
    for mine, theirs in zip(cross, other):
        here = jnp.where(first, mine[0], mine[1])
        there = jnp.where(first, theirs[0], theirs[1])
        values.append(jnp.where(first, here, there))
        values.append(jnp.where(first, there, here))
    return values


def front_kernel(levels, *refs):
    length, far_length, given = refs[:3]
    msg, target, basis, skel_target, numbers, keep, give = refs[3:10]
    buf, pair_buf, turned_src = refs[10:]
    points = given[16:19, :]
    for slot, value in enumerate((length[0], far_length[0])):
        lengths = jnp.full((1, 128), value, FULL)
        numbers[slot : slot + 1, :] = ROOT_THREE / lengths
        numbers[slot + 2 : slot + 3, :] = (-LOG2_E * ROOT_THREE) / lengths
    write_rows(buf, 0, points, False)
    target[...] = buf[...].astype(HALF)
    pair_buf[SRC_ROWS:, :] = buf[...].astype(HALF)
    write_rows(buf, 0, points, True)
    pair_buf[0:SRC_ROWS, :] = buf[...].astype(HALF)
    msg[32:64, :] = buf[...].astype(HALF)
    rows, rank = points.shape[1], skel_target.shape[2]
    sources = []
    for level in range(levels):
        spot = lax.broadcasted_iota(jnp.int32, (rows, rank), 0).astype(FULL)
        picks = jnp.where(spot == given[24 + level : 25 + level, 0:rank], 1.0, 0.0).astype(HALF)
        both = dot(pair_buf[...], picks)
        skel_target[level] = both[SRC_ROWS:].astype(HALF)
        skel_source = both[:SRC_ROWS]
        sources.append(skel_source.astype(HALF))
        turned_src[level * rank : (level + 1) * rank, :] = skel_source.T.astype(HALF)
    rates = numbers[1:2, :], numbers[3:4, :]
    for col in range(0, rows, TILE):
        squared = dot(turned_src[...], target[:, col : col + TILE])
        basis[:, col : col + TILE] = matern(squared, rates)[0].astype(HALF)
    high, low = split_two(given[0:16, :])
    msg[0:16, :] = low
    msg[16:32, :] = high
    coef = merged(dot_rows(msg[0:VEC_ROWS, :], basis[...]))
    lev = []
    for level in range(levels):
        high, low = split_two(coef[:, level * rank : (level + 1) * rank])
        lev.append(jnp.concatenate([high, low, sources[level]], axis=0))
    share(lev, keep, give)


def near_block(msg, target, turned_src, rates, kept):
    rows = target.shape[1]
    turned_src[...] = turned(msg[32:64, :])
    for col in range(0, rows, TILE):
        squared = dot(turned_src[...], target[:, col : col + TILE])
        value, slope = matern(squared, rates)
        value = value.astype(HALF)
        kept[:, col : col + TILE] = value
        pair = jnp.concatenate([value, slope.astype(HALF)], axis=1)
        total = dot(msg[0:VEC_ROWS, :], pair)
        yield slice(col, col + TILE), merged(total[:, :TILE]), total[16:32, TILE:]


def own_kernel(numbers, msg, target, keep, got, kept, image, slopes, *rest):
    packs, turned_src = rest[:-1], rest[-1]
    gather_share(keep, got, packs)
    rates = numbers[0:1, :], numbers[2:3, :]
    for span, part, slope in near_block(msg, target, turned_src, rates, kept):
        image[:, span] = part
        slopes[:, span] = slope


def side_kernel(numbers, msg, target, image_in, slopes_in, kept, image, slopes, turned_src):
    rates = numbers[0:1, :], numbers[2:3, :]
    for span, part, slope in near_block(msg, target, turned_src, rates, kept):
        image[:, span] = image_in[:, span] + part
        slopes[:, span] = slopes_in[:, span] + slope


def far_kernel(half, far_scale, *refs):
    numbers, image, given, basis, skel_target = refs[:5]
    lev = level_values(refs[5 : 5 + half], refs[5 + half : 5 + 2 * half])
    coup_high, coup_low, row_sum, first, wmsg, keep, give = refs[5 + 2 * half :]
    rank = skel_target.shape[2]
    far_rates = [jnp.concatenate([numbers[row : row + 1, :]] * (rank // 128), axis=1) for row in (1, 3)]
    mixed = []
    for level, value in enumerate(lev):
        squared = dot(turned(value[64:96]), skel_target[level])
        high, low = split_two(matern(squared, far_rates)[0])
        coup_high[level] = high
        coup_low[level] = low
        both = dot(value[0:64], high)
        part = both[0:32] + both[32:64] + dot(value[0:32], low)
        mixed.append(jnp.concatenate(split_two(part), axis=0))
    far = dot(jnp.concatenate(mixed, axis=1), basis[...])
    total = image[...] + far_scale * (far[0:32] + far[32:64])
    sums = total[16:17, :]
    row_sum[...] = sums
    value = SCALE * (total[0:16] + sums * given[0:16, :])
    first[...] = value
    high, low = split_two(value)
    wmsg[0:16, :] = high
    wmsg[16:32, :] = low
    both = dot_rows(wmsg[...], basis[...])
    high, low = split_two(both[0:16] + both[16:32])
    both = jnp.concatenate([high, low], axis=0)
    share([both[:, level * rank : (level + 1) * rank] for level in range(len(lev))], keep, give)


def pack_kernel(keep, got, *packs):
    gather_share(keep, got, packs)


def near_kernel(wmsg, wmsg_a, wmsg_b, kept, kept_a, kept_b, out):
    out[...] = dot(wmsg[...], kept[...]) + dot(wmsg_a[...], kept_a[...]) + dot(wmsg_b[...], kept_b[...])


def row_total(a, b):
    return jnp.sum(a * b, axis=1, keepdims=True)


def second_kernel(half, far_scale, *refs):
    near, basis, coup_high, coup_low, row_sum, first, given, slope_sum = refs[:8]
    wlev = level_values(refs[8 : 8 + half], refs[8 + half : 8 + 2 * half])
    sums, first_rest, second_rest, shift_out = refs[8 + 2 * half :]
    pieces = []
    for level, coef in enumerate(wlev):
        mixed = dot(coef, coup_high[level])
        mixed = mixed[0:16] + mixed[16:32] + dot(coef[0:16], coup_low[level])
        pieces.append(jnp.concatenate(split_two(mixed), axis=0))
    both = near[...] + far_scale * dot(jnp.concatenate(pieces, axis=1), basis[...])
    base = given[0:16, :]
    value = first[...]
    image = SCALE * (both[0:16] + both[16:32] + row_sum[...] * value)
    weight = row_total(base, base)
    shift = jnp.where(weight > 0.0, row_total(base, value) / jnp.where(weight > 0.0, weight, 1.0), 0.0)
    value = value - shift * base
    image = image - (2.0 * shift) * value - (shift * shift) * base
    first_rest[...] = value
    second_rest[...] = image
    shift_out[...] = jnp.broadcast_to(shift, shift_out.shape)
    slope = slope_sum[...]
    parts = (
        shift,
        weight,
        row_total(value, value),
        row_total(value, image),
        row_total(base, image),
        row_total(base, value),
        row_total(base, slope),
        row_total(value, slope),
    )
    lane = lax.broadcasted_iota(jnp.int32, (16, 128), 1)
    row = lax.broadcasted_iota(jnp.int32, (16, 128), 0)
    packed = jnp.zeros((16, 128), FULL)
    for slot, part in enumerate(parts):
        packed = jnp.where(lane == row + 16 * slot, part, packed)
    sums[...] = jnp.broadcast_to(jnp.sum(packed, axis=0, keepdims=True), sums.shape)


def last_kernel(point_total, signal, noise, numbers, table, shift_in, first_rest, second_rest, given, out, res, trace):
    gathered = table[...]
    shift = gathered

    def slot(index):
        return pltpu.roll(gathered, 128 - 16 * index, 1)

    weight, ww, wz, rz, rw, rs, ws = (slot(index) for index in range(1, 8))

    def total(value):
        return jnp.sum(value, axis=0, keepdims=True)

    gain = signal[0] / SCALE
    rate = numbers[0:1, :]
    norm = total(weight)
    center = total(shift * weight + rw) / norm
    off = shift - center
    cross = total(rw + off * weight)
    square = total(ww + 2.0 * off * rw + off * off * weight)
    mixed = total(rz + 2.0 * off * rw + off * off * weight)
    second = total(
        wz + 2.0 * off * ww + off * off * rw + off * rz + 2.0 * off * off * rw + off * off * off * weight
    )
    held = total(rs)
    along = total(ws + off * rs)
    cross = gain * cross
    square = (gain * gain) * square
    mixed = (gain * gain) * mixed
    second = (gain * gain) * gain * second
    level = noise[0] + gain * center
    lead = level * norm + cross
    alpha = norm / lead
    part = cross / lead
    norm_next = part * part * norm - 2.0 * part * alpha * cross + alpha * alpha * square
    lean = part + norm_next / norm
    direction = lean * lean * norm - 2.0 * lean * alpha * cross + alpha * alpha * square
    bend = lean * lean * cross - lean * alpha * (mixed + square) + alpha * alpha * second
    beta = norm_next / (level * direction + bend)
    factor = signal[0] * (rate * rate)
    trace[...] = (((alpha + beta * lean) * held - beta * alpha * gain * along) * factor / point_total)[:, 0:16]

    lane = lax.broadcasted_iota(jnp.int32, (16, 128), 1)
    row = lax.broadcasted_iota(jnp.int32, (16, 128), 0)

    def column(value):
        return jnp.sum(jnp.where(lane == row, value, 0.0), axis=1, keepdims=True)

    own_off = shift_in[:, 0:1] - column(center)
    base = given[0:16, :]
    rest = first_rest[...]
    value = rest + own_off * base
    image = second_rest[...] + (2.0 * own_off) * rest + (own_off * own_off) * base
    out[...] = column(alpha + beta * lean) * base - column(beta * alpha * gain) * value
    res[...] = (
        column(part - beta * level * lean) * base
        - column((alpha - beta * level * alpha + beta * lean) * gain) * value
        + column(beta * alpha * gain * gain) * image
    )


def slope_kernel(signal, numbers, source, dest):
    rate = numbers[0:1, 0:1]
    dest[...] = (signal[0] * rate * rate) * source[...]


def call(kernel, outs, spaces, scratch=(), micros=2.0):
    params = pltpu.CompilerParams(vmem_limit_bytes=40 * 2**20)
    cost = pl.CostEstimate(flops=int(micros * 1e9), bytes_accessed=2**16, transcendentals=0)
    return pl.pallas_call(
        kernel,
        out_shape=[jax.ShapeDtypeStruct(shape, kind) for shape, kind in outs],
        in_specs=[pl.BlockSpec(memory_space=space) for space in spaces],
        out_specs=[pl.BlockSpec(memory_space=VMEM) for _ in outs],
        scratch_shapes=list(scratch),
        compiler_params=params,
        cost_estimate=cost,
    )


def shards(points, right_sides, skeleton, lengthscale, far_length, signal, noise_var):
    probes, rows = right_sides.shape
    levels, rank = skeleton.shape
    half = levels // 2
    count = lax.axis_size("loc")
    far_scale = 1.0 / (rank * rank * levels)
    beside = [(i, i ^ 1) for i in range(count)]
    across = [(i, i + 1) for i in range(1, count - 1, 2)]
    across = across + [(j, i) for i, j in across]

    def partner(value, slot):
        pairs = [(i, i ^ (2 << (2 * slot + i % 2))) for i in range(count)]
        return lax.ppermute(value, "loc", pairs)

    def sibling(value):
        return lax.ppermute(value, "loc", beside)

    def sides(value):
        return lax.ppermute(value, "loc", beside), lax.ppermute(value, "loc", across)

    height = -(-(24 + levels) // 8) * 8
    given = jnp.pad(right_sides, ((0, height - probes), (0, 0)))
    given += jnp.pad(points, ((16, height - 19), (0, 0)))
    given += jnp.pad(skeleton, ((24, height - 24 - levels), (0, rows - rank))).astype(FULL)
    msg, target, basis, skel_target, numbers, keep, give = call(
        functools.partial(front_kernel, levels),
        [
            ((MSG_ROWS, rows), HALF),
            ((SRC_ROWS, rows), HALF),
            ((levels * rank, rows), HALF),
            ((levels, SRC_ROWS, rank), HALF),
            ((8, 128), FULL),
            ((half, 96, rank), HALF),
            ((half, 96, rank), HALF),
        ],
        [SMEM, SMEM, VMEM],
        [
            VMEM((SRC_ROWS, rows), FULL),
            VMEM((2 * SRC_ROWS, rows), HALF),
            VMEM((levels * rank, SRC_ROWS), HALF),
        ],
    )(lengthscale, far_length, given)
    got = sibling(give)
    msg_a, msg_b = sides(msg)
    near_outs = [((rows, rows), HALF), ((32, rows), FULL), ((probes, rows), FULL)]
    turned_buf = [VMEM((rows, SRC_ROWS), HALF)]
    kept, image, slopes, *packs = call(
        own_kernel,
        near_outs + [((2, 96, rank), HALF)] * half,
        [VMEM] * 5,
        turned_buf,
    )(numbers, msg, target, keep, got)
    cross = [partner(pack, slot) for slot, pack in enumerate(packs)]
    kept_a, image, slopes = call(side_kernel, near_outs, [VMEM] * 5, turned_buf)(numbers, msg_a, target, image, slopes)
    other = [sibling(value) for value in cross]
    kept_b, image, slopes = call(side_kernel, near_outs, [VMEM] * 5, turned_buf)(numbers, msg_b, target, image, slopes)
    coup_high, coup_low, row_sum, first, wmsg, keep, give = call(
        functools.partial(far_kernel, half, far_scale),
        [
            ((levels, rank, rank), HALF),
            ((levels, rank, rank), HALF),
            ((1, rows), FULL),
            ((probes, rows), FULL),
            ((2 * probes, rows), HALF),
            ((half, 2 * probes, rank), HALF),
            ((half, 2 * probes, rank), HALF),
        ],
        [VMEM] * (5 + levels),
    )(numbers, image, given, basis, skel_target, *cross, *other)
    got = sibling(give)
    wmsg_a, wmsg_b = sides(wmsg)
    packs = call(pack_kernel, [((2, 2 * probes, rank), HALF)] * half, [VMEM] * 2, micros=0.1)(keep, got)
    cross = [partner(pack, slot) for slot, pack in enumerate(packs)]
    (near,) = call(near_kernel, [((2 * probes, rows), FULL)], [VMEM] * 6, micros=1.2)(wmsg, wmsg_a, wmsg_b, kept, kept_a, kept_b)
    other = [sibling(value) for value in cross]
    sums, first_rest, second_rest, shift = call(
        functools.partial(second_kernel, half, far_scale),
        [((count, 128), FULL), ((probes, rows), FULL), ((probes, rows), FULL), ((probes, 128), FULL)],
        [VMEM] * (8 + levels),
    )(near, basis, coup_high, coup_low, row_sum, first, given, slopes, *cross, *other)
    table = lax.all_to_all(sums, "loc", 0, 0, tiled=True)
    (slope_image,) = call(slope_kernel, [((probes, rows), FULL)], [SMEM, VMEM, VMEM])(signal, numbers, slopes)
    solution, residual, trace = call(
        functools.partial(last_kernel, float(rows * count)),
        [((probes, rows), FULL), ((probes, rows), FULL), ((1, probes), FULL)],
        [SMEM, SMEM] + [VMEM] * 6,
    )(signal, noise_var, numbers, table, shift, first_rest, second_rest, given)
    return (solution, residual, slope_image, trace.reshape(probes))


def solution(mesh):
    placed = (P(None, "loc"), P(None, "loc"), P(None, "loc"), P(), P(), P(), P())
    return jax.shard_map(
        shards,
        mesh=mesh,
        in_specs=placed,
        out_specs=(P(None, "loc"), P(None, "loc"), P(None, "loc"), P()),
        check_vma=False,
    )
```

```python
import functools

import jax
import jax.numpy as jnp
from jax import lax
from jax.experimental import pallas as pl
from jax.experimental.pallas import tpu as pltpu
from jax.sharding import PartitionSpec as P

HALF = jnp.bfloat16
FULL = jnp.float32
LOG2_E = 1.4426950408889634
ROOT_THREE = 1.7320508075688772
TINY = 1e-30
SCALE = 2.0**-10
SRC_ROWS = 32
MSG_ROWS = 64
VEC_ROWS = 48
TILE = 128
WIDE_TILE = 512
VMEM = pltpu.VMEM
SMEM = pltpu.SMEM


def split_two(value):
    high = value.astype(HALF)
    low = (value - high.astype(FULL)).astype(HALF)
    return high, low


def split_three(value):
    first = value.astype(HALF).astype(FULL)
    rest = value - first
    second = rest.astype(HALF).astype(FULL)
    third = (rest - second).astype(HALF).astype(FULL)
    return first, second, third


def matern(squared, rates):
    rate, falling_rate = rates
    squared = jnp.maximum(squared, TINY)
    radius = squared * lax.rsqrt(squared)
    decay = jnp.exp2(radius * falling_rate)
    falling = radius * decay
    return decay + rate * falling, radius * falling


def excess(pts):
    total = jnp.full((1, pts.shape[1]), -1.0, FULL)
    lost = jnp.zeros_like(total)
    small = jnp.zeros_like(total)
    for axis in range(3):
        value = pts[axis : axis + 1, :]
        head = value.astype(HALF).astype(FULL)
        tail = value - head
        small = small + tail * tail
        for term in (head * head, 2.0 * head * tail):
            grown = total + term
            back = grown - total
            lost = lost + ((total - (grown - back)) + (term - back))
            total = grown
    return total + (lost + small)


def write_rows(buf, base, pts, source):
    over = excess(pts)
    first = over.astype(HALF).astype(FULL)
    second = over - first
    unit = jnp.ones_like(over)
    if source:
        rows = (unit, unit, unit, first, second)
        order = (0, 0, 0, 1, 1, 1, 2, 2, 2)
        pieces = split_three(pts)
    else:
        rows = (unit + unit, first, second, unit, unit)
        order = (0, 1, 2, 0, 1, 2, 0, 1, 2)
        pieces = split_three(-2.0 * pts)
    for slot, row in enumerate(rows):
        buf[base + slot : base + slot + 1, :] = row
    for slot, index in enumerate(order):
        start = base + 5 + 3 * slot
        buf[start : start + 3, :] = pieces[index]


def dot(a, b):
    return jnp.dot(a, b, preferred_element_type=FULL)


def dot_rows(a, b):
    return lax.dot_general(a, b, (((1,), (1,)), ((), ())), preferred_element_type=FULL)


def turned(value):
    return value.astype(FULL).T.astype(HALF)


def merged(both):
    return jnp.concatenate([both[0:16] + both[16:32], both[32:48]], axis=0)


def on_first_core():
    return lax.rem(lax.axis_index("loc"), 2) == 0


def share(values, keep, give):
    first = on_first_core()
    for slot in range(len(values) // 2):
        even, odd = values[2 * slot], values[2 * slot + 1]
        keep[slot] = jnp.where(first, even, odd)
        give[slot] = jnp.where(first, odd, even)


def gather_share(keep, got, packs):
    first = on_first_core()
    for slot, pack in enumerate(packs):
        pack[0] = jnp.where(first, keep[slot], got[slot])
        pack[1] = jnp.where(first, got[slot], keep[slot])


def level_values(cross, other):
    first = on_first_core()
    values = []
    for mine, theirs in zip(cross, other):
        here = jnp.where(first, mine[0], mine[1])
        there = jnp.where(first, theirs[0], theirs[1])
        values.append(jnp.where(first, here, there))
        values.append(jnp.where(first, there, here))
    return values


def front_kernel(levels, *refs):
    length, far_length, given = refs[:3]
    msg, target, basis, skel_target, numbers, keep, give = refs[3:10]
    buf, pair_buf, turned_src = refs[10:]
    points = given[16:19, :]
    for slot, value in enumerate((length[0], far_length[0])):
        lengths = jnp.full((1, 128), value, FULL)
        numbers[slot : slot + 1, :] = ROOT_THREE / lengths
        numbers[slot + 2 : slot + 3, :] = (-LOG2_E * ROOT_THREE) / lengths
    write_rows(buf, 0, points, False)
    target[...] = buf[...].astype(HALF)
    pair_buf[SRC_ROWS:, :] = buf[...].astype(HALF)
    write_rows(buf, 0, points, True)
    pair_buf[0:SRC_ROWS, :] = buf[...].astype(HALF)
    msg[32:64, :] = buf[...].astype(HALF)
    rows, rank = points.shape[1], skel_target.shape[2]
    sources = []
    for level in range(levels):
        spot = lax.broadcasted_iota(jnp.int32, (rows, rank), 0).astype(FULL)
        picks = jnp.where(spot == given[24 + level : 25 + level, 0:rank], 1.0, 0.0).astype(HALF)
        both = dot(pair_buf[...], picks)
        skel_target[level] = both[SRC_ROWS:].astype(HALF)
        skel_source = both[:SRC_ROWS]
        sources.append(skel_source.astype(HALF))
        turned_src[level * rank : (level + 1) * rank, :] = skel_source.T.astype(HALF)
    rates = [jnp.concatenate([numbers[row : row + 1, :]] * (WIDE_TILE // 128), axis=1) for row in (1, 3)]
    for col in range(0, rows, WIDE_TILE):
        squared = dot(turned_src[...], target[:, col : col + WIDE_TILE])
        basis[:, col : col + WIDE_TILE] = matern(squared, rates)[0].astype(HALF)
    high, low = split_two(given[0:16, :])
    msg[0:16, :] = low
    msg[16:32, :] = high
    coef = merged(dot_rows(msg[0:VEC_ROWS, :], basis[...]))
    lev = []
    for level in range(levels):
        high, low = split_two(coef[:, level * rank : (level + 1) * rank])
        lev.append(jnp.concatenate([high, low, sources[level]], axis=0))
    share(lev, keep, give)


def near_block(msg, target, turned_src, rates, kept):
    rows = target.shape[1]
    turned_src[...] = turned(msg[32:64, :])
    for col in range(0, rows, TILE):
        squared = dot(turned_src[...], target[:, col : col + TILE])
        value, slope = matern(squared, rates)
        value = value.astype(HALF)
        kept[:, col : col + TILE] = value
        pair = jnp.concatenate([value, slope.astype(HALF)], axis=1)
        total = dot(msg[0:VEC_ROWS, :], pair)
        yield slice(col, col + TILE), merged(total[:, :TILE]), total[16:32, TILE:]


def own_kernel(numbers, msg, target, keep, got, kept, image, slopes, *rest):
    packs, turned_src = rest[:-1], rest[-1]
    gather_share(keep, got, packs)
    rates = numbers[0:1, :], numbers[2:3, :]
    for span, part, slope in near_block(msg, target, turned_src, rates, kept):
        image[:, span] = part
        slopes[:, span] = slope


def side_kernel(numbers, msg, target, image_in, slopes_in, kept, image, slopes, turned_src):
    rates = numbers[0:1, :], numbers[2:3, :]
    for span, part, slope in near_block(msg, target, turned_src, rates, kept):
        image[:, span] = image_in[:, span] + part
        slopes[:, span] = slopes_in[:, span] + slope


def far_kernel(half, far_scale, *refs):
    numbers, image, given, basis, skel_target = refs[:5]
    lev = level_values(refs[5 : 5 + half], refs[5 + half : 5 + 2 * half])
    coup_high, coup_low, row_sum, first, wmsg, keep, give = refs[5 + 2 * half :]
    rank = skel_target.shape[2]
    far_rates = [jnp.concatenate([numbers[row : row + 1, :]] * (rank // 128), axis=1) for row in (1, 3)]
    mixed = []
    for level, value in enumerate(lev):
        squared = dot(turned(value[64:96]), skel_target[level])
        high, low = split_two(matern(squared, far_rates)[0])
        coup_high[level] = high
        coup_low[level] = low
        both = dot(value[0:64], high)
        part = both[0:32] + both[32:64] + dot(value[0:32], low)
        mixed.append(jnp.concatenate(split_two(part), axis=0))
    far = dot(jnp.concatenate(mixed, axis=1), basis[...])
    total = image[...] + far_scale * (far[0:32] + far[32:64])
    sums = total[16:17, :]
    row_sum[...] = sums
    value = SCALE * (total[0:16] + sums * given[0:16, :])
    first[...] = value
    high, low = split_two(value)
    wmsg[0:16, :] = high
    wmsg[16:32, :] = low
    both = dot_rows(wmsg[...], basis[...])
    high, low = split_two(both[0:16] + both[16:32])
    both = jnp.concatenate([high, low], axis=0)
    share([both[:, level * rank : (level + 1) * rank] for level in range(len(lev))], keep, give)


def pack_kernel(keep, got, *packs):
    gather_share(keep, got, packs)


def near_kernel(wmsg, wmsg_a, wmsg_b, kept, kept_a, kept_b, out):
    out[...] = dot(wmsg[...], kept[...]) + dot(wmsg_a[...], kept_a[...]) + dot(wmsg_b[...], kept_b[...])


def row_total(a, b):
    return jnp.sum(a * b, axis=1, keepdims=True)


def second_kernel(half, far_scale, *refs):
    near, basis, coup_high, coup_low, row_sum, first, given, slope_sum = refs[:8]
    wlev = level_values(refs[8 : 8 + half], refs[8 + half : 8 + 2 * half])
    sums, first_rest, second_rest, shift_out = refs[8 + 2 * half :]
    pieces = []
    for level, coef in enumerate(wlev):
        mixed = dot(coef, coup_high[level])
        mixed = mixed[0:16] + mixed[16:32] + dot(coef[0:16], coup_low[level])
        pieces.append(jnp.concatenate(split_two(mixed), axis=0))
    both = near[...] + far_scale * dot(jnp.concatenate(pieces, axis=1), basis[...])
    base = given[0:16, :]
    value = first[...]
    image = SCALE * (both[0:16] + both[16:32] + row_sum[...] * value)
    weight = row_total(base, base)
    shift = jnp.where(weight > 0.0, row_total(base, value) / jnp.where(weight > 0.0, weight, 1.0), 0.0)
    value = value - shift * base
    image = image - (2.0 * shift) * value - (shift * shift) * base
    first_rest[...] = value
    second_rest[...] = image
    shift_out[...] = jnp.broadcast_to(shift, shift_out.shape)
    slope = slope_sum[...]
    parts = (
        shift,
        weight,
        row_total(value, value),
        row_total(value, image),
        row_total(base, image),
        row_total(base, value),
        row_total(base, slope),
        row_total(value, slope),
    )
    lane = lax.broadcasted_iota(jnp.int32, (16, 128), 1)
    row = lax.broadcasted_iota(jnp.int32, (16, 128), 0)
    packed = jnp.zeros((16, 128), FULL)
    for slot, part in enumerate(parts):
        packed = jnp.where(lane == row + 16 * slot, part, packed)
    sums[...] = jnp.broadcast_to(jnp.sum(packed, axis=0, keepdims=True), sums.shape)


def last_kernel(point_total, signal, noise, numbers, table, shift_in, first_rest, second_rest, given, out, res, trace):
    gathered = table[...]
    shift = gathered

    def slot(index):
        return pltpu.roll(gathered, 128 - 16 * index, 1)

    weight, ww, wz, rz, rw, rs, ws = (slot(index) for index in range(1, 8))

    def total(value):
        return jnp.sum(value, axis=0, keepdims=True)

    gain = signal[0] / SCALE
    rate = numbers[0:1, :]
    norm = total(weight)
    center = total(shift * weight + rw) / norm
    off = shift - center
    cross = total(rw + off * weight)
    square = total(ww + 2.0 * off * rw + off * off * weight)
    mixed = total(rz + 2.0 * off * rw + off * off * weight)
    second = total(
        wz + 2.0 * off * ww + off * off * rw + off * rz + 2.0 * off * off * rw + off * off * off * weight
    )
    held = total(rs)
    along = total(ws + off * rs)
    cross = gain * cross
    square = (gain * gain) * square
    mixed = (gain * gain) * mixed
    second = (gain * gain) * gain * second
    level = noise[0] + gain * center
    lead = level * norm + cross
    alpha = norm / lead
    part = cross / lead
    norm_next = part * part * norm - 2.0 * part * alpha * cross + alpha * alpha * square
    lean = part + norm_next / norm
    direction = lean * lean * norm - 2.0 * lean * alpha * cross + alpha * alpha * square
    bend = lean * lean * cross - lean * alpha * (mixed + square) + alpha * alpha * second
    beta = norm_next / (level * direction + bend)
    factor = signal[0] * (rate * rate)
    trace[...] = (((alpha + beta * lean) * held - beta * alpha * gain * along) * factor / point_total)[:, 0:16]

    lane = lax.broadcasted_iota(jnp.int32, (16, 128), 1)
    row = lax.broadcasted_iota(jnp.int32, (16, 128), 0)

    def column(value):
        return jnp.sum(jnp.where(lane == row, value, 0.0), axis=1, keepdims=True)

    own_off = shift_in[:, 0:1] - column(center)
    base = given[0:16, :]
    rest = first_rest[...]
    value = rest + own_off * base
    image = second_rest[...] + (2.0 * own_off) * rest + (own_off * own_off) * base
    out[...] = column(alpha + beta * lean) * base - column(beta * alpha * gain) * value
    res[...] = (
        column(part - beta * level * lean) * base
        - column((alpha - beta * level * alpha + beta * lean) * gain) * value
        + column(beta * alpha * gain * gain) * image
    )


def slope_kernel(signal, numbers, source, dest):
    rate = numbers[0:1, 0:1]
    dest[...] = (signal[0] * rate * rate) * source[...]


def call(kernel, outs, spaces, scratch=(), micros=2.0):
    params = pltpu.CompilerParams(vmem_limit_bytes=40 * 2**20)
    cost = pl.CostEstimate(flops=int(micros * 1e9), bytes_accessed=2**16, transcendentals=0)
    return pl.pallas_call(
        kernel,
        out_shape=[jax.ShapeDtypeStruct(shape, kind) for shape, kind in outs],
        in_specs=[pl.BlockSpec(memory_space=space) for space in spaces],
        out_specs=[pl.BlockSpec(memory_space=VMEM) for _ in outs],
        scratch_shapes=list(scratch),
        compiler_params=params,
        cost_estimate=cost,
    )


def shards(points, right_sides, skeleton, lengthscale, far_length, signal, noise_var):
    probes, rows = right_sides.shape
    levels, rank = skeleton.shape
    half = levels // 2
    count = lax.axis_size("loc")
    far_scale = 1.0 / (rank * rank * levels)
    beside = [(i, i ^ 1) for i in range(count)]
    across = [(i, i + 1) for i in range(1, count - 1, 2)]
    across = across + [(j, i) for i, j in across]

    def partner(value, slot):
        pairs = [(i, i ^ (2 << (2 * slot + i % 2))) for i in range(count)]
        return lax.ppermute(value, "loc", pairs)

    def sibling(value):
        return lax.ppermute(value, "loc", beside)

    def sides(value):
        return lax.ppermute(value, "loc", beside), lax.ppermute(value, "loc", across)

    height = -(-(24 + levels) // 8) * 8
    given = jnp.pad(right_sides, ((0, height - probes), (0, 0)))
    given += jnp.pad(points, ((16, height - 19), (0, 0)))
    given += jnp.pad(skeleton, ((24, height - 24 - levels), (0, rows - rank))).astype(FULL)
    msg, target, basis, skel_target, numbers, keep, give = call(
        functools.partial(front_kernel, levels),
        [
            ((MSG_ROWS, rows), HALF),
            ((SRC_ROWS, rows), HALF),
            ((levels * rank, rows), HALF),
            ((levels, SRC_ROWS, rank), HALF),
            ((8, 128), FULL),
            ((half, 96, rank), HALF),
            ((half, 96, rank), HALF),
        ],
        [SMEM, SMEM, VMEM],
        [
            VMEM((SRC_ROWS, rows), FULL),
            VMEM((2 * SRC_ROWS, rows), HALF),
            VMEM((levels * rank, SRC_ROWS), HALF),
        ],
    )(lengthscale, far_length, given)
    got = sibling(give)
    msg_a, msg_b = sides(msg)
    near_outs = [((rows, rows), HALF), ((32, rows), FULL), ((probes, rows), FULL)]
    turned_buf = [VMEM((rows, SRC_ROWS), HALF)]
    kept, image, slopes, *packs = call(
        own_kernel,
        near_outs + [((2, 96, rank), HALF)] * half,
        [VMEM] * 5,
        turned_buf,
    )(numbers, msg, target, keep, got)
    cross = [partner(pack, slot) for slot, pack in enumerate(packs)]
    kept_a, image, slopes = call(side_kernel, near_outs, [VMEM] * 5, turned_buf)(numbers, msg_a, target, image, slopes)
    other = [sibling(value) for value in cross]
    kept_b, image, slopes = call(side_kernel, near_outs, [VMEM] * 5, turned_buf)(numbers, msg_b, target, image, slopes)
    coup_high, coup_low, row_sum, first, wmsg, keep, give = call(
        functools.partial(far_kernel, half, far_scale),
        [
            ((levels, rank, rank), HALF),
            ((levels, rank, rank), HALF),
            ((1, rows), FULL),
            ((probes, rows), FULL),
            ((2 * probes, rows), HALF),
            ((half, 2 * probes, rank), HALF),
            ((half, 2 * probes, rank), HALF),
        ],
        [VMEM] * (5 + levels),
    )(numbers, image, given, basis, skel_target, *cross, *other)
    got = sibling(give)
    wmsg_a, wmsg_b = sides(wmsg)
    packs = call(pack_kernel, [((2, 2 * probes, rank), HALF)] * half, [VMEM] * 2, micros=0.1)(keep, got)
    cross = [partner(pack, slot) for slot, pack in enumerate(packs)]
    (near,) = call(near_kernel, [((2 * probes, rows), FULL)], [VMEM] * 6, micros=1.2)(wmsg, wmsg_a, wmsg_b, kept, kept_a, kept_b)
    other = [sibling(value) for value in cross]
    sums, first_rest, second_rest, shift = call(
        functools.partial(second_kernel, half, far_scale),
        [((count, 128), FULL), ((probes, rows), FULL), ((probes, rows), FULL), ((probes, 128), FULL)],
        [VMEM] * (8 + levels),
    )(near, basis, coup_high, coup_low, row_sum, first, given, slopes, *cross, *other)
    sums, signal, noise_var = lax.optimization_barrier((sums, signal, noise_var))
    table = lax.all_to_all(sums, "loc", 0, 0, tiled=True)
    (slope_image,) = call(slope_kernel, [((probes, rows), FULL)], [SMEM, VMEM, VMEM])(signal, numbers, slopes)
    solution, residual, trace = call(
        functools.partial(last_kernel, float(rows * count)),
        [((probes, rows), FULL), ((probes, rows), FULL), ((1, probes), FULL)],
        [SMEM, SMEM] + [VMEM] * 6,
    )(signal, noise_var, numbers, table, shift, first_rest, second_rest, given)
    return (solution, residual, slope_image, trace.reshape(probes))


def solution(mesh):
    placed = (P(None, "loc"), P(None, "loc"), P(None, "loc"), P(), P(), P(), P())
    return jax.shard_map(
        shards,
        mesh=mesh,
        in_specs=placed,
        out_specs=(P(None, "loc"), P(None, "loc"), P(None, "loc"), P()),
        check_vma=False,
    )
```

```python
import functools

import jax
import jax.numpy as jnp
from jax import lax
from jax.experimental import pallas as pl
from jax.experimental.pallas import tpu as pltpu
from jax.sharding import PartitionSpec as P

HALF = jnp.bfloat16
FULL = jnp.float32
LOG2_E = 1.4426950408889634
ROOT_THREE = 1.7320508075688772
TINY = 1e-30
SCALE = 2.0**-10
SRC_ROWS = 32
MSG_ROWS = 64
VEC_ROWS = 48
TILE = 128
WIDE_TILE = 512
VMEM = pltpu.VMEM
SMEM = pltpu.SMEM


def split_two(value):
    high = value.astype(HALF)
    low = (value - high.astype(FULL)).astype(HALF)
    return high, low


def split_three(value):
    first = value.astype(HALF).astype(FULL)
    rest = value - first
    second = rest.astype(HALF).astype(FULL)
    third = (rest - second).astype(HALF).astype(FULL)
    return first, second, third


def matern(squared, rates):
    rate, falling_rate = rates
    squared = jnp.maximum(squared, TINY)
    radius = squared * lax.rsqrt(squared)
    decay = jnp.exp2(radius * falling_rate)
    falling = radius * decay
    return decay + rate * falling, radius * falling


def excess(pts):
    total = jnp.full((1, pts.shape[1]), -1.0, FULL)
    lost = jnp.zeros_like(total)
    small = jnp.zeros_like(total)
    for axis in range(3):
        value = pts[axis : axis + 1, :]
        head = value.astype(HALF).astype(FULL)
        tail = value - head
        small = small + tail * tail
        for term in (head * head, 2.0 * head * tail):
            grown = total + term
            back = grown - total
            lost = lost + ((total - (grown - back)) + (term - back))
            total = grown
    return total + (lost + small)


def write_rows(buf, base, pts, source):
    over = excess(pts)
    first = over.astype(HALF).astype(FULL)
    second = over - first
    unit = jnp.ones_like(over)
    if source:
        rows = (unit, unit, unit, first, second)
        order = (0, 0, 0, 1, 1, 1, 2, 2, 2)
        pieces = split_three(pts)
    else:
        rows = (unit + unit, first, second, unit, unit)
        order = (0, 1, 2, 0, 1, 2, 0, 1, 2)
        pieces = split_three(-2.0 * pts)
    for slot, row in enumerate(rows):
        buf[base + slot : base + slot + 1, :] = row
    for slot, index in enumerate(order):
        start = base + 5 + 3 * slot
        buf[start : start + 3, :] = pieces[index]


def dot(a, b):
    return jnp.dot(a, b, preferred_element_type=FULL)


def dot_rows(a, b):
    return lax.dot_general(a, b, (((1,), (1,)), ((), ())), preferred_element_type=FULL)


def turned(value):
    return value.astype(FULL).T.astype(HALF)


def merged(both):
    return jnp.concatenate([both[0:16] + both[16:32], both[32:48]], axis=0)


def on_first_core():
    return lax.rem(lax.axis_index("loc"), 2) == 0


def gather_share(keep, got, packs):
    first = on_first_core()
    for slot, pack in enumerate(packs):
        pack[0] = jnp.where(first, keep[slot], got[slot])
        pack[1] = jnp.where(first, got[slot], keep[slot])


def own_part(values):
    first = on_first_core()
    return [jnp.where(first, value[0], value[1]) for value in values]


def front_kernel(levels, *refs):
    length, far_length, given = refs[:3]
    msg, target, basis, skel_target, numbers, keep, give = refs[3:10]
    buf, pair_buf, turned_src = refs[10:]
    points = given[16:19, :]
    for slot, value in enumerate((length[0], far_length[0])):
        lengths = jnp.full((1, 128), value, FULL)
        numbers[slot : slot + 1, :] = ROOT_THREE / lengths
        numbers[slot + 2 : slot + 3, :] = (-LOG2_E * ROOT_THREE) / lengths
    write_rows(buf, 0, points, False)
    target[...] = buf[...].astype(HALF)
    pair_buf[SRC_ROWS:, :] = buf[...].astype(HALF)
    write_rows(buf, 0, points, True)
    pair_buf[0:SRC_ROWS, :] = buf[...].astype(HALF)
    msg[32:64, :] = buf[...].astype(HALF)
    rows, rank = points.shape[1], skel_target.shape[2]
    first = on_first_core()
    skel = [given[24 + level : 25 + level, 0:rank] for level in range(levels)]
    order = [jnp.where(first, skel[level], skel[level + 1]) for level in range(0, levels, 2)]
    order += [jnp.where(first, skel[level + 1], skel[level]) for level in range(0, levels, 2)]
    stride = rows // rank
    shift = stride.bit_length() - 1
    spot = lax.broadcasted_iota(jnp.int32, (rows, rank), 0)
    slot = lax.broadcasted_iota(jnp.int32, (rows, rank), 1)
    group = jnp.where(lax.shift_right_logical(spot, shift) == slot, 1.0, 0.0).astype(HALF)
    steps = lax.broadcasted_iota(jnp.int32, (len(order), rank), 1).astype(FULL) * stride
    wanted = dot_rows((jnp.concatenate(order, axis=0) - steps).astype(HALF), group)
    place = jnp.bitwise_and(lax.broadcasted_iota(jnp.int32, wanted.shape, 1), stride - 1).astype(FULL)
    chosen = jnp.where(wanted == place, 1.0, 0.0).astype(HALF)
    both_rows = pair_buf[...]
    picked = dot(jnp.concatenate([both_rows * chosen[level : level + 1] for level in range(levels)], axis=0), group)
    sources = []
    for level in range(levels):
        skel_source = picked[2 * SRC_ROWS * level : 2 * SRC_ROWS * level + SRC_ROWS]
        skel_target[level] = picked[2 * SRC_ROWS * level + SRC_ROWS : 2 * SRC_ROWS * (level + 1)].astype(HALF)
        sources.append(skel_source.astype(HALF))
        turned_src[level * rank : (level + 1) * rank, :] = skel_source.T.astype(HALF)
    rates = [jnp.concatenate([numbers[row : row + 1, :]] * (WIDE_TILE // 128), axis=1) for row in (1, 3)]
    for col in range(0, rows, WIDE_TILE):
        squared = dot(turned_src[...], target[:, col : col + WIDE_TILE])
        basis[:, col : col + WIDE_TILE] = matern(squared, rates)[0].astype(HALF)
    high, low = split_two(given[0:16, :])
    msg[0:16, :] = low
    msg[16:32, :] = high
    coef = merged(dot_rows(msg[0:VEC_ROWS, :], basis[...]))
    for level in range(levels):
        high, low = split_two(coef[:, level * rank : (level + 1) * rank])
        dest = keep.at[level] if level < levels // 2 else give.at[level - levels // 2]
        dest[0:32, :] = high
        dest[32:64, :] = low
        dest[64:96, :] = sources[level]


def near_block(msg, target, turned_src, rates, kept):
    rows = target.shape[1]
    turned_src[...] = turned(msg[32:64, :])
    for col in range(0, rows, TILE):
        squared = dot(turned_src[...], target[:, col : col + TILE])
        value, slope = matern(squared, rates)
        value = value.astype(HALF)
        kept[:, col : col + TILE] = value
        pair = jnp.concatenate([value, slope.astype(HALF)], axis=1)
        total = dot(msg[0:VEC_ROWS, :], pair)
        yield slice(col, col + TILE), merged(total[:, :TILE]), total[16:32, TILE:]


def own_kernel(numbers, msg, target, keep, got, kept, image, slopes, *rest):
    packs, turned_src = rest[:-1], rest[-1]
    gather_share(keep, got, packs)
    rates = numbers[0:1, :], numbers[2:3, :]
    for span, part, slope in near_block(msg, target, turned_src, rates, kept):
        image[:, span] = part
        slopes[:, span] = slope


def side_kernel(numbers, msg, target, image_in, slopes_in, kept, image, slopes, turned_src):
    rates = numbers[0:1, :], numbers[2:3, :]
    for span, part, slope in near_block(msg, target, turned_src, rates, kept):
        image[:, span] = image_in[:, span] + part
        slopes[:, span] = slopes_in[:, span] + slope


def far_part(lev, start, numbers, skel_target, basis, coup_high, coup_low):
    rank = skel_target.shape[2]
    rates = [jnp.concatenate([numbers[row : row + 1, :]] * (rank // 128), axis=1) for row in (1, 3)]
    mixed = []
    for slot, value in enumerate(lev):
        squared = dot(turned(value[64:96]), skel_target[start + slot])
        high, low = split_two(matern(squared, rates)[0])
        coup_high[slot] = high
        coup_low[slot] = low
        both = dot(value[0:64], high)
        part = both[0:32] + both[32:64] + dot(value[0:32], low)
        mixed.append(jnp.concatenate(split_two(part), axis=0))
    far = dot(jnp.concatenate(mixed, axis=1), basis[start * rank : (start + len(lev)) * rank, :])
    return far[0:32] + far[32:64]


def carried_kernel(half, far_scale, *refs):
    numbers, image_in, basis, skel_target = refs[:4]
    lev = own_part(refs[4 : 4 + half])
    image, coup_high, coup_low = refs[4 + half :]
    image[...] = image_in[...] + far_scale * far_part(lev, 0, numbers, skel_target, basis, coup_high, coup_low)


def far_kernel(half, far_scale, *refs):
    numbers, image, given, basis, skel_target = refs[:5]
    lev = own_part(refs[5 : 5 + half])
    coup_high, coup_low, row_sum, first, wmsg, keep, give = refs[5 + half :]
    rank = skel_target.shape[2]
    total = image[...] + far_scale * far_part(lev, half, numbers, skel_target, basis, coup_high, coup_low)
    sums = total[16:17, :]
    row_sum[...] = sums
    value = SCALE * (total[0:16] + sums * given[0:16, :])
    first[...] = value
    high, low = split_two(value)
    wmsg[0:16, :] = high
    wmsg[16:32, :] = low
    both = dot_rows(wmsg[...], basis[...])
    high, low = split_two(both[0:16] + both[16:32])
    for slot in range(2 * half):
        dest = keep.at[slot] if slot < half else give.at[slot - half]
        span = slice(slot * rank, (slot + 1) * rank)
        dest[0:16, :] = high[:, span]
        dest[16:32, :] = low[:, span]


def pack_kernel(keep, got, *packs):
    gather_share(keep, got, packs)


def near_kernel(wmsg, wmsg_a, wmsg_b, kept, kept_a, kept_b, out):
    out[...] = dot(wmsg[...], kept[...]) + dot(wmsg_a[...], kept_a[...]) + dot(wmsg_b[...], kept_b[...])


def row_total(a, b):
    return jnp.sum(a * b, axis=1, keepdims=True)


def second_kernel(half, far_scale, *refs):
    near, basis, own_high, own_low, other_high, other_low, row_sum, first, given, slope_sum = refs[:10]
    wlev = own_part(refs[10 : 10 + 2 * half])
    sums, first_rest, second_rest, shift_out = refs[10 + 2 * half :]
    coup_high = [own_high[slot] for slot in range(half)] + [other_high[slot] for slot in range(half)]
    coup_low = [own_low[slot] for slot in range(half)] + [other_low[slot] for slot in range(half)]
    pieces = []
    for coef, high, low in zip(wlev, coup_high, coup_low):
        mixed = dot(coef, high)
        mixed = mixed[0:16] + mixed[16:32] + dot(coef[0:16], low)
        pieces.append(jnp.concatenate(split_two(mixed), axis=0))
    both = near[...] + far_scale * dot(jnp.concatenate(pieces, axis=1), basis[...])
    base = given[0:16, :]
    value = first[...]
    image = SCALE * (both[0:16] + both[16:32] + row_sum[...] * value)
    weight = row_total(base, base)
    shift = jnp.where(weight > 0.0, row_total(base, value) / jnp.where(weight > 0.0, weight, 1.0), 0.0)
    value = value - shift * base
    image = image - (2.0 * shift) * value - (shift * shift) * base
    first_rest[...] = value
    second_rest[...] = image
    shift_out[...] = jnp.broadcast_to(shift, shift_out.shape)
    slope = slope_sum[...]
    parts = (
        shift,
        weight,
        row_total(value, value),
        row_total(value, image),
        row_total(base, image),
        row_total(base, value),
        row_total(base, slope),
        row_total(value, slope),
    )
    lane = lax.broadcasted_iota(jnp.int32, (16, 128), 1)
    row = lax.broadcasted_iota(jnp.int32, (16, 128), 0)
    packed = jnp.zeros((16, 128), FULL)
    for slot, part in enumerate(parts):
        packed = jnp.where(lane == row + 16 * slot, part, packed)
    sums[...] = jnp.broadcast_to(jnp.sum(packed, axis=0, keepdims=True), sums.shape)


def last_kernel(point_total, signal, noise, numbers, table, shift_in, first_rest, second_rest, given, out, res, trace):
    gathered = table[...]
    shift = gathered

    def slot(index):
        return pltpu.roll(gathered, 128 - 16 * index, 1)

    weight, ww, wz, rz, rw, rs, ws = (slot(index) for index in range(1, 8))

    def total(value):
        return jnp.sum(value, axis=0, keepdims=True)

    gain = signal[0] / SCALE
    rate = numbers[0:1, :]
    norm = total(weight)
    center = total(shift * weight + rw) / norm
    off = shift - center
    cross = total(rw + off * weight)
    square = total(ww + 2.0 * off * rw + off * off * weight)
    mixed = total(rz + 2.0 * off * rw + off * off * weight)
    second = total(
        wz + 2.0 * off * ww + off * off * rw + off * rz + 2.0 * off * off * rw + off * off * off * weight
    )
    held = total(rs)
    along = total(ws + off * rs)
    cross = gain * cross
    square = (gain * gain) * square
    mixed = (gain * gain) * mixed
    second = (gain * gain) * gain * second
    level = noise[0] + gain * center
    lead = level * norm + cross
    alpha = norm / lead
    part = cross / lead
    norm_next = part * part * norm - 2.0 * part * alpha * cross + alpha * alpha * square
    lean = part + norm_next / norm
    direction = lean * lean * norm - 2.0 * lean * alpha * cross + alpha * alpha * square
    bend = lean * lean * cross - lean * alpha * (mixed + square) + alpha * alpha * second
    beta = norm_next / (level * direction + bend)
    factor = signal[0] * (rate * rate)
    trace[...] = (((alpha + beta * lean) * held - beta * alpha * gain * along) * factor / point_total)[:, 0:16]

    lane = lax.broadcasted_iota(jnp.int32, (16, 128), 1)
    row = lax.broadcasted_iota(jnp.int32, (16, 128), 0)

    def column(value):
        return jnp.sum(jnp.where(lane == row, value, 0.0), axis=1, keepdims=True)

    own_off = shift_in[:, 0:1] - column(center)
    base = given[0:16, :]
    rest = first_rest[...]
    value = rest + own_off * base
    image = second_rest[...] + (2.0 * own_off) * rest + (own_off * own_off) * base
    out[...] = column(alpha + beta * lean) * base - column(beta * alpha * gain) * value
    res[...] = (
        column(part - beta * level * lean) * base
        - column((alpha - beta * level * alpha + beta * lean) * gain) * value
        + column(beta * alpha * gain * gain) * image
    )


def slope_kernel(signal, numbers, source, dest):
    rate = numbers[0:1, 0:1]
    dest[...] = (signal[0] * rate * rate) * source[...]


def call(kernel, outs, spaces, scratch=(), micros=2.0):
    params = pltpu.CompilerParams(vmem_limit_bytes=40 * 2**20)
    cost = pl.CostEstimate(flops=int(micros * 1e9), bytes_accessed=2**16, transcendentals=0)
    return pl.pallas_call(
        kernel,
        out_shape=[jax.ShapeDtypeStruct(shape, kind) for shape, kind in outs],
        in_specs=[pl.BlockSpec(memory_space=space) for space in spaces],
        out_specs=[pl.BlockSpec(memory_space=VMEM) for _ in outs],
        scratch_shapes=list(scratch),
        compiler_params=params,
        cost_estimate=cost,
    )


def shards(points, right_sides, skeleton, lengthscale, far_length, signal, noise_var):
    probes, rows = right_sides.shape
    levels, rank = skeleton.shape
    half = levels // 2
    count = lax.axis_size("loc")
    far_scale = 1.0 / (rank * rank * levels)
    beside = [(i, i ^ 1) for i in range(count)]
    across = [(i, i + 1) for i in range(1, count - 1, 2)]
    across = across + [(j, i) for i, j in across]

    def partner(value, slot):
        pairs = [(i, i ^ (2 << (2 * slot + i % 2))) for i in range(count)]
        return lax.ppermute(value, "loc", pairs)

    def sibling(value):
        return lax.ppermute(value, "loc", beside)

    def sides(value):
        return lax.ppermute(value, "loc", beside), lax.ppermute(value, "loc", across)

    height = -(-(24 + levels) // 8) * 8
    given = jnp.pad(right_sides, ((0, height - probes), (0, 0)))
    given += jnp.pad(points, ((16, height - 19), (0, 0)))
    given += jnp.pad(skeleton, ((24, height - 24 - levels), (0, rows - rank))).astype(FULL)
    msg, target, basis, skel_target, numbers, keep, give = call(
        functools.partial(front_kernel, levels),
        [
            ((MSG_ROWS, rows), HALF),
            ((SRC_ROWS, rows), HALF),
            ((levels * rank, rows), HALF),
            ((levels, SRC_ROWS, rank), HALF),
            ((8, 128), FULL),
            ((half, 96, rank), HALF),
            ((half, 96, rank), HALF),
        ],
        [SMEM, SMEM, VMEM],
        [
            VMEM((SRC_ROWS, rows), FULL),
            VMEM((2 * SRC_ROWS, rows), HALF),
            VMEM((levels * rank, SRC_ROWS), HALF),
        ],
    )(lengthscale, far_length, given)
    got = sibling(give)
    msg_a, msg_b = sides(msg)
    near_outs = [((rows, rows), HALF), ((32, rows), FULL), ((probes, rows), FULL)]
    turned_buf = [VMEM((rows, SRC_ROWS), HALF)]
    kept, image, slopes, *packs = call(
        own_kernel,
        near_outs + [((2, 96, rank), HALF)] * half,
        [VMEM] * 5,
        turned_buf,
    )(numbers, msg, target, keep, got)
    cross = [partner(pack, slot) for slot, pack in enumerate(packs)]
    kept_a, image, slopes = call(side_kernel, near_outs, [VMEM] * 5, turned_buf)(numbers, msg_a, target, image, slopes)
    kept_b, image, slopes = call(side_kernel, near_outs, [VMEM] * 5, turned_buf)(numbers, msg_b, target, image, slopes)
    image, cross = lax.optimization_barrier((image, cross))
    other = [sibling(value) for value in cross]
    couplings = [((half, rank, rank), HALF)] * 2
    image, own_high, own_low = call(
        functools.partial(carried_kernel, half, far_scale), [((32, rows), FULL)] + couplings, [VMEM] * (4 + half), micros=1.0
    )(numbers, image, basis, skel_target, *cross)
    other_high, other_low, row_sum, first, wmsg, keep, give = call(
        functools.partial(far_kernel, half, far_scale),
        couplings
        + [
            ((1, rows), FULL),
            ((probes, rows), FULL),
            ((2 * probes, rows), HALF),
            ((half, 2 * probes, rank), HALF),
            ((half, 2 * probes, rank), HALF),
        ],
        [VMEM] * (5 + half),
    )(numbers, image, given, basis, skel_target, *other)
    got = sibling(give)
    wmsg_a, wmsg_b = sides(wmsg)
    packs = call(pack_kernel, [((2, 2 * probes, rank), HALF)] * half, [VMEM] * 2, micros=0.1)(keep, got)
    cross = [partner(pack, slot) for slot, pack in enumerate(packs)]
    (near,) = call(near_kernel, [((2 * probes, rows), FULL)], [VMEM] * 6, micros=1.2)(wmsg, wmsg_a, wmsg_b, kept, kept_a, kept_b)
    other = [sibling(value) for value in cross]
    sums, first_rest, second_rest, shift = call(
        functools.partial(second_kernel, half, far_scale),
        [((count, 128), FULL), ((probes, rows), FULL), ((probes, rows), FULL), ((probes, 128), FULL)],
        [VMEM] * (10 + levels),
    )(near, basis, own_high, own_low, other_high, other_low, row_sum, first, given, slopes, *cross, *other)
    sums, signal, noise_var = lax.optimization_barrier((sums, signal, noise_var))
    table = lax.all_to_all(sums, "loc", 0, 0, tiled=True)
    (slope_image,) = call(slope_kernel, [((probes, rows), FULL)], [SMEM, VMEM, VMEM])(signal, numbers, slopes)
    solution, residual, trace = call(
        functools.partial(last_kernel, float(rows * count)),
        [((probes, rows), FULL), ((probes, rows), FULL), ((1, probes), FULL)],
        [SMEM, SMEM] + [VMEM] * 6,
    )(signal, noise_var, numbers, table, shift, first_rest, second_rest, given)
    return (solution, residual, slope_image, trace.reshape(probes))


def solution(mesh):
    placed = (P(None, "loc"), P(None, "loc"), P(None, "loc"), P(), P(), P(), P())
    return jax.shard_map(
        shards,
        mesh=mesh,
        in_specs=placed,
        out_specs=(P(None, "loc"), P(None, "loc"), P(None, "loc"), P()),
        check_vma=False,
    )
```

```python
import functools

import jax
import jax.numpy as jnp
from jax import lax
from jax.experimental import pallas as pl
from jax.experimental.pallas import tpu as pltpu
from jax.sharding import PartitionSpec as P

HALF = jnp.bfloat16
FULL = jnp.float32
LOG2_E = 1.4426950408889634
ROOT_THREE = 1.7320508075688772
TINY = 1e-30
SCALE = 2.0**-10
SRC_ROWS = 32
MSG_ROWS = 64
VEC_ROWS = 48
TILE = 128
WIDE_TILE = 256
VMEM = pltpu.VMEM
SMEM = pltpu.SMEM


def split_two(value):
    high = value.astype(HALF)
    low = (value - high.astype(FULL)).astype(HALF)
    return high, low


def split_three(value):
    first = value.astype(HALF).astype(FULL)
    rest = value - first
    second = rest.astype(HALF).astype(FULL)
    third = (rest - second).astype(HALF).astype(FULL)
    return first, second, third


def matern(squared, rates):
    rate, falling_rate = rates
    squared = jnp.maximum(squared, TINY)
    radius = squared * lax.rsqrt(squared)
    decay = jnp.exp2(radius * falling_rate)
    falling = radius * decay
    return decay + rate * falling, radius * falling


def excess(pts):
    total = jnp.full((1, pts.shape[1]), -1.0, FULL)
    lost = jnp.zeros_like(total)
    small = jnp.zeros_like(total)
    for axis in range(3):
        value = pts[axis : axis + 1, :]
        head = value.astype(HALF).astype(FULL)
        tail = value - head
        small = small + tail * tail
        for term in (head * head, 2.0 * head * tail):
            grown = total + term
            back = grown - total
            lost = lost + ((total - (grown - back)) + (term - back))
            total = grown
    return total + (lost + small)


def write_rows(buf, base, pts, source):
    over = excess(pts)
    first = over.astype(HALF).astype(FULL)
    second = over - first
    unit = jnp.ones_like(over)
    if source:
        rows = (unit, unit, unit, first, second)
        order = (0, 0, 0, 1, 1, 1, 2, 2, 2)
        pieces = split_three(pts)
    else:
        rows = (unit + unit, first, second, unit, unit)
        order = (0, 1, 2, 0, 1, 2, 0, 1, 2)
        pieces = split_three(-2.0 * pts)
    for slot, row in enumerate(rows):
        buf[base + slot : base + slot + 1, :] = row
    for slot, index in enumerate(order):
        start = base + 5 + 3 * slot
        buf[start : start + 3, :] = pieces[index]


def dot(a, b):
    return jnp.dot(a, b, preferred_element_type=FULL)


def dot_rows(a, b):
    return lax.dot_general(a, b, (((1,), (1,)), ((), ())), preferred_element_type=FULL)


def turned(value):
    return value.astype(FULL).T.astype(HALF)


def merged(both):
    return jnp.concatenate([both[0:16] + both[16:32], both[32:48]], axis=0)


def on_first_core():
    return lax.rem(lax.axis_index("loc"), 2) == 0


def gather_share(keep, got, packs):
    first = on_first_core()
    for slot, pack in enumerate(packs):
        pack[0] = jnp.where(first, keep[slot], got[slot])
        pack[1] = jnp.where(first, got[slot], keep[slot])


def own_part(values):
    first = on_first_core()
    return [jnp.where(first, value[0], value[1]) for value in values]


def front_kernel(levels, *refs):
    length, far_length, given = refs[:3]
    msg, target, basis, skel_target, numbers, keep, give = refs[3:10]
    buf, pair_buf, turned_src = refs[10:]
    points = given[16:19, :]
    for slot, value in enumerate((length[0], far_length[0])):
        lengths = jnp.full((1, 128), value, FULL)
        numbers[slot : slot + 1, :] = ROOT_THREE / lengths
        numbers[slot + 2 : slot + 3, :] = (-LOG2_E * ROOT_THREE) / lengths
    write_rows(buf, 0, points, False)
    target[...] = buf[...].astype(HALF)
    pair_buf[SRC_ROWS:, :] = buf[...].astype(HALF)
    write_rows(buf, 0, points, True)
    pair_buf[0:SRC_ROWS, :] = buf[...].astype(HALF)
    msg[32:64, :] = buf[...].astype(HALF)
    rows, rank = points.shape[1], skel_target.shape[2]
    first = on_first_core()
    skel = [given[24 + level : 25 + level, 0:rank] for level in range(levels)]
    order = [jnp.where(first, skel[level], skel[level + 1]) for level in range(0, levels, 2)]
    order += [jnp.where(first, skel[level + 1], skel[level]) for level in range(0, levels, 2)]
    spot = lax.broadcasted_iota(jnp.int32, (rows, rank), 0).astype(FULL)
    sources = []
    for level in range(levels):
        picks = jnp.where(spot == order[level], 1.0, 0.0).astype(HALF)
        both = dot(pair_buf[...], picks)
        skel_target[level] = both[SRC_ROWS:].astype(HALF)
        skel_source = both[:SRC_ROWS]
        sources.append(skel_source.astype(HALF))
        turned_src[level * rank : (level + 1) * rank, :] = skel_source.T.astype(HALF)
    rates = [jnp.concatenate([numbers[row : row + 1, :]] * (WIDE_TILE // 128), axis=1) for row in (1, 3)]
    for row in range(0, levels * rank, 1024):
        for col in range(0, rows, WIDE_TILE):
            squared = dot(turned_src[row : row + 1024, :], target[:, col : col + WIDE_TILE])
            basis[row : row + 1024, col : col + WIDE_TILE] = matern(squared, rates)[0].astype(HALF)
    high, low = split_two(given[0:16, :])
    msg[0:16, :] = low
    msg[16:32, :] = high
    coef = merged(dot_rows(msg[0:VEC_ROWS, :], basis[...]))
    for level in range(levels):
        high, low = split_two(coef[:, level * rank : (level + 1) * rank])
        dest = keep.at[level] if level < levels // 2 else give.at[level - levels // 2]
        dest[0:32, :] = high
        dest[32:64, :] = low
        dest[64:96, :] = sources[level]


def near_block(msg, target, turned_src, rates, kept):
    rows = target.shape[1]
    turned_src[...] = turned(msg[32:64, :])
    for col in range(0, rows, TILE):
        squared = dot(turned_src[...], target[:, col : col + TILE])
        value, slope = matern(squared, rates)
        value = value.astype(HALF)
        kept[:, col : col + TILE] = value
        pair = jnp.concatenate([value, slope.astype(HALF)], axis=1)
        total = dot(msg[0:VEC_ROWS, :], pair)
        yield slice(col, col + TILE), merged(total[:, :TILE]), total[16:32, TILE:]


def own_kernel(numbers, msg, target, keep, got, kept, image, slopes, *rest):
    packs, turned_src = rest[:-1], rest[-1]
    gather_share(keep, got, packs)
    rates = numbers[0:1, :], numbers[2:3, :]
    for span, part, slope in near_block(msg, target, turned_src, rates, kept):
        image[:, span] = part
        slopes[:, span] = slope


def side_kernel(numbers, msg, target, image_in, slopes_in, kept, image, slopes, turned_src):
    rates = numbers[0:1, :], numbers[2:3, :]
    for span, part, slope in near_block(msg, target, turned_src, rates, kept):
        image[:, span] = image_in[:, span] + part
        slopes[:, span] = slopes_in[:, span] + slope


def far_part(lev, start, numbers, skel_target, basis, coup_high, coup_low):
    rank = skel_target.shape[2]
    rates = [jnp.concatenate([numbers[row : row + 1, :]] * (rank // 128), axis=1) for row in (1, 3)]
    mixed = []
    for slot, value in enumerate(lev):
        squared = dot(turned(value[64:96]), skel_target[start + slot])
        high, low = split_two(matern(squared, rates)[0])
        coup_high[slot] = high
        coup_low[slot] = low
        both = dot(value[0:64], high)
        part = both[0:32] + both[32:64] + dot(value[0:32], low)
        mixed.append(jnp.concatenate(split_two(part), axis=0))
    far = dot(jnp.concatenate(mixed, axis=1), basis[start * rank : (start + len(lev)) * rank, :])
    return far[0:32] + far[32:64]


def carried_kernel(half, far_scale, *refs):
    numbers, image_in, basis, skel_target = refs[:4]
    lev = own_part(refs[4 : 4 + half])
    image, coup_high, coup_low = refs[4 + half :]
    image[...] = image_in[...] + far_scale * far_part(lev, 0, numbers, skel_target, basis, coup_high, coup_low)


def far_kernel(half, far_scale, *refs):
    numbers, image, given, basis, skel_target = refs[:5]
    lev = own_part(refs[5 : 5 + half])
    coup_high, coup_low, row_sum, first, wmsg, keep, beside = refs[5 + half :]
    rank = skel_target.shape[2]
    total = image[...] + far_scale * far_part(lev, half, numbers, skel_target, basis, coup_high, coup_low)
    sums = total[16:17, :]
    row_sum[...] = sums
    value = SCALE * (total[0:16] + sums * given[0:16, :])
    first[...] = value
    high, low = split_two(value)
    rows = wmsg.shape[1]
    wmsg[0:16, :] = high
    wmsg[16:32, :] = low
    beside[0:16, 0:rows] = high
    beside[16:32, 0:rows] = low
    both = dot_rows(wmsg[...], basis[...])
    high, low = split_two(both[0:16] + both[16:32])
    keep[0:16, :] = high[:, : half * rank]
    keep[16:32, :] = low[:, : half * rank]
    beside[0:16, rows:] = high[:, half * rank :]
    beside[16:32, rows:] = low[:, half * rank :]


def pack_kernel(keep, got, *packs):
    rank = packs[0].shape[2]
    start = got.shape[1] - keep.shape[1]
    spans = [slice(slot * rank, (slot + 1) * rank) for slot in range(len(packs))]
    there = [slice(start + span.start, start + span.stop) for span in spans]
    gather_share([keep[:, span] for span in spans], [got[:, span] for span in there], packs)


def near_kernel(wmsg, wmsg_a, wmsg_b, kept, kept_a, kept_b, out):
    rows = kept_a.shape[0]
    out[...] = dot(wmsg[...], kept[...]) + dot(wmsg_a[:, 0:rows], kept_a[...]) + dot(wmsg_b[...], kept_b[...])


def row_total(a, b):
    return jnp.sum(a * b, axis=1, keepdims=True)


def second_kernel(half, far_scale, *refs):
    near, basis, own_high, own_low, other_high, other_low, row_sum, first, given, slope_sum = refs[:10]
    wlev = own_part(refs[10 : 10 + 2 * half])
    sums, first_rest, second_rest, shift_out = refs[10 + 2 * half :]
    coup_high = [own_high[slot] for slot in range(half)] + [other_high[slot] for slot in range(half)]
    coup_low = [own_low[slot] for slot in range(half)] + [other_low[slot] for slot in range(half)]
    pieces = []
    for coef, high, low in zip(wlev, coup_high, coup_low):
        mixed = dot(coef, high)
        mixed = mixed[0:16] + mixed[16:32] + dot(coef[0:16], low)
        pieces.append(jnp.concatenate(split_two(mixed), axis=0))
    both = near[...] + far_scale * dot(jnp.concatenate(pieces, axis=1), basis[...])
    base = given[0:16, :]
    value = first[...]
    image = SCALE * (both[0:16] + both[16:32] + row_sum[...] * value)
    weight = row_total(base, base)
    shift = jnp.where(weight > 0.0, row_total(base, value) / jnp.where(weight > 0.0, weight, 1.0), 0.0)
    value = value - shift * base
    image = image - (2.0 * shift) * value - (shift * shift) * base
    first_rest[...] = value
    second_rest[...] = image
    shift_out[...] = jnp.broadcast_to(shift, shift_out.shape)
    slope = slope_sum[...]
    parts = (
        shift,
        weight,
        row_total(value, value),
        row_total(value, image),
        row_total(base, image),
        row_total(base, value),
        row_total(base, slope),
        row_total(value, slope),
    )
    lane = lax.broadcasted_iota(jnp.int32, (16, 128), 1)
    row = lax.broadcasted_iota(jnp.int32, (16, 128), 0)
    packed = jnp.zeros((16, 128), FULL)
    for slot, part in enumerate(parts):
        packed = jnp.where(lane == row + 16 * slot, part, packed)
    sums[...] = jnp.broadcast_to(jnp.sum(packed, axis=0, keepdims=True), sums.shape)


def last_kernel(point_total, signal, noise, numbers, table, shift_in, first_rest, second_rest, given, out, res, trace):
    gathered = table[...]
    shift = gathered

    def slot(index):
        return pltpu.roll(gathered, 128 - 16 * index, 1)

    weight, ww, wz, rz, rw, rs, ws = (slot(index) for index in range(1, 8))

    def total(value):
        return jnp.sum(value, axis=0, keepdims=True)

    gain = signal[0] / SCALE
    rate = numbers[0:1, :]
    norm = total(weight)
    center = total(shift * weight + rw) / norm
    off = shift - center
    cross = total(rw + off * weight)
    square = total(ww + 2.0 * off * rw + off * off * weight)
    mixed = total(rz + 2.0 * off * rw + off * off * weight)
    second = total(
        wz + 2.0 * off * ww + off * off * rw + off * rz + 2.0 * off * off * rw + off * off * off * weight
    )
    held = total(rs)
    along = total(ws + off * rs)
    cross = gain * cross
    square = (gain * gain) * square
    mixed = (gain * gain) * mixed
    second = (gain * gain) * gain * second
    level = noise[0] + gain * center
    lead = level * norm + cross
    alpha = norm / lead
    part = cross / lead
    norm_next = part * part * norm - 2.0 * part * alpha * cross + alpha * alpha * square
    lean = part + norm_next / norm
    direction = lean * lean * norm - 2.0 * lean * alpha * cross + alpha * alpha * square
    bend = lean * lean * cross - lean * alpha * (mixed + square) + alpha * alpha * second
    beta = norm_next / (level * direction + bend)
    factor = signal[0] * (rate * rate)
    trace[...] = (((alpha + beta * lean) * held - beta * alpha * gain * along) * factor / point_total)[:, 0:16]

    lane = lax.broadcasted_iota(jnp.int32, (16, 128), 1)
    row = lax.broadcasted_iota(jnp.int32, (16, 128), 0)

    def column(value):
        return jnp.sum(jnp.where(lane == row, value, 0.0), axis=1, keepdims=True)

    own_off = shift_in[:, 0:1] - column(center)
    base = given[0:16, :]
    rest = first_rest[...]
    value = rest + own_off * base
    image = second_rest[...] + (2.0 * own_off) * rest + (own_off * own_off) * base
    out[...] = column(alpha + beta * lean) * base - column(beta * alpha * gain) * value
    res[...] = (
        column(part - beta * level * lean) * base
        - column((alpha - beta * level * alpha + beta * lean) * gain) * value
        + column(beta * alpha * gain * gain) * image
    )


def slope_kernel(signal, numbers, source, dest):
    rate = numbers[0:1, 0:1]
    dest[...] = (signal[0] * rate * rate) * source[...]


def call(kernel, outs, spaces, scratch=(), micros=2.0):
    params = pltpu.CompilerParams(vmem_limit_bytes=40 * 2**20)
    cost = pl.CostEstimate(flops=int(micros * 1e9), bytes_accessed=2**16, transcendentals=0)
    return pl.pallas_call(
        kernel,
        out_shape=[jax.ShapeDtypeStruct(shape, kind) for shape, kind in outs],
        in_specs=[pl.BlockSpec(memory_space=space) for space in spaces],
        out_specs=[pl.BlockSpec(memory_space=VMEM) for _ in outs],
        scratch_shapes=list(scratch),
        compiler_params=params,
        cost_estimate=cost,
    )


def shards(points, right_sides, skeleton, lengthscale, far_length, signal, noise_var):
    probes, rows = right_sides.shape
    levels, rank = skeleton.shape
    half = levels // 2
    count = lax.axis_size("loc")
    far_scale = 1.0 / (rank * rank * levels)
    beside = [(i, i ^ 1) for i in range(count)]
    across = [(i, i + 1) for i in range(1, count - 1, 2)]
    across = across + [(j, i) for i, j in across]

    def partner(value, slot):
        pairs = [(i, i ^ (2 << (2 * slot + i % 2))) for i in range(count)]
        return lax.ppermute(value, "loc", pairs)

    def sibling(value):
        return lax.ppermute(value, "loc", beside)

    def sides(value):
        return lax.ppermute(value, "loc", beside), lax.ppermute(value, "loc", across)

    height = -(-(24 + levels) // 8) * 8
    given = jnp.pad(right_sides, ((0, height - probes), (0, 0)))
    given += jnp.pad(points, ((16, height - 19), (0, 0)))
    given += jnp.pad(skeleton, ((24, height - 24 - levels), (0, rows - rank))).astype(FULL)
    msg, target, basis, skel_target, numbers, keep, give = call(
        functools.partial(front_kernel, levels),
        [
            ((MSG_ROWS, rows), HALF),
            ((SRC_ROWS, rows), HALF),
            ((levels * rank, rows), HALF),
            ((levels, SRC_ROWS, rank), HALF),
            ((8, 128), FULL),
            ((half, 96, rank), HALF),
            ((half, 96, rank), HALF),
        ],
        [SMEM, SMEM, VMEM],
        [
            VMEM((SRC_ROWS, rows), FULL),
            VMEM((2 * SRC_ROWS, rows), HALF),
            VMEM((levels * rank, SRC_ROWS), HALF),
        ],
    )(lengthscale, far_length, given)
    got = sibling(give)
    msg_a, msg_b = sides(msg)
    near_outs = [((rows, rows), HALF), ((32, rows), FULL), ((probes, rows), FULL)]
    turned_buf = [VMEM((rows, SRC_ROWS), HALF)]
    kept, image, slopes, *packs = call(
        own_kernel,
        near_outs + [((2, 96, rank), HALF)] * half,
        [VMEM] * 5,
        turned_buf,
    )(numbers, msg, target, keep, got)
    cross = [partner(pack, slot) for slot, pack in enumerate(packs)]
    kept_a, image, slopes = call(side_kernel, near_outs, [VMEM] * 5, turned_buf)(numbers, msg_a, target, image, slopes)
    kept_b, image, slopes = call(side_kernel, near_outs, [VMEM] * 5, turned_buf)(numbers, msg_b, target, image, slopes)
    image, cross = lax.optimization_barrier((image, cross))
    other = [sibling(value) for value in cross]
    couplings = [((half, rank, rank), HALF)] * 2
    image, own_high, own_low = call(
        functools.partial(carried_kernel, half, far_scale), [((32, rows), FULL)] + couplings, [VMEM] * (4 + half), micros=1.0
    )(numbers, image, basis, skel_target, *cross)
    other_high, other_low, row_sum, first, wmsg, keep, beside_msg = call(
        functools.partial(far_kernel, half, far_scale),
        couplings
        + [
            ((1, rows), FULL),
            ((probes, rows), FULL),
            ((2 * probes, rows), HALF),
            ((2 * probes, half * rank), HALF),
            ((2 * probes, rows + half * rank), HALF),
        ],
        [VMEM] * (5 + half),
    )(numbers, image, given, basis, skel_target, *other)
    wmsg_a = sibling(beside_msg)
    wmsg_b = lax.ppermute(wmsg, "loc", across)
    packs = call(pack_kernel, [((2, 2 * probes, rank), HALF)] * half, [VMEM] * 2, micros=0.1)(keep, wmsg_a)
    cross = [partner(pack, slot) for slot, pack in enumerate(packs)]
    (near,) = call(near_kernel, [((2 * probes, rows), FULL)], [VMEM] * 6, micros=1.2)(wmsg, wmsg_a, wmsg_b, kept, kept_a, kept_b)
    other = [sibling(value) for value in cross]
    sums, first_rest, second_rest, shift = call(
        functools.partial(second_kernel, half, far_scale),
        [((count, 128), FULL), ((probes, rows), FULL), ((probes, rows), FULL), ((probes, 128), FULL)],
        [VMEM] * (10 + levels),
    )(near, basis, own_high, own_low, other_high, other_low, row_sum, first, given, slopes, *cross, *other)
    sums, signal, noise_var = lax.optimization_barrier((sums, signal, noise_var))
    table = lax.all_to_all(sums, "loc", 0, 0, tiled=True)
    (slope_image,) = call(slope_kernel, [((probes, rows), FULL)], [SMEM, VMEM, VMEM])(signal, numbers, slopes)
    solution, residual, trace = call(
        functools.partial(last_kernel, float(rows * count)),
        [((probes, rows), FULL), ((probes, rows), FULL), ((1, probes), FULL)],
        [SMEM, SMEM] + [VMEM] * 6,
    )(signal, noise_var, numbers, table, shift, first_rest, second_rest, given)
    return (solution, residual, slope_image, trace.reshape(probes))


def solution(mesh):
    placed = (P(None, "loc"), P(None, "loc"), P(None, "loc"), P(), P(), P(), P())
    return jax.shard_map(
        shards,
        mesh=mesh,
        in_specs=placed,
        out_specs=(P(None, "loc"), P(None, "loc"), P(None, "loc"), P()),
        check_vma=False,
    )
```

```python
import functools

import jax
import jax.numpy as jnp
from jax import lax
from jax.experimental import pallas as pl
from jax.experimental.pallas import tpu as pltpu
from jax.sharding import PartitionSpec as P

HALF = jnp.bfloat16
FULL = jnp.float32
LOG2_E = 1.4426950408889634
ROOT_THREE = 1.7320508075688772
TINY = 1e-30
SCALE = 2.0**-10
SRC_ROWS = 32
MSG_ROWS = 64
VEC_ROWS = 48
TILE = 128
WIDE_TILE = 256
VMEM = pltpu.VMEM
SMEM = pltpu.SMEM


def split_two(value):
    high = value.astype(HALF)
    low = (value - high.astype(FULL)).astype(HALF)
    return high, low


def split_three(value):
    first = value.astype(HALF).astype(FULL)
    rest = value - first
    second = rest.astype(HALF).astype(FULL)
    third = (rest - second).astype(HALF).astype(FULL)
    return first, second, third


def matern(squared, rates):
    rate, falling_rate = rates
    squared = jnp.maximum(squared, TINY)
    radius = squared * lax.rsqrt(squared)
    decay = jnp.exp2(radius * falling_rate)
    falling = radius * decay
    return decay + rate * falling, radius * falling


def excess(pts):
    total = jnp.full((1, pts.shape[1]), -1.0, FULL)
    lost = jnp.zeros_like(total)
    small = jnp.zeros_like(total)
    for axis in range(3):
        value = pts[axis : axis + 1, :]
        head = value.astype(HALF).astype(FULL)
        tail = value - head
        small = small + tail * tail
        for term in (head * head, 2.0 * head * tail):
            grown = total + term
            back = grown - total
            lost = lost + ((total - (grown - back)) + (term - back))
            total = grown
    return total + (lost + small)


def write_rows(buf, base, pts, source):
    over = excess(pts)
    first = over.astype(HALF).astype(FULL)
    second = over - first
    unit = jnp.ones_like(over)
    if source:
        rows = (unit, unit, unit, first, second)
        order = (0, 0, 0, 1, 1, 1, 2, 2, 2)
        pieces = split_three(pts)
    else:
        rows = (unit + unit, first, second, unit, unit)
        order = (0, 1, 2, 0, 1, 2, 0, 1, 2)
        pieces = split_three(-2.0 * pts)
    for slot, row in enumerate(rows):
        buf[base + slot : base + slot + 1, :] = row
    for slot, index in enumerate(order):
        start = base + 5 + 3 * slot
        buf[start : start + 3, :] = pieces[index]


def dot(a, b):
    return jnp.dot(a, b, preferred_element_type=FULL)


def dot_rows(a, b):
    return lax.dot_general(a, b, (((1,), (1,)), ((), ())), preferred_element_type=FULL)


def turned(value):
    return value.astype(FULL).T.astype(HALF)


def merged(both):
    return jnp.concatenate([both[0:16] + both[16:32], both[32:48]], axis=0)


def on_first_core():
    return lax.rem(lax.axis_index("loc"), 2) == 0


def gather_share(keep, got, packs):
    first = on_first_core()
    for slot, pack in enumerate(packs):
        pack[0] = jnp.where(first, keep[slot], got[slot])
        pack[1] = jnp.where(first, got[slot], keep[slot])


def own_part(values):
    first = on_first_core()
    return [jnp.where(first, value[0], value[1]) for value in values]


def front_kernel(levels, *refs):
    length, far_length, given = refs[:3]
    msg, target, basis, skel_target, numbers, keep, beside = refs[3:10]
    buf, pair_buf, turned_src = refs[10:]
    points = given[16:19, :]
    for slot, value in enumerate((length[0], far_length[0])):
        lengths = jnp.full((1, 128), value, FULL)
        numbers[slot : slot + 1, :] = ROOT_THREE / lengths
        numbers[slot + 2 : slot + 3, :] = (-LOG2_E * ROOT_THREE) / lengths
    write_rows(buf, 0, points, False)
    target[...] = buf[...].astype(HALF)
    pair_buf[SRC_ROWS:, :] = buf[...].astype(HALF)
    write_rows(buf, 0, points, True)
    pair_buf[0:SRC_ROWS, :] = buf[...].astype(HALF)
    msg[32:64, :] = buf[...].astype(HALF)
    rows, rank = points.shape[1], skel_target.shape[2]
    first = on_first_core()
    skel = [given[24 + level : 25 + level, 0:rank] for level in range(levels)]
    order = [jnp.where(first, skel[level], skel[level + 1]) for level in range(0, levels, 2)]
    order += [jnp.where(first, skel[level + 1], skel[level]) for level in range(0, levels, 2)]
    spot = lax.broadcasted_iota(jnp.int32, (rows, rank), 0).astype(FULL)
    sources = []
    for level in range(levels):
        picks = jnp.where(spot == order[level], 1.0, 0.0).astype(HALF)
        both = dot(pair_buf[...], picks)
        skel_target[level] = both[SRC_ROWS:].astype(HALF)
        skel_source = both[:SRC_ROWS]
        sources.append(skel_source.astype(HALF))
        turned_src[level * rank : (level + 1) * rank, :] = skel_source.T.astype(HALF)
    rates = [jnp.concatenate([numbers[row : row + 1, :]] * (WIDE_TILE // 128), axis=1) for row in (1, 3)]
    for row in range(0, levels * rank, 1024):
        for col in range(0, rows, WIDE_TILE):
            squared = dot(turned_src[row : row + 1024, :], target[:, col : col + WIDE_TILE])
            basis[row : row + 1024, col : col + WIDE_TILE] = matern(squared, rates)[0].astype(HALF)
    high, low = split_two(given[0:16, :])
    msg[0:16, :] = low
    msg[16:32, :] = high
    coef = merged(dot_rows(msg[0:VEC_ROWS, :], basis[...]))
    for level in range(levels):
        high, low = split_two(coef[:, level * rank : (level + 1) * rank])
        if level < levels // 2:
            keep[level, 0:32, :] = high
            keep[level, 32:64, :] = low
            keep[level, 64:96, :] = sources[level]
        else:
            start = rows + (level - levels // 2) * 2 * rank
            beside[0:32, start : start + rank] = high
            beside[32:64, start : start + rank] = low
            beside[0:32, start + rank : start + 2 * rank] = sources[level]
            beside[32:64, start + rank : start + 2 * rank] = sources[level]
    beside[:, 0:rows] = msg[...]


def near_block(msg, target, turned_src, rates, kept):
    rows = target.shape[1]
    turned_src[...] = turned(msg[32:64, 0:rows])
    for col in range(0, rows, TILE):
        squared = dot(turned_src[...], target[:, col : col + TILE])
        value, slope = matern(squared, rates)
        value = value.astype(HALF)
        kept[:, col : col + TILE] = value
        pair = jnp.concatenate([value, slope.astype(HALF)], axis=1)
        total = dot(msg[0:VEC_ROWS, 0:rows], pair)
        yield slice(col, col + TILE), merged(total[:, :TILE]), total[16:32, TILE:]


def own_kernel(numbers, msg, target, keep, got, kept, image, slopes, *rest):
    packs, turned_src = rest[:-1], rest[-1]
    rows, rank = target.shape[1], keep.shape[2]
    starts = [rows + 2 * rank * slot for slot in range(len(packs))]
    parts = [(got[:, start : start + rank], got[0:32, start + rank : start + 2 * rank]) for start in starts]
    gather_share(keep, [jnp.concatenate(part, axis=0) for part in parts], packs)
    rates = numbers[0:1, :], numbers[2:3, :]
    for span, part, slope in near_block(msg, target, turned_src, rates, kept):
        image[:, span] = part
        slopes[:, span] = slope


def side_kernel(numbers, msg, target, image_in, slopes_in, kept, image, slopes, turned_src):
    rates = numbers[0:1, :], numbers[2:3, :]
    for span, part, slope in near_block(msg, target, turned_src, rates, kept):
        image[:, span] = image_in[:, span] + part
        slopes[:, span] = slopes_in[:, span] + slope


def far_part(lev, start, numbers, skel_target, basis, coup_high, coup_low):
    rank = skel_target.shape[2]
    rates = [jnp.concatenate([numbers[row : row + 1, :]] * (rank // 128), axis=1) for row in (1, 3)]
    mixed = []
    for slot, value in enumerate(lev):
        squared = dot(turned(value[64:96]), skel_target[start + slot])
        high, low = split_two(matern(squared, rates)[0])
        coup_high[slot] = high
        coup_low[slot] = low
        both = dot(value[0:64], high)
        part = both[0:32] + both[32:64] + dot(value[0:32], low)
        mixed.append(jnp.concatenate(split_two(part), axis=0))
    far = dot(jnp.concatenate(mixed, axis=1), basis[start * rank : (start + len(lev)) * rank, :])
    return far[0:32] + far[32:64]


def carried_kernel(half, far_scale, *refs):
    numbers, image_in, basis, skel_target = refs[:4]
    lev = own_part(refs[4 : 4 + half])
    image, coup_high, coup_low = refs[4 + half :]
    image[...] = image_in[...] + far_scale * far_part(lev, 0, numbers, skel_target, basis, coup_high, coup_low)


def far_kernel(half, far_scale, *refs):
    numbers, image, given, basis, skel_target = refs[:5]
    lev = own_part(refs[5 : 5 + half])
    coup_high, coup_low, row_sum, first, wmsg, keep, beside = refs[5 + half :]
    rank = skel_target.shape[2]
    total = image[...] + far_scale * far_part(lev, half, numbers, skel_target, basis, coup_high, coup_low)
    sums = total[16:17, :]
    row_sum[...] = sums
    value = SCALE * (total[0:16] + sums * given[0:16, :])
    first[...] = value
    high, low = split_two(value)
    rows = wmsg.shape[1]
    wmsg[0:16, :] = high
    wmsg[16:32, :] = low
    beside[0:16, 0:rows] = high
    beside[16:32, 0:rows] = low
    both = dot_rows(wmsg[...], basis[...])
    high, low = split_two(both[0:16] + both[16:32])
    keep[0:16, :] = high[:, : half * rank]
    keep[16:32, :] = low[:, : half * rank]
    beside[0:16, rows:] = high[:, half * rank :]
    beside[16:32, rows:] = low[:, half * rank :]


def pack_kernel(keep, got, *packs):
    rank = packs[0].shape[2]
    start = got.shape[1] - keep.shape[1]
    spans = [slice(slot * rank, (slot + 1) * rank) for slot in range(len(packs))]
    there = [slice(start + span.start, start + span.stop) for span in spans]
    gather_share([keep[:, span] for span in spans], [got[:, span] for span in there], packs)


def near_kernel(wmsg, wmsg_a, wmsg_b, kept, kept_a, kept_b, out):
    rows = kept_a.shape[0]
    out[...] = dot(wmsg[...], kept[...]) + dot(wmsg_a[:, 0:rows], kept_a[...]) + dot(wmsg_b[...], kept_b[...])


def row_total(a, b):
    return jnp.sum(a * b, axis=1, keepdims=True)


def second_kernel(half, far_scale, *refs):
    near, basis, own_high, own_low, other_high, other_low, row_sum, first, given, slope_sum = refs[:10]
    wlev = own_part(refs[10 : 10 + 2 * half])
    sums, first_rest, second_rest, shift_out = refs[10 + 2 * half :]
    coup_high = [own_high[slot] for slot in range(half)] + [other_high[slot] for slot in range(half)]
    coup_low = [own_low[slot] for slot in range(half)] + [other_low[slot] for slot in range(half)]
    pieces = []
    for coef, high, low in zip(wlev, coup_high, coup_low):
        mixed = dot(coef, high)
        mixed = mixed[0:16] + mixed[16:32] + dot(coef[0:16], low)
        pieces.append(jnp.concatenate(split_two(mixed), axis=0))
    both = near[...] + far_scale * dot(jnp.concatenate(pieces, axis=1), basis[...])
    base = given[0:16, :]
    value = first[...]
    image = SCALE * (both[0:16] + both[16:32] + row_sum[...] * value)
    weight = row_total(base, base)
    shift = jnp.where(weight > 0.0, row_total(base, value) / jnp.where(weight > 0.0, weight, 1.0), 0.0)
    value = value - shift * base
    image = image - (2.0 * shift) * value - (shift * shift) * base
    first_rest[...] = value
    second_rest[...] = image
    shift_out[...] = jnp.broadcast_to(shift, shift_out.shape)
    slope = slope_sum[...]
    parts = (
        shift,
        weight,
        row_total(value, value),
        row_total(value, image),
        row_total(base, image),
        row_total(base, value),
        row_total(base, slope),
        row_total(value, slope),
    )
    lane = lax.broadcasted_iota(jnp.int32, (16, 128), 1)
    row = lax.broadcasted_iota(jnp.int32, (16, 128), 0)
    packed = jnp.zeros((16, 128), FULL)
    for slot, part in enumerate(parts):
        packed = jnp.where(lane == row + 16 * slot, part, packed)
    sums[...] = jnp.broadcast_to(jnp.sum(packed, axis=0, keepdims=True), sums.shape)


def last_kernel(point_total, signal, noise, numbers, table, shift_in, first_rest, second_rest, given, out, res, trace):
    gathered = table[...]
    shift = gathered

    def slot(index):
        return pltpu.roll(gathered, 128 - 16 * index, 1)

    weight, ww, wz, rz, rw, rs, ws = (slot(index) for index in range(1, 8))

    def total(value):
        return jnp.sum(value, axis=0, keepdims=True)

    gain = signal[0] / SCALE
    rate = numbers[0:1, :]
    norm = total(weight)
    center = total(shift * weight + rw) / norm
    off = shift - center
    cross = total(rw + off * weight)
    square = total(ww + 2.0 * off * rw + off * off * weight)
    mixed = total(rz + 2.0 * off * rw + off * off * weight)
    second = total(
        wz + 2.0 * off * ww + off * off * rw + off * rz + 2.0 * off * off * rw + off * off * off * weight
    )
    held = total(rs)
    along = total(ws + off * rs)
    cross = gain * cross
    square = (gain * gain) * square
    mixed = (gain * gain) * mixed
    second = (gain * gain) * gain * second
    level = noise[0] + gain * center
    lead = level * norm + cross
    alpha = norm / lead
    part = cross / lead
    norm_next = part * part * norm - 2.0 * part * alpha * cross + alpha * alpha * square
    lean = part + norm_next / norm
    direction = lean * lean * norm - 2.0 * lean * alpha * cross + alpha * alpha * square
    bend = lean * lean * cross - lean * alpha * (mixed + square) + alpha * alpha * second
    beta = norm_next / (level * direction + bend)
    factor = signal[0] * (rate * rate)
    trace[...] = (((alpha + beta * lean) * held - beta * alpha * gain * along) * factor / point_total)[:, 0:16]

    lane = lax.broadcasted_iota(jnp.int32, (16, 128), 1)
    row = lax.broadcasted_iota(jnp.int32, (16, 128), 0)

    def column(value):
        return jnp.sum(jnp.where(lane == row, value, 0.0), axis=1, keepdims=True)

    own_off = shift_in[:, 0:1] - column(center)
    base = given[0:16, :]
    rest = first_rest[...]
    value = rest + own_off * base
    image = second_rest[...] + (2.0 * own_off) * rest + (own_off * own_off) * base
    out[...] = column(alpha + beta * lean) * base - column(beta * alpha * gain) * value
    res[...] = (
        column(part - beta * level * lean) * base
        - column((alpha - beta * level * alpha + beta * lean) * gain) * value
        + column(beta * alpha * gain * gain) * image
    )


def slope_kernel(signal, numbers, source, dest):
    rate = numbers[0:1, 0:1]
    dest[...] = (signal[0] * rate * rate) * source[...]


def call(kernel, outs, spaces, scratch=(), micros=2.0):
    params = pltpu.CompilerParams(vmem_limit_bytes=40 * 2**20)
    cost = pl.CostEstimate(flops=int(micros * 1e9), bytes_accessed=2**16, transcendentals=0)
    return pl.pallas_call(
        kernel,
        out_shape=[jax.ShapeDtypeStruct(shape, kind) for shape, kind in outs],
        in_specs=[pl.BlockSpec(memory_space=space) for space in spaces],
        out_specs=[pl.BlockSpec(memory_space=VMEM) for _ in outs],
        scratch_shapes=list(scratch),
        compiler_params=params,
        cost_estimate=cost,
    )


def shards(points, right_sides, skeleton, lengthscale, far_length, signal, noise_var):
    probes, rows = right_sides.shape
    levels, rank = skeleton.shape
    half = levels // 2
    count = lax.axis_size("loc")
    far_scale = 1.0 / (rank * rank * levels)
    beside = [(i, i ^ 1) for i in range(count)]
    across = [(i, i + 1) for i in range(1, count - 1, 2)]
    across = across + [(j, i) for i, j in across]

    def partner(value, slot):
        pairs = [(i, i ^ (2 << (2 * slot + i % 2))) for i in range(count)]
        return lax.ppermute(value, "loc", pairs)

    def sibling(value):
        return lax.ppermute(value, "loc", beside)

    height = -(-(24 + levels) // 8) * 8
    given = jnp.pad(right_sides, ((0, height - probes), (0, 0)))
    given += jnp.pad(points, ((16, height - 19), (0, 0)))
    given += jnp.pad(skeleton, ((24, height - 24 - levels), (0, rows - rank))).astype(FULL)
    msg, target, basis, skel_target, numbers, keep, beside_msg = call(
        functools.partial(front_kernel, levels),
        [
            ((MSG_ROWS, rows), HALF),
            ((SRC_ROWS, rows), HALF),
            ((levels * rank, rows), HALF),
            ((levels, SRC_ROWS, rank), HALF),
            ((8, 128), FULL),
            ((half, 96, rank), HALF),
            ((MSG_ROWS, rows + 2 * half * rank), HALF),
        ],
        [SMEM, SMEM, VMEM],
        [
            VMEM((SRC_ROWS, rows), FULL),
            VMEM((2 * SRC_ROWS, rows), HALF),
            VMEM((levels * rank, SRC_ROWS), HALF),
        ],
    )(lengthscale, far_length, given)
    msg_a = sibling(beside_msg)
    msg_b = lax.ppermute(msg, "loc", across)
    near_outs = [((rows, rows), HALF), ((32, rows), FULL), ((probes, rows), FULL)]
    turned_buf = [VMEM((rows, SRC_ROWS), HALF)]
    kept, image, slopes, *packs = call(
        own_kernel,
        near_outs + [((2, 96, rank), HALF)] * half,
        [VMEM] * 5,
        turned_buf,
    )(numbers, msg, target, keep, msg_a)
    cross = [partner(pack, slot) for slot, pack in enumerate(packs)]
    kept_a, image, slopes = call(side_kernel, near_outs, [VMEM] * 5, turned_buf)(numbers, msg_a, target, image, slopes)
    kept_b, image, slopes = call(side_kernel, near_outs, [VMEM] * 5, turned_buf)(numbers, msg_b, target, image, slopes)
    image, cross = lax.optimization_barrier((image, cross))
    other = [sibling(value) for value in cross]
    couplings = [((half, rank, rank), HALF)] * 2
    image, own_high, own_low = call(
        functools.partial(carried_kernel, half, far_scale), [((32, rows), FULL)] + couplings, [VMEM] * (4 + half), micros=1.0
    )(numbers, image, basis, skel_target, *cross)
    other_high, other_low, row_sum, first, wmsg, keep, beside_msg = call(
        functools.partial(far_kernel, half, far_scale),
        couplings
        + [
            ((1, rows), FULL),
            ((probes, rows), FULL),
            ((2 * probes, rows), HALF),
            ((2 * probes, half * rank), HALF),
            ((2 * probes, rows + half * rank), HALF),
        ],
        [VMEM] * (5 + half),
    )(numbers, image, given, basis, skel_target, *other)
    wmsg_a = sibling(beside_msg)
    wmsg_b = lax.ppermute(wmsg, "loc", across)
    packs = call(pack_kernel, [((2, 2 * probes, rank), HALF)] * half, [VMEM] * 2, micros=0.1)(keep, wmsg_a)
    cross = [partner(pack, slot) for slot, pack in enumerate(packs)]
    (near,) = call(near_kernel, [((2 * probes, rows), FULL)], [VMEM] * 6, micros=1.2)(wmsg, wmsg_a, wmsg_b, kept, kept_a, kept_b)
    other = [sibling(value) for value in cross]
    sums, first_rest, second_rest, shift = call(
        functools.partial(second_kernel, half, far_scale),
        [((count, 128), FULL), ((probes, rows), FULL), ((probes, rows), FULL), ((probes, 128), FULL)],
        [VMEM] * (10 + levels),
    )(near, basis, own_high, own_low, other_high, other_low, row_sum, first, given, slopes, *cross, *other)
    sums, signal, noise_var = lax.optimization_barrier((sums, signal, noise_var))
    table = lax.all_to_all(sums, "loc", 0, 0, tiled=True)
    (slope_image,) = call(slope_kernel, [((probes, rows), FULL)], [SMEM, VMEM, VMEM])(signal, numbers, slopes)
    solution, residual, trace = call(
        functools.partial(last_kernel, float(rows * count)),
        [((probes, rows), FULL), ((probes, rows), FULL), ((1, probes), FULL)],
        [SMEM, SMEM] + [VMEM] * 6,
    )(signal, noise_var, numbers, table, shift, first_rest, second_rest, given)
    return (solution, residual, slope_image, trace.reshape(probes))


def solution(mesh):
    placed = (P(None, "loc"), P(None, "loc"), P(None, "loc"), P(), P(), P(), P())
    return jax.shard_map(
        shards,
        mesh=mesh,
        in_specs=placed,
        out_specs=(P(None, "loc"), P(None, "loc"), P(None, "loc"), P()),
        check_vma=False,
    )
```

```python
import functools

import jax
import jax.numpy as jnp
from jax import lax
from jax.experimental import pallas as pl
from jax.experimental.pallas import tpu as pltpu
from jax.sharding import PartitionSpec as P

HALF = jnp.bfloat16
FULL = jnp.float32
LOG2_E = 1.4426950408889634
ROOT_THREE = 1.7320508075688772
TINY = 1e-30
SCALE = 2.0**-10
SRC_ROWS = 32
MSG_ROWS = 64
VEC_ROWS = 48
TILE = 128
WIDE_TILE = 256
VMEM = pltpu.VMEM
SMEM = pltpu.SMEM


def split_two(value):
    high = value.astype(HALF)
    low = (value - high.astype(FULL)).astype(HALF)
    return high, low


def split_three(value):
    first = value.astype(HALF).astype(FULL)
    rest = value - first
    second = rest.astype(HALF).astype(FULL)
    third = (rest - second).astype(HALF).astype(FULL)
    return first, second, third


def matern(squared, rates):
    rate, falling_rate = rates
    squared = jnp.maximum(squared, TINY)
    radius = squared * lax.rsqrt(squared)
    decay = jnp.exp2(radius * falling_rate)
    falling = radius * decay
    return decay + rate * falling, radius * falling


def excess(pts):
    total = jnp.full((1, pts.shape[1]), -1.0, FULL)
    lost = jnp.zeros_like(total)
    small = jnp.zeros_like(total)
    for axis in range(3):
        value = pts[axis : axis + 1, :]
        head = value.astype(HALF).astype(FULL)
        tail = value - head
        small = small + tail * tail
        for term in (head * head, 2.0 * head * tail):
            grown = total + term
            back = grown - total
            lost = lost + ((total - (grown - back)) + (term - back))
            total = grown
    return total + (lost + small)


def write_rows(buf, base, pts, source):
    over = excess(pts)
    first = over.astype(HALF).astype(FULL)
    second = over - first
    unit = jnp.ones_like(over)
    if source:
        rows = (unit, unit, unit, first, second)
        order = (0, 0, 0, 1, 1, 1, 2, 2, 2)
        pieces = split_three(pts)
    else:
        rows = (unit + unit, first, second, unit, unit)
        order = (0, 1, 2, 0, 1, 2, 0, 1, 2)
        pieces = split_three(-2.0 * pts)
    for slot, row in enumerate(rows):
        buf[base + slot : base + slot + 1, :] = row
    for slot, index in enumerate(order):
        start = base + 5 + 3 * slot
        buf[start : start + 3, :] = pieces[index]


def dot(a, b):
    return jnp.dot(a, b, preferred_element_type=FULL)


def dot_rows(a, b):
    return lax.dot_general(a, b, (((1,), (1,)), ((), ())), preferred_element_type=FULL)


def turned(value):
    return value.astype(FULL).T.astype(HALF)


def merged(both):
    return jnp.concatenate([both[0:16] + both[16:32], both[32:48]], axis=0)


def on_first_core():
    return lax.rem(lax.axis_index("loc"), 2) == 0


def gather_share(keep, got, packs):
    first = on_first_core()
    for slot, pack in enumerate(packs):
        pack[0] = jnp.where(first, keep[slot], got[slot])
        pack[1] = jnp.where(first, got[slot], keep[slot])


def own_part(values):
    first = on_first_core()
    return [jnp.where(first, value[0], value[1]) for value in values]


def front_kernel(levels, *refs):
    length, far_length, given = refs[:3]
    msg, target, basis, skel_target, numbers, keep, beside = refs[3:10]
    buf, pair_buf, turned_src = refs[10:]
    points = given[16:19, :]
    for slot, value in enumerate((length[0], far_length[0])):
        lengths = jnp.full((1, 128), value, FULL)
        numbers[slot : slot + 1, :] = ROOT_THREE / lengths
        numbers[slot + 2 : slot + 3, :] = (-LOG2_E * ROOT_THREE) / lengths
    write_rows(buf, 0, points, False)
    target[...] = buf[...].astype(HALF)
    pair_buf[SRC_ROWS:, :] = buf[...].astype(HALF)
    write_rows(buf, 0, points, True)
    pair_buf[0:SRC_ROWS, :] = buf[...].astype(HALF)
    msg[32:64, :] = buf[...].astype(HALF)
    rows, rank = points.shape[1], skel_target.shape[2]
    first = on_first_core()
    skel = [given[24 + level : 25 + level, 0:rank] for level in range(levels)]
    order = [jnp.where(first, skel[level], skel[level + 1]) for level in range(0, levels, 2)]
    order += [jnp.where(first, skel[level + 1], skel[level]) for level in range(0, levels, 2)]
    spot = lax.broadcasted_iota(jnp.int32, (rows, rank), 0).astype(FULL)
    sources = []
    for level in range(levels):
        picks = jnp.where(spot == order[level], 1.0, 0.0).astype(HALF)
        both = dot(pair_buf[...], picks)
        skel_target[level] = both[SRC_ROWS:].astype(HALF)
        skel_source = both[:SRC_ROWS]
        sources.append(skel_source.astype(HALF))
        turned_src[level * rank : (level + 1) * rank, :] = skel_source.T.astype(HALF)
    rates = [jnp.concatenate([numbers[row : row + 1, :]] * (WIDE_TILE // 128), axis=1) for row in (1, 3)]
    for row in range(0, levels * rank, 1024):
        for col in range(0, rows, WIDE_TILE):
            squared = dot(turned_src[row : row + 1024, :], target[:, col : col + WIDE_TILE])
            basis[row : row + 1024, col : col + WIDE_TILE] = matern(squared, rates)[0].astype(HALF)
    high, low = split_two(given[0:16, :])
    msg[0:16, :] = low
    msg[16:32, :] = high
    coef = merged(dot_rows(msg[0:VEC_ROWS, :], basis[...]))
    for level in range(levels):
        high, low = split_two(coef[:, level * rank : (level + 1) * rank])
        if level < levels // 2:
            keep[level, 0:32, :] = high
            keep[level, 32:64, :] = low
            keep[level, 64:96, :] = sources[level]
        else:
            start = rows + (level - levels // 2) * 2 * rank
            beside[0:32, start : start + rank] = high
            beside[32:64, start : start + rank] = low
            beside[0:32, start + rank : start + 2 * rank] = sources[level]
            beside[32:64, start + rank : start + 2 * rank] = sources[level]
    beside[:, 0:rows] = msg[...]


def near_block(msg, target, turned_src, rates, kept):
    rows = target.shape[1]
    turned_src[...] = turned(msg[32:64, 0:rows])
    for col in range(0, rows, TILE):
        squared = dot(turned_src[...], target[:, col : col + TILE])
        value, slope = matern(squared, rates)
        value = value.astype(HALF)
        kept[:, col : col + TILE] = value
        pair = jnp.concatenate([value, slope.astype(HALF)], axis=1)
        total = dot(msg[0:VEC_ROWS, 0:rows], pair)
        yield slice(col, col + TILE), merged(total[:, :TILE]), total[16:32, TILE:]


def first_pack_kernel(keep, got, *packs):
    rank = keep.shape[2]
    rows = got.shape[1] - 2 * rank * len(packs)
    starts = [rows + 2 * rank * slot for slot in range(len(packs))]
    parts = [(got[:, start : start + rank], got[0:32, start + rank : start + 2 * rank]) for start in starts]
    gather_share(keep, [jnp.concatenate(part, axis=0) for part in parts], packs)


def own_kernel(numbers, msg, target, kept, image, slopes, turned_src):
    rates = numbers[0:1, :], numbers[2:3, :]
    for span, part, slope in near_block(msg, target, turned_src, rates, kept):
        image[:, span] = part
        slopes[:, span] = slope


def side_kernel(numbers, msg, target, image_in, slopes_in, kept, image, slopes, turned_src):
    rates = numbers[0:1, :], numbers[2:3, :]
    for span, part, slope in near_block(msg, target, turned_src, rates, kept):
        image[:, span] = image_in[:, span] + part
        slopes[:, span] = slopes_in[:, span] + slope


def far_part(lev, start, numbers, skel_target, basis, coup_high, coup_low):
    rank = skel_target.shape[2]
    rates = [jnp.concatenate([numbers[row : row + 1, :]] * (rank // 128), axis=1) for row in (1, 3)]
    mixed = []
    for slot, value in enumerate(lev):
        squared = dot(turned(value[64:96]), skel_target[start + slot])
        high, low = split_two(matern(squared, rates)[0])
        coup_high[slot] = high
        coup_low[slot] = low
        both = dot(value[0:64], high)
        part = both[0:32] + both[32:64] + dot(value[0:32], low)
        mixed.append(jnp.concatenate(split_two(part), axis=0))
    far = dot(jnp.concatenate(mixed, axis=1), basis[start * rank : (start + len(lev)) * rank, :])
    return far[0:32] + far[32:64]


def carried_kernel(half, far_scale, *refs):
    numbers, image_in, basis, skel_target = refs[:4]
    lev = own_part(refs[4 : 4 + half])
    image, coup_high, coup_low = refs[4 + half :]
    image[...] = image_in[...] + far_scale * far_part(lev, 0, numbers, skel_target, basis, coup_high, coup_low)


def far_kernel(half, far_scale, *refs):
    numbers, image, given, basis, skel_target = refs[:5]
    lev = own_part(refs[5 : 5 + half])
    coup_high, coup_low, row_sum, first, wmsg, keep, beside = refs[5 + half :]
    rank = skel_target.shape[2]
    total = image[...] + far_scale * far_part(lev, half, numbers, skel_target, basis, coup_high, coup_low)
    sums = total[16:17, :]
    row_sum[...] = sums
    value = SCALE * (total[0:16] + sums * given[0:16, :])
    first[...] = value
    high, low = split_two(value)
    rows = wmsg.shape[1]
    wmsg[0:16, :] = high
    wmsg[16:32, :] = low
    beside[0:16, 0:rows] = high
    beside[16:32, 0:rows] = low
    both = dot_rows(wmsg[...], basis[...])
    high, low = split_two(both[0:16] + both[16:32])
    keep[0:16, :] = high[:, : half * rank]
    keep[16:32, :] = low[:, : half * rank]
    beside[0:16, rows:] = high[:, half * rank :]
    beside[16:32, rows:] = low[:, half * rank :]


def pack_kernel(keep, got, *packs):
    rank = packs[0].shape[2]
    start = got.shape[1] - keep.shape[1]
    spans = [slice(slot * rank, (slot + 1) * rank) for slot in range(len(packs))]
    there = [slice(start + span.start, start + span.stop) for span in spans]
    gather_share([keep[:, span] for span in spans], [got[:, span] for span in there], packs)


def near_kernel(wmsg, wmsg_a, wmsg_b, kept, kept_a, kept_b, out):
    rows = kept_a.shape[0]
    out[...] = dot(wmsg[...], kept[...]) + dot(wmsg_a[:, 0:rows], kept_a[...]) + dot(wmsg_b[...], kept_b[...])


def row_total(a, b):
    return jnp.sum(a * b, axis=1, keepdims=True)


def second_kernel(half, far_scale, *refs):
    near, basis, own_high, own_low, other_high, other_low, row_sum, first, given, slope_sum = refs[:10]
    wlev = own_part(refs[10 : 10 + 2 * half])
    sums, first_rest, second_rest, shift_out = refs[10 + 2 * half :]
    coup_high = [own_high[slot] for slot in range(half)] + [other_high[slot] for slot in range(half)]
    coup_low = [own_low[slot] for slot in range(half)] + [other_low[slot] for slot in range(half)]
    pieces = []
    for coef, high, low in zip(wlev, coup_high, coup_low):
        mixed = dot(coef, high)
        mixed = mixed[0:16] + mixed[16:32] + dot(coef[0:16], low)
        pieces.append(jnp.concatenate(split_two(mixed), axis=0))
    both = near[...] + far_scale * dot(jnp.concatenate(pieces, axis=1), basis[...])
    base = given[0:16, :]
    value = first[...]
    image = SCALE * (both[0:16] + both[16:32] + row_sum[...] * value)
    weight = row_total(base, base)
    shift = jnp.where(weight > 0.0, row_total(base, value) / jnp.where(weight > 0.0, weight, 1.0), 0.0)
    value = value - shift * base
    image = image - (2.0 * shift) * value - (shift * shift) * base
    first_rest[...] = value
    second_rest[...] = image
    shift_out[...] = jnp.broadcast_to(shift, shift_out.shape)
    slope = slope_sum[...]
    parts = (
        shift,
        weight,
        row_total(value, value),
        row_total(value, image),
        row_total(base, image),
        row_total(base, value),
        row_total(base, slope),
        row_total(value, slope),
    )
    lane = lax.broadcasted_iota(jnp.int32, (16, 128), 1)
    row = lax.broadcasted_iota(jnp.int32, (16, 128), 0)
    packed = jnp.zeros((16, 128), FULL)
    for slot, part in enumerate(parts):
        packed = jnp.where(lane == row + 16 * slot, part, packed)
    sums[...] = jnp.broadcast_to(jnp.sum(packed, axis=0, keepdims=True), sums.shape)


def last_kernel(point_total, signal, noise, numbers, table, shift_in, first_rest, second_rest, given, out, res, trace):
    gathered = table[...]
    shift = gathered

    def slot(index):
        return pltpu.roll(gathered, 128 - 16 * index, 1)

    weight, ww, wz, rz, rw, rs, ws = (slot(index) for index in range(1, 8))

    def total(value):
        return jnp.sum(value, axis=0, keepdims=True)

    gain = signal[0] / SCALE
    rate = numbers[0:1, :]
    norm = total(weight)
    center = total(shift * weight + rw) / norm
    off = shift - center
    cross = total(rw + off * weight)
    square = total(ww + 2.0 * off * rw + off * off * weight)
    mixed = total(rz + 2.0 * off * rw + off * off * weight)
    second = total(
        wz + 2.0 * off * ww + off * off * rw + off * rz + 2.0 * off * off * rw + off * off * off * weight
    )
    held = total(rs)
    along = total(ws + off * rs)
    cross = gain * cross
    square = (gain * gain) * square
    mixed = (gain * gain) * mixed
    second = (gain * gain) * gain * second
    level = noise[0] + gain * center
    lead = level * norm + cross
    alpha = norm / lead
    part = cross / lead
    norm_next = part * part * norm - 2.0 * part * alpha * cross + alpha * alpha * square
    lean = part + norm_next / norm
    direction = lean * lean * norm - 2.0 * lean * alpha * cross + alpha * alpha * square
    bend = lean * lean * cross - lean * alpha * (mixed + square) + alpha * alpha * second
    beta = norm_next / (level * direction + bend)
    factor = signal[0] * (rate * rate)
    trace[...] = (((alpha + beta * lean) * held - beta * alpha * gain * along) * factor / point_total)[:, 0:16]

    lane = lax.broadcasted_iota(jnp.int32, (16, 128), 1)
    row = lax.broadcasted_iota(jnp.int32, (16, 128), 0)

    def column(value):
        return jnp.sum(jnp.where(lane == row, value, 0.0), axis=1, keepdims=True)

    own_off = shift_in[:, 0:1] - column(center)
    base = given[0:16, :]
    rest = first_rest[...]
    value = rest + own_off * base
    image = second_rest[...] + (2.0 * own_off) * rest + (own_off * own_off) * base
    out[...] = column(alpha + beta * lean) * base - column(beta * alpha * gain) * value
    res[...] = (
        column(part - beta * level * lean) * base
        - column((alpha - beta * level * alpha + beta * lean) * gain) * value
        + column(beta * alpha * gain * gain) * image
    )


def slope_kernel(signal, numbers, source, dest):
    rate = numbers[0:1, 0:1]
    dest[...] = (signal[0] * rate * rate) * source[...]


def call(kernel, outs, spaces, scratch=(), micros=2.0):
    params = pltpu.CompilerParams(vmem_limit_bytes=40 * 2**20)
    cost = pl.CostEstimate(flops=int(micros * 1e9), bytes_accessed=2**16, transcendentals=0)
    return pl.pallas_call(
        kernel,
        out_shape=[jax.ShapeDtypeStruct(shape, kind) for shape, kind in outs],
        in_specs=[pl.BlockSpec(memory_space=space) for space in spaces],
        out_specs=[pl.BlockSpec(memory_space=VMEM) for _ in outs],
        scratch_shapes=list(scratch),
        compiler_params=params,
        cost_estimate=cost,
    )


def shards(points, right_sides, skeleton, lengthscale, far_length, signal, noise_var):
    probes, rows = right_sides.shape
    levels, rank = skeleton.shape
    half = levels // 2
    count = lax.axis_size("loc")
    far_scale = 1.0 / (rank * rank * levels)
    beside = [(i, i ^ 1) for i in range(count)]
    across = [(i, i + 1) for i in range(1, count - 1, 2)]
    across = across + [(j, i) for i, j in across]

    def partner(value, slot):
        pairs = [(i, i ^ (2 << (2 * slot + i % 2))) for i in range(count)]
        return lax.ppermute(value, "loc", pairs)

    def sibling(value):
        return lax.ppermute(value, "loc", beside)

    height = -(-(24 + levels) // 8) * 8
    given = jnp.pad(right_sides, ((0, height - probes), (0, 0)))
    given += jnp.pad(points, ((16, height - 19), (0, 0)))
    given += jnp.pad(skeleton, ((24, height - 24 - levels), (0, rows - rank))).astype(FULL)
    msg, target, basis, skel_target, numbers, keep, beside_msg = call(
        functools.partial(front_kernel, levels),
        [
            ((MSG_ROWS, rows), HALF),
            ((SRC_ROWS, rows), HALF),
            ((levels * rank, rows), HALF),
            ((levels, SRC_ROWS, rank), HALF),
            ((8, 128), FULL),
            ((half, 96, rank), HALF),
            ((MSG_ROWS, rows + 2 * half * rank), HALF),
        ],
        [SMEM, SMEM, VMEM],
        [
            VMEM((SRC_ROWS, rows), FULL),
            VMEM((2 * SRC_ROWS, rows), HALF),
            VMEM((levels * rank, SRC_ROWS), HALF),
        ],
    )(lengthscale, far_length, given)
    msg_a = sibling(beside_msg)
    msg_b = lax.ppermute(msg, "loc", across)
    near_outs = [((rows, rows), HALF), ((32, rows), FULL), ((probes, rows), FULL)]
    turned_buf = [VMEM((rows, SRC_ROWS), HALF)]
    packs = call(first_pack_kernel, [((2, 96, rank), HALF)] * half, [VMEM] * 2, micros=0.1)(keep, msg_a)
    msg, packs = lax.optimization_barrier((msg, packs))
    kept, image, slopes = call(own_kernel, near_outs, [VMEM] * 3, turned_buf)(numbers, msg, target)
    cross = [partner(pack, slot) for slot, pack in enumerate(packs)]
    kept_a, image, slopes = call(side_kernel, near_outs, [VMEM] * 5, turned_buf)(numbers, msg_a, target, image, slopes)
    kept_b, image, slopes = call(side_kernel, near_outs, [VMEM] * 5, turned_buf)(numbers, msg_b, target, image, slopes)
    image, cross = lax.optimization_barrier((image, cross))
    other = [sibling(value) for value in cross]
    couplings = [((half, rank, rank), HALF)] * 2
    image, own_high, own_low = call(
        functools.partial(carried_kernel, half, far_scale), [((32, rows), FULL)] + couplings, [VMEM] * (4 + half), micros=1.0
    )(numbers, image, basis, skel_target, *cross)
    other_high, other_low, row_sum, first, wmsg, keep, beside_msg = call(
        functools.partial(far_kernel, half, far_scale),
        couplings
        + [
            ((1, rows), FULL),
            ((probes, rows), FULL),
            ((2 * probes, rows), HALF),
            ((2 * probes, half * rank), HALF),
            ((2 * probes, rows + half * rank), HALF),
        ],
        [VMEM] * (5 + half),
    )(numbers, image, given, basis, skel_target, *other)
    wmsg_a = sibling(beside_msg)
    wmsg_b = lax.ppermute(wmsg, "loc", across)
    packs = call(pack_kernel, [((2, 2 * probes, rank), HALF)] * half, [VMEM] * 2, micros=0.1)(keep, wmsg_a)
    cross = [partner(pack, slot) for slot, pack in enumerate(packs)]
    (near,) = call(near_kernel, [((2 * probes, rows), FULL)], [VMEM] * 6, micros=1.2)(wmsg, wmsg_a, wmsg_b, kept, kept_a, kept_b)
    other = [sibling(value) for value in cross]
    sums, first_rest, second_rest, shift = call(
        functools.partial(second_kernel, half, far_scale),
        [((count, 128), FULL), ((probes, rows), FULL), ((probes, rows), FULL), ((probes, 128), FULL)],
        [VMEM] * (10 + levels),
    )(near, basis, own_high, own_low, other_high, other_low, row_sum, first, given, slopes, *cross, *other)
    sums, signal, noise_var = lax.optimization_barrier((sums, signal, noise_var))
    table = lax.all_to_all(sums, "loc", 0, 0, tiled=True)
    (slope_image,) = call(slope_kernel, [((probes, rows), FULL)], [SMEM, VMEM, VMEM])(signal, numbers, slopes)
    solution, residual, trace = call(
        functools.partial(last_kernel, float(rows * count)),
        [((probes, rows), FULL), ((probes, rows), FULL), ((1, probes), FULL)],
        [SMEM, SMEM] + [VMEM] * 6,
    )(signal, noise_var, numbers, table, shift, first_rest, second_rest, given)
    return (solution, residual, slope_image, trace.reshape(probes))


def solution(mesh):
    placed = (P(None, "loc"), P(None, "loc"), P(None, "loc"), P(), P(), P(), P())
    return jax.shard_map(
        shards,
        mesh=mesh,
        in_specs=placed,
        out_specs=(P(None, "loc"), P(None, "loc"), P(None, "loc"), P()),
        check_vma=False,
    )
```

```python
import functools

import jax
import jax.numpy as jnp
from jax import lax
from jax.experimental import pallas as pl
from jax.experimental.pallas import tpu as pltpu
from jax.sharding import PartitionSpec as P

HALF = jnp.bfloat16
FULL = jnp.float32
LOG2_E = 1.4426950408889634
ROOT_THREE = 1.7320508075688772
TINY = 1e-30
SCALE = 2.0**-10
SRC_ROWS = 32
MSG_ROWS = 64
VEC_ROWS = 48
TILE = 128
WIDE_TILE = 256
VMEM = pltpu.VMEM
SMEM = pltpu.SMEM


def split_two(value):
    high = value.astype(HALF)
    low = (value - high.astype(FULL)).astype(HALF)
    return high, low


def split_three(value):
    first = value.astype(HALF).astype(FULL)
    rest = value - first
    second = rest.astype(HALF).astype(FULL)
    third = (rest - second).astype(HALF).astype(FULL)
    return first, second, third


def matern(squared, rates):
    rate, falling_rate = rates
    squared = jnp.maximum(squared, TINY)
    radius = squared * lax.rsqrt(squared)
    decay = jnp.exp2(radius * falling_rate)
    falling = radius * decay
    return decay + rate * falling, radius * falling


def excess(pts):
    total = jnp.full((1, pts.shape[1]), -1.0, FULL)
    lost = jnp.zeros_like(total)
    small = jnp.zeros_like(total)
    for axis in range(3):
        value = pts[axis : axis + 1, :]
        head = value.astype(HALF).astype(FULL)
        tail = value - head
        small = small + tail * tail
        for term in (head * head, 2.0 * head * tail):
            grown = total + term
            back = grown - total
            lost = lost + ((total - (grown - back)) + (term - back))
            total = grown
    return total + (lost + small)


def write_rows(buf, base, pts, source):
    over = excess(pts)
    first = over.astype(HALF).astype(FULL)
    second = over - first
    unit = jnp.ones_like(over)
    if source:
        rows = (unit, unit, unit, first, second)
        order = (0, 0, 0, 1, 1, 1, 2, 2, 2)
        pieces = split_three(pts)
    else:
        rows = (unit + unit, first, second, unit, unit)
        order = (0, 1, 2, 0, 1, 2, 0, 1, 2)
        pieces = split_three(-2.0 * pts)
    for slot, row in enumerate(rows):
        buf[base + slot : base + slot + 1, :] = row
    for slot, index in enumerate(order):
        start = base + 5 + 3 * slot
        buf[start : start + 3, :] = pieces[index]


def dot(a, b):
    return jnp.dot(a, b, preferred_element_type=FULL)


def dot_rows(a, b):
    return lax.dot_general(a, b, (((1,), (1,)), ((), ())), preferred_element_type=FULL)


def turned(value):
    return value.astype(FULL).T.astype(HALF)


def merged(both):
    return jnp.concatenate([both[0:16] + both[16:32], both[32:48]], axis=0)


def on_first_core():
    return lax.rem(lax.axis_index("loc"), 2) == 0


def gather_share(keep, got, packs):
    first = on_first_core()
    for slot, pack in enumerate(packs):
        pack[0] = jnp.where(first, keep[slot], got[slot])
        pack[1] = jnp.where(first, got[slot], keep[slot])


def own_part(values):
    first = on_first_core()
    return [jnp.where(first, value[0], value[1]) for value in values]


def front_kernel(levels, *refs):
    length, far_length, given = refs[:3]
    msg, target, basis, skel_target, numbers, keep, beside = refs[3:10]
    buf, pair_buf, turned_src = refs[10:]
    points = given[16:19, :]
    for slot, value in enumerate((length[0], far_length[0])):
        lengths = jnp.full((1, 128), value, FULL)
        numbers[slot : slot + 1, :] = ROOT_THREE / lengths
        numbers[slot + 2 : slot + 3, :] = (-LOG2_E * ROOT_THREE) / lengths
    write_rows(buf, 0, points, False)
    target[...] = buf[...].astype(HALF)
    pair_buf[SRC_ROWS:, :] = buf[...].astype(HALF)
    write_rows(buf, 0, points, True)
    pair_buf[0:SRC_ROWS, :] = buf[...].astype(HALF)
    msg[32:64, :] = buf[...].astype(HALF)
    rows, rank = points.shape[1], skel_target.shape[2]
    first = on_first_core()
    skel = [given[24 + level : 25 + level, 0:rank] for level in range(levels)]
    order = [jnp.where(first, skel[level], skel[level + 1]) for level in range(0, levels, 2)]
    order += [jnp.where(first, skel[level + 1], skel[level]) for level in range(0, levels, 2)]
    spot = lax.broadcasted_iota(jnp.int32, (rows, rank), 0).astype(FULL)
    sources = []
    for level in range(levels):
        picks = jnp.where(spot == order[level], 1.0, 0.0).astype(HALF)
        both = dot(pair_buf[...], picks)
        skel_target[level] = both[SRC_ROWS:].astype(HALF)
        skel_source = both[:SRC_ROWS]
        sources.append(skel_source.astype(HALF))
        turned_src[level * rank : (level + 1) * rank, :] = skel_source.T.astype(HALF)
    rates = [jnp.concatenate([numbers[row : row + 1, :]] * (WIDE_TILE // 128), axis=1) for row in (1, 3)]
    for row in range(0, levels * rank, 1024):
        for col in range(0, rows, WIDE_TILE):
            squared = dot(turned_src[row : row + 1024, :], target[:, col : col + WIDE_TILE])
            basis[row : row + 1024, col : col + WIDE_TILE] = matern(squared, rates)[0].astype(HALF)
    high, low = split_two(given[0:16, :])
    msg[0:16, :] = low
    msg[16:32, :] = high
    coef = merged(dot_rows(msg[0:VEC_ROWS, :], basis[...]))
    for level in range(levels):
        high, low = split_two(coef[:, level * rank : (level + 1) * rank])
        if level < levels // 2:
            keep[level, 0:32, :] = high
            keep[level, 32:64, :] = low
            keep[level, 64:96, :] = sources[level]
        else:
            start = rows + (level - levels // 2) * 2 * rank
            beside[0:32, start : start + rank] = high
            beside[32:64, start : start + rank] = low
            beside[0:32, start + rank : start + 2 * rank] = sources[level]
            beside[32:64, start + rank : start + 2 * rank] = sources[level]
    beside[:, 0:rows] = msg[...]


def near_block(msg, target, turned_src, rates, kept):
    rows = target.shape[1]
    turned_src[...] = turned(msg[32:64, 0:rows])
    for col in range(0, rows, TILE):
        squared = dot(turned_src[...], target[:, col : col + TILE])
        value, slope = matern(squared, rates)
        value = value.astype(HALF)
        kept[:, col : col + TILE] = value
        pair = jnp.concatenate([value, slope.astype(HALF)], axis=1)
        total = dot(msg[0:VEC_ROWS, 0:rows], pair)
        yield slice(col, col + TILE), merged(total[:, :TILE]), total[16:32, TILE:]


def first_pack_kernel(keep, got, *packs):
    rank = keep.shape[2]
    rows = got.shape[1] - 2 * rank * len(packs)
    starts = [rows + 2 * rank * slot for slot in range(len(packs))]
    parts = [(got[:, start : start + rank], got[0:32, start + rank : start + 2 * rank]) for start in starts]
    gather_share(keep, [jnp.concatenate(part, axis=0) for part in parts], packs)


def own_kernel(numbers, msg, target, kept, image, slopes, turned_src):
    rates = numbers[0:1, :], numbers[2:3, :]
    for span, part, slope in near_block(msg, target, turned_src, rates, kept):
        image[:, span] = part
        slopes[:, span] = slope


def side_kernel(numbers, msg, target, image_in, slopes_in, kept, image, slopes, turned_src):
    rates = numbers[0:1, :], numbers[2:3, :]
    for span, part, slope in near_block(msg, target, turned_src, rates, kept):
        image[:, span] = image_in[:, span] + part
        slopes[:, span] = slopes_in[:, span] + slope


def far_part(lev, start, numbers, skel_target, basis, coup_high):
    rank = skel_target.shape[2]
    rates = [jnp.concatenate([numbers[row : row + 1, :]] * (rank // 128), axis=1) for row in (1, 3)]
    mixed = []
    for slot, value in enumerate(lev):
        squared = dot(turned(value[64:96]), skel_target[start + slot])
        high = matern(squared, rates)[0].astype(HALF)
        coup_high[slot] = high
        both = dot(value[0:64], high)
        part = both[0:32] + both[32:64]
        mixed.append(jnp.concatenate(split_two(part), axis=0))
    far = dot(jnp.concatenate(mixed, axis=1), basis[start * rank : (start + len(lev)) * rank, :])
    return far[0:32] + far[32:64]


def carried_kernel(half, far_scale, *refs):
    numbers, image_in, basis, skel_target = refs[:4]
    lev = own_part(refs[4 : 4 + half])
    image, coup_high = refs[4 + half :]
    image[...] = image_in[...] + far_scale * far_part(lev, 0, numbers, skel_target, basis, coup_high)


def far_kernel(half, far_scale, *refs):
    numbers, image, given, basis, skel_target = refs[:5]
    lev = own_part(refs[5 : 5 + half])
    coup_high, row_sum, first, wmsg, keep, beside = refs[5 + half :]
    rank = skel_target.shape[2]
    total = image[...] + far_scale * far_part(lev, half, numbers, skel_target, basis, coup_high)
    sums = total[16:17, :]
    row_sum[...] = sums
    value = SCALE * (total[0:16] + sums * given[0:16, :])
    first[...] = value
    high, low = split_two(value)
    rows = wmsg.shape[1]
    wmsg[0:16, :] = high
    wmsg[16:32, :] = low
    beside[0:16, 0:rows] = high
    beside[16:32, 0:rows] = low
    both = dot_rows(wmsg[...], basis[...])
    high, low = split_two(both[0:16] + both[16:32])
    keep[0:16, :] = high[:, : half * rank]
    keep[16:32, :] = low[:, : half * rank]
    beside[0:16, rows:] = high[:, half * rank :]
    beside[16:32, rows:] = low[:, half * rank :]


def pack_kernel(keep, got, *packs):
    rank = packs[0].shape[2]
    start = got.shape[1] - keep.shape[1]
    spans = [slice(slot * rank, (slot + 1) * rank) for slot in range(len(packs))]
    there = [slice(start + span.start, start + span.stop) for span in spans]
    gather_share([keep[:, span] for span in spans], [got[:, span] for span in there], packs)


def near_kernel(wmsg, wmsg_a, wmsg_b, kept, kept_a, kept_b, out):
    rows = kept_a.shape[0]
    out[...] = dot(wmsg[...], kept[...]) + dot(wmsg_a[:, 0:rows], kept_a[...]) + dot(wmsg_b[...], kept_b[...])


def row_total(a, b):
    return jnp.sum(a * b, axis=1, keepdims=True)


def second_kernel(half, far_scale, *refs):
    near, basis, own_high, other_high, row_sum, first, given, slope_sum = refs[:8]
    wlev = own_part(refs[8 : 8 + 2 * half])
    sums, first_rest, second_rest, shift_out = refs[8 + 2 * half :]
    coup_high = [own_high[slot] for slot in range(half)] + [other_high[slot] for slot in range(half)]
    pieces = []
    for coef, high in zip(wlev, coup_high):
        mixed = dot(coef, high)
        mixed = mixed[0:16] + mixed[16:32]
        pieces.append(jnp.concatenate(split_two(mixed), axis=0))
    both = near[...] + far_scale * dot(jnp.concatenate(pieces, axis=1), basis[...])
    base = given[0:16, :]
    value = first[...]
    image = SCALE * (both[0:16] + both[16:32] + row_sum[...] * value)
    weight = row_total(base, base)
    shift = jnp.where(weight > 0.0, row_total(base, value) / jnp.where(weight > 0.0, weight, 1.0), 0.0)
    value = value - shift * base
    image = image - (2.0 * shift) * value - (shift * shift) * base
    first_rest[...] = value
    second_rest[...] = image
    shift_out[...] = jnp.broadcast_to(shift, shift_out.shape)
    slope = slope_sum[...]
    parts = (
        shift,
        weight,
        row_total(value, value),
        row_total(value, image),
        row_total(base, image),
        row_total(base, value),
        row_total(base, slope),
        row_total(value, slope),
    )
    lane = lax.broadcasted_iota(jnp.int32, (16, 128), 1)
    row = lax.broadcasted_iota(jnp.int32, (16, 128), 0)
    packed = jnp.zeros((16, 128), FULL)
    for slot, part in enumerate(parts):
        packed = jnp.where(lane == row + 16 * slot, part, packed)
    sums[...] = jnp.broadcast_to(jnp.sum(packed, axis=0, keepdims=True), sums.shape)


def last_kernel(point_total, signal, noise, numbers, table, shift_in, first_rest, second_rest, given, out, res, trace):
    gathered = table[...]
    shift = gathered

    def slot(index):
        return pltpu.roll(gathered, 128 - 16 * index, 1)

    weight, ww, wz, rz, rw, rs, ws = (slot(index) for index in range(1, 8))

    def total(value):
        return jnp.sum(value, axis=0, keepdims=True)

    gain = signal[0] / SCALE
    rate = numbers[0:1, :]
    norm = total(weight)
    center = total(shift * weight + rw) / norm
    off = shift - center
    cross = total(rw + off * weight)
    square = total(ww + 2.0 * off * rw + off * off * weight)
    mixed = total(rz + 2.0 * off * rw + off * off * weight)
    second = total(
        wz + 2.0 * off * ww + off * off * rw + off * rz + 2.0 * off * off * rw + off * off * off * weight
    )
    held = total(rs)
    along = total(ws + off * rs)
    cross = gain * cross
    square = (gain * gain) * square
    mixed = (gain * gain) * mixed
    second = (gain * gain) * gain * second
    level = noise[0] + gain * center
    lead = level * norm + cross
    alpha = norm / lead
    part = cross / lead
    norm_next = part * part * norm - 2.0 * part * alpha * cross + alpha * alpha * square
    lean = part + norm_next / norm
    direction = lean * lean * norm - 2.0 * lean * alpha * cross + alpha * alpha * square
    bend = lean * lean * cross - lean * alpha * (mixed + square) + alpha * alpha * second
    beta = norm_next / (level * direction + bend)
    factor = signal[0] * (rate * rate)
    trace[...] = (((alpha + beta * lean) * held - beta * alpha * gain * along) * factor / point_total)[:, 0:16]

    lane = lax.broadcasted_iota(jnp.int32, (16, 128), 1)
    row = lax.broadcasted_iota(jnp.int32, (16, 128), 0)

    def column(value):
        return jnp.sum(jnp.where(lane == row, value, 0.0), axis=1, keepdims=True)

    own_off = shift_in[:, 0:1] - column(center)
    base = given[0:16, :]
    rest = first_rest[...]
    value = rest + own_off * base
    image = second_rest[...] + (2.0 * own_off) * rest + (own_off * own_off) * base
    out[...] = column(alpha + beta * lean) * base - column(beta * alpha * gain) * value
    res[...] = (
        column(part - beta * level * lean) * base
        - column((alpha - beta * level * alpha + beta * lean) * gain) * value
        + column(beta * alpha * gain * gain) * image
    )


def slope_kernel(signal, numbers, source, dest):
    rate = numbers[0:1, 0:1]
    dest[...] = (signal[0] * rate * rate) * source[...]


def call(kernel, outs, spaces, scratch=(), micros=2.0):
    params = pltpu.CompilerParams(vmem_limit_bytes=40 * 2**20)
    cost = pl.CostEstimate(flops=int(micros * 1e9), bytes_accessed=2**16, transcendentals=0)
    return pl.pallas_call(
        kernel,
        out_shape=[jax.ShapeDtypeStruct(shape, kind) for shape, kind in outs],
        in_specs=[pl.BlockSpec(memory_space=space) for space in spaces],
        out_specs=[pl.BlockSpec(memory_space=VMEM) for _ in outs],
        scratch_shapes=list(scratch),
        compiler_params=params,
        cost_estimate=cost,
    )


def shards(points, right_sides, skeleton, lengthscale, far_length, signal, noise_var):
    probes, rows = right_sides.shape
    levels, rank = skeleton.shape
    half = levels // 2
    count = lax.axis_size("loc")
    far_scale = 1.0 / (rank * rank * levels)
    beside = [(i, i ^ 1) for i in range(count)]
    across = [(i, i + 1) for i in range(1, count - 1, 2)]
    across = across + [(j, i) for i, j in across]

    def partner(value, slot):
        pairs = [(i, i ^ (2 << (2 * slot + i % 2))) for i in range(count)]
        return lax.ppermute(value, "loc", pairs)

    def sibling(value):
        return lax.ppermute(value, "loc", beside)

    height = -(-(24 + levels) // 8) * 8
    given = jnp.pad(right_sides, ((0, height - probes), (0, 0)))
    given += jnp.pad(points, ((16, height - 19), (0, 0)))
    given += jnp.pad(skeleton, ((24, height - 24 - levels), (0, rows - rank))).astype(FULL)
    msg, target, basis, skel_target, numbers, keep, beside_msg = call(
        functools.partial(front_kernel, levels),
        [
            ((MSG_ROWS, rows), HALF),
            ((SRC_ROWS, rows), HALF),
            ((levels * rank, rows), HALF),
            ((levels, SRC_ROWS, rank), HALF),
            ((8, 128), FULL),
            ((half, 96, rank), HALF),
            ((MSG_ROWS, rows + 2 * half * rank), HALF),
        ],
        [SMEM, SMEM, VMEM],
        [
            VMEM((SRC_ROWS, rows), FULL),
            VMEM((2 * SRC_ROWS, rows), HALF),
            VMEM((levels * rank, SRC_ROWS), HALF),
        ],
    )(lengthscale, far_length, given)
    msg_a = sibling(beside_msg)
    msg_b = lax.ppermute(msg, "loc", across)
    near_outs = [((rows, rows), HALF), ((32, rows), FULL), ((probes, rows), FULL)]
    turned_buf = [VMEM((rows, SRC_ROWS), HALF)]
    packs = call(first_pack_kernel, [((2, 96, rank), HALF)] * half, [VMEM] * 2, micros=0.1)(keep, msg_a)
    msg, packs = lax.optimization_barrier((msg, packs))
    kept, image, slopes = call(own_kernel, near_outs, [VMEM] * 3, turned_buf)(numbers, msg, target)
    cross = [partner(pack, slot) for slot, pack in enumerate(packs)]
    kept_a, image, slopes = call(side_kernel, near_outs, [VMEM] * 5, turned_buf)(numbers, msg_a, target, image, slopes)
    kept_b, image, slopes = call(side_kernel, near_outs, [VMEM] * 5, turned_buf)(numbers, msg_b, target, image, slopes)
    image, cross = lax.optimization_barrier((image, cross))
    other = [sibling(value) for value in cross]
    couplings = [((half, rank, rank), HALF)]
    image, own_high = call(
        functools.partial(carried_kernel, half, far_scale), [((32, rows), FULL)] + couplings, [VMEM] * (4 + half), micros=1.0
    )(numbers, image, basis, skel_target, *cross)
    other_high, row_sum, first, wmsg, keep, beside_msg = call(
        functools.partial(far_kernel, half, far_scale),
        couplings
        + [
            ((1, rows), FULL),
            ((probes, rows), FULL),
            ((2 * probes, rows), HALF),
            ((2 * probes, half * rank), HALF),
            ((2 * probes, rows + half * rank), HALF),
        ],
        [VMEM] * (5 + half),
    )(numbers, image, given, basis, skel_target, *other)
    wmsg_a = sibling(beside_msg)
    wmsg_b = lax.ppermute(wmsg, "loc", across)
    packs = call(pack_kernel, [((2, 2 * probes, rank), HALF)] * half, [VMEM] * 2, micros=0.1)(keep, wmsg_a)
    cross = [partner(pack, slot) for slot, pack in enumerate(packs)]
    (near,) = call(near_kernel, [((2 * probes, rows), FULL)], [VMEM] * 6, micros=1.2)(wmsg, wmsg_a, wmsg_b, kept, kept_a, kept_b)
    other = [sibling(value) for value in cross]
    sums, first_rest, second_rest, shift = call(
        functools.partial(second_kernel, half, far_scale),
        [((count, 128), FULL), ((probes, rows), FULL), ((probes, rows), FULL), ((probes, 128), FULL)],
        [VMEM] * (8 + levels),
    )(near, basis, own_high, other_high, row_sum, first, given, slopes, *cross, *other)
    sums, signal, noise_var = lax.optimization_barrier((sums, signal, noise_var))
    table = lax.all_to_all(sums, "loc", 0, 0, tiled=True)
    (slope_image,) = call(slope_kernel, [((probes, rows), FULL)], [SMEM, VMEM, VMEM])(signal, numbers, slopes)
    solution, residual, trace = call(
        functools.partial(last_kernel, float(rows * count)),
        [((probes, rows), FULL), ((probes, rows), FULL), ((1, probes), FULL)],
        [SMEM, SMEM] + [VMEM] * 6,
    )(signal, noise_var, numbers, table, shift, first_rest, second_rest, given)
    return (solution, residual, slope_image, trace.reshape(probes))


def solution(mesh):
    placed = (P(None, "loc"), P(None, "loc"), P(None, "loc"), P(), P(), P(), P())
    return jax.shard_map(
        shards,
        mesh=mesh,
        in_specs=placed,
        out_specs=(P(None, "loc"), P(None, "loc"), P(None, "loc"), P()),
        check_vma=False,
    )
```

```python
import functools

import jax
import jax.numpy as jnp
from jax import lax
from jax.experimental import pallas as pl
from jax.experimental.pallas import tpu as pltpu
from jax.sharding import PartitionSpec as P

HALF = jnp.bfloat16
FULL = jnp.float32
LOG2_E = 1.4426950408889634
ROOT_THREE = 1.7320508075688772
TINY = 1e-30
SCALE = 2.0**-10
SRC_ROWS = 32
MSG_ROWS = 64
VEC_ROWS = 48
TILE = 128
WIDE_TILE = 256
VMEM = pltpu.VMEM
SMEM = pltpu.SMEM


def split_two(value):
    high = value.astype(HALF)
    low = (value - high.astype(FULL)).astype(HALF)
    return high, low


def split_three(value):
    first = value.astype(HALF).astype(FULL)
    rest = value - first
    second = rest.astype(HALF).astype(FULL)
    third = (rest - second).astype(HALF).astype(FULL)
    return first, second, third


def matern(squared, rates, packed=False):
    rate, falling_rate = rates
    squared = jnp.maximum(squared, TINY)
    radius = squared * lax.rsqrt(squared)
    decay = jnp.exp2(radius * falling_rate)
    if packed:
        scaled = (radius * rate).astype(HALF)
        decay = decay.astype(HALF)
        falling = scaled * decay
        return decay + falling, scaled * falling
    falling = radius * decay
    return decay + rate * falling, radius * falling


def excess(pts):
    total = jnp.full((1, pts.shape[1]), -1.0, FULL)
    lost = jnp.zeros_like(total)
    small = jnp.zeros_like(total)
    for axis in range(3):
        value = pts[axis : axis + 1, :]
        head = value.astype(HALF).astype(FULL)
        tail = value - head
        small = small + tail * tail
        for term in (head * head, 2.0 * head * tail):
            grown = total + term
            back = grown - total
            lost = lost + ((total - (grown - back)) + (term - back))
            total = grown
    return total + (lost + small)


def write_rows(buf, base, pts, source):
    over = excess(pts)
    first = over.astype(HALF).astype(FULL)
    second = over - first
    unit = jnp.ones_like(over)
    if source:
        rows = (unit, unit, unit, first, second)
        order = (0, 0, 0, 1, 1, 1, 2, 2, 2)
        pieces = split_three(pts)
    else:
        rows = (unit + unit, first, second, unit, unit)
        order = (0, 1, 2, 0, 1, 2, 0, 1, 2)
        pieces = split_three(-2.0 * pts)
    for slot, row in enumerate(rows):
        buf[base + slot : base + slot + 1, :] = row
    for slot, index in enumerate(order):
        start = base + 5 + 3 * slot
        buf[start : start + 3, :] = pieces[index]


def dot(a, b):
    return jnp.dot(a, b, preferred_element_type=FULL)


def dot_rows(a, b):
    return lax.dot_general(a, b, (((1,), (1,)), ((), ())), preferred_element_type=FULL)


def turned(value):
    return value.astype(FULL).T.astype(HALF)


def merged(both):
    return jnp.concatenate([both[0:16] + both[16:32], both[32:48]], axis=0)


def on_first_core():
    return lax.rem(lax.axis_index("loc"), 2) == 0


def gather_share(keep, got, packs):
    first = on_first_core()
    for slot, pack in enumerate(packs):
        pack[0] = jnp.where(first, keep[slot], got[slot])
        pack[1] = jnp.where(first, got[slot], keep[slot])


def own_part(values):
    first = on_first_core()
    return [jnp.where(first, value[0], value[1]) for value in values]


def front_kernel(levels, *refs):
    length, far_length, given = refs[:3]
    msg, target, basis, skel_target, numbers, keep, beside = refs[3:10]
    buf, pair_buf, turned_src = refs[10:]
    points = given[16:19, :]
    for slot, value in enumerate((length[0], far_length[0])):
        lengths = jnp.full((1, 128), value, FULL)
        numbers[slot : slot + 1, :] = ROOT_THREE / lengths
        numbers[slot + 2 : slot + 3, :] = (-LOG2_E * ROOT_THREE) / lengths
    write_rows(buf, 0, points, False)
    target[...] = buf[...].astype(HALF)
    pair_buf[SRC_ROWS:, :] = buf[...].astype(HALF)
    write_rows(buf, 0, points, True)
    pair_buf[0:SRC_ROWS, :] = buf[...].astype(HALF)
    msg[32:64, :] = buf[...].astype(HALF)
    rows, rank = points.shape[1], skel_target.shape[2]
    first = on_first_core()
    skel = [given[24 + level : 25 + level, 0:rank] for level in range(levels)]
    order = [jnp.where(first, skel[level], skel[level + 1]) for level in range(0, levels, 2)]
    order += [jnp.where(first, skel[level + 1], skel[level]) for level in range(0, levels, 2)]
    spot = lax.broadcasted_iota(jnp.int32, (rows, rank), 0).astype(FULL)
    sources = []
    for level in range(levels):
        picks = jnp.where(spot == order[level], 1.0, 0.0).astype(HALF)
        both = dot(pair_buf[...], picks)
        skel_target[level] = both[SRC_ROWS:].astype(HALF)
        skel_source = both[:SRC_ROWS]
        sources.append(skel_source.astype(HALF))
        turned_src[level * rank : (level + 1) * rank, :] = skel_source.T.astype(HALF)
    rates = [jnp.concatenate([numbers[row : row + 1, :]] * (WIDE_TILE // 128), axis=1) for row in (1, 3)]
    for row in range(0, levels * rank, 1024):
        for col in range(0, rows, WIDE_TILE):
            squared = dot(turned_src[row : row + 1024, :], target[:, col : col + WIDE_TILE])
            basis[row : row + 1024, col : col + WIDE_TILE] = matern(squared, rates)[0].astype(HALF)
    high, low = split_two(given[0:16, :])
    msg[0:16, :] = low
    msg[16:32, :] = high
    coef = merged(dot_rows(msg[0:VEC_ROWS, :], basis[...]))
    for level in range(levels):
        high, low = split_two(coef[:, level * rank : (level + 1) * rank])
        if level < levels // 2:
            keep[level, 0:32, :] = high
            keep[level, 32:64, :] = low
            keep[level, 64:96, :] = sources[level]
        else:
            start = rows + (level - levels // 2) * 2 * rank
            beside[0:32, start : start + rank] = high
            beside[32:64, start : start + rank] = low
            beside[0:32, start + rank : start + 2 * rank] = sources[level]
            beside[32:64, start + rank : start + 2 * rank] = sources[level]
    beside[:, 0:rows] = msg[...]


def near_block(msg, target, turned_src, rates, kept):
    rows = target.shape[1]
    turned_src[...] = turned(msg[32:64, 0:rows])
    for col in range(0, rows, TILE):
        squared = dot(turned_src[...], target[:, col : col + TILE])
        value, slope = matern(squared, rates, True)
        value = value.astype(HALF)
        kept[:, col : col + TILE] = value
        pair = jnp.concatenate([value, slope.astype(HALF)], axis=1)
        total = dot(msg[0:VEC_ROWS, 0:rows], pair)
        yield slice(col, col + TILE), merged(total[:, :TILE]), total[16:32, TILE:]


def first_pack_kernel(keep, got, *packs):
    rank = keep.shape[2]
    rows = got.shape[1] - 2 * rank * len(packs)
    starts = [rows + 2 * rank * slot for slot in range(len(packs))]
    parts = [(got[:, start : start + rank], got[0:32, start + rank : start + 2 * rank]) for start in starts]
    gather_share(keep, [jnp.concatenate(part, axis=0) for part in parts], packs)


def own_kernel(numbers, msg, target, kept, image, slopes, turned_src):
    rates = numbers[0:1, :], numbers[2:3, :]
    for span, part, slope in near_block(msg, target, turned_src, rates, kept):
        image[:, span] = part
        slopes[:, span] = slope


def side_kernel(numbers, msg, target, image_in, slopes_in, kept, image, slopes, turned_src):
    rates = numbers[0:1, :], numbers[2:3, :]
    for span, part, slope in near_block(msg, target, turned_src, rates, kept):
        image[:, span] = image_in[:, span] + part
        slopes[:, span] = slopes_in[:, span] + slope


def far_part(lev, start, numbers, skel_target, basis, coup_high):
    rank = skel_target.shape[2]
    rates = [jnp.concatenate([numbers[row : row + 1, :]] * (rank // 128), axis=1) for row in (1, 3)]
    mixed = []
    for slot, value in enumerate(lev):
        squared = dot(turned(value[64:96]), skel_target[start + slot])
        high = matern(squared, rates)[0].astype(HALF)
        coup_high[slot] = high
        both = dot(value[0:64], high)
        part = both[0:32] + both[32:64]
        mixed.append(jnp.concatenate(split_two(part), axis=0))
    far = dot(jnp.concatenate(mixed, axis=1), basis[start * rank : (start + len(lev)) * rank, :])
    return far[0:32] + far[32:64]


def carried_kernel(half, far_scale, *refs):
    numbers, image_in, basis, skel_target = refs[:4]
    lev = own_part(refs[4 : 4 + half])
    image, coup_high = refs[4 + half :]
    image[...] = image_in[...] + far_scale * far_part(lev, 0, numbers, skel_target, basis, coup_high)


def far_kernel(half, far_scale, *refs):
    numbers, image, given, basis, skel_target = refs[:5]
    lev = own_part(refs[5 : 5 + half])
    coup_high, row_sum, first, wmsg, keep, beside = refs[5 + half :]
    rank = skel_target.shape[2]
    total = image[...] + far_scale * far_part(lev, half, numbers, skel_target, basis, coup_high)
    sums = total[16:17, :]
    row_sum[...] = sums
    value = SCALE * (total[0:16] + sums * given[0:16, :])
    first[...] = value
    high, low = split_two(value)
    rows = wmsg.shape[1]
    wmsg[0:16, :] = high
    wmsg[16:32, :] = low
    beside[0:16, 0:rows] = high
    beside[16:32, 0:rows] = low
    both = dot_rows(wmsg[...], basis[...])
    high, low = split_two(both[0:16] + both[16:32])
    keep[0:16, :] = high[:, : half * rank]
    keep[16:32, :] = low[:, : half * rank]
    beside[0:16, rows:] = high[:, half * rank :]
    beside[16:32, rows:] = low[:, half * rank :]


def pack_kernel(keep, got, *packs):
    rank = packs[0].shape[2]
    start = got.shape[1] - keep.shape[1]
    spans = [slice(slot * rank, (slot + 1) * rank) for slot in range(len(packs))]
    there = [slice(start + span.start, start + span.stop) for span in spans]
    gather_share([keep[:, span] for span in spans], [got[:, span] for span in there], packs)


def near_kernel(wmsg, wmsg_a, wmsg_b, kept, kept_a, kept_b, out):
    rows = kept_a.shape[0]
    out[...] = dot(wmsg[...], kept[...]) + dot(wmsg_a[:, 0:rows], kept_a[...]) + dot(wmsg_b[...], kept_b[...])


def row_total(a, b):
    return jnp.sum(a * b, axis=1, keepdims=True)


def second_kernel(half, far_scale, *refs):
    near, basis, own_high, other_high, row_sum, first, given, slope_sum = refs[:8]
    wlev = own_part(refs[8 : 8 + 2 * half])
    sums, first_rest, second_rest, shift_out = refs[8 + 2 * half :]
    coup_high = [own_high[slot] for slot in range(half)] + [other_high[slot] for slot in range(half)]
    pieces = []
    for coef, high in zip(wlev, coup_high):
        mixed = dot(coef, high)
        mixed = mixed[0:16] + mixed[16:32]
        pieces.append(jnp.concatenate(split_two(mixed), axis=0))
    both = near[...] + far_scale * dot(jnp.concatenate(pieces, axis=1), basis[...])
    base = given[0:16, :]
    value = first[...]
    image = SCALE * (both[0:16] + both[16:32] + row_sum[...] * value)
    weight = row_total(base, base)
    shift = jnp.where(weight > 0.0, row_total(base, value) / jnp.where(weight > 0.0, weight, 1.0), 0.0)
    value = value - shift * base
    image = image - (2.0 * shift) * value - (shift * shift) * base
    first_rest[...] = value
    second_rest[...] = image
    shift_out[...] = jnp.broadcast_to(shift, shift_out.shape)
    slope = slope_sum[...]
    parts = (
        shift,
        weight,
        row_total(value, value),
        row_total(value, image),
        row_total(base, image),
        row_total(base, value),
        row_total(base, slope),
        row_total(value, slope),
    )
    lane = lax.broadcasted_iota(jnp.int32, (16, 128), 1)
    row = lax.broadcasted_iota(jnp.int32, (16, 128), 0)
    packed = jnp.zeros((16, 128), FULL)
    for slot, part in enumerate(parts):
        packed = jnp.where(lane == row + 16 * slot, part, packed)
    sums[...] = jnp.broadcast_to(jnp.sum(packed, axis=0, keepdims=True), sums.shape)


def last_kernel(point_total, signal, noise, numbers, table, shift_in, first_rest, second_rest, given, out, res, trace):
    gathered = table[...]
    shift = gathered

    def slot(index):
        return pltpu.roll(gathered, 128 - 16 * index, 1)

    weight, ww, wz, rz, rw, rs, ws = (slot(index) for index in range(1, 8))

    def total(value):
        return jnp.sum(value, axis=0, keepdims=True)

    gain = signal[0] / SCALE
    rate = numbers[0:1, :]
    norm = total(weight)
    center = total(shift * weight + rw) / norm
    off = shift - center
    cross = total(rw + off * weight)
    square = total(ww + 2.0 * off * rw + off * off * weight)
    mixed = total(rz + 2.0 * off * rw + off * off * weight)
    second = total(
        wz + 2.0 * off * ww + off * off * rw + off * rz + 2.0 * off * off * rw + off * off * off * weight
    )
    held = total(rs)
    along = total(ws + off * rs)
    cross = gain * cross
    square = (gain * gain) * square
    mixed = (gain * gain) * mixed
    second = (gain * gain) * gain * second
    level = noise[0] + gain * center
    lead = level * norm + cross
    alpha = norm / lead
    part = cross / lead
    norm_next = part * part * norm - 2.0 * part * alpha * cross + alpha * alpha * square
    lean = part + norm_next / norm
    direction = lean * lean * norm - 2.0 * lean * alpha * cross + alpha * alpha * square
    bend = lean * lean * cross - lean * alpha * (mixed + square) + alpha * alpha * second
    beta = norm_next / (level * direction + bend)
    factor = signal[0]
    trace[...] = (((alpha + beta * lean) * held - beta * alpha * gain * along) * factor / point_total)[:, 0:16]

    lane = lax.broadcasted_iota(jnp.int32, (16, 128), 1)
    row = lax.broadcasted_iota(jnp.int32, (16, 128), 0)

    def column(value):
        return jnp.sum(jnp.where(lane == row, value, 0.0), axis=1, keepdims=True)

    own_off = shift_in[:, 0:1] - column(center)
    base = given[0:16, :]
    rest = first_rest[...]
    value = rest + own_off * base
    image = second_rest[...] + (2.0 * own_off) * rest + (own_off * own_off) * base
    out[...] = column(alpha + beta * lean) * base - column(beta * alpha * gain) * value
    res[...] = (
        column(part - beta * level * lean) * base
        - column((alpha - beta * level * alpha + beta * lean) * gain) * value
        + column(beta * alpha * gain * gain) * image
    )


def slope_kernel(signal, numbers, source, dest):
    dest[...] = signal[0] * source[...]


def call(kernel, outs, spaces, scratch=(), micros=2.0):
    params = pltpu.CompilerParams(vmem_limit_bytes=40 * 2**20)
    cost = pl.CostEstimate(flops=int(micros * 1e9), bytes_accessed=2**16, transcendentals=0)
    return pl.pallas_call(
        kernel,
        out_shape=[jax.ShapeDtypeStruct(shape, kind) for shape, kind in outs],
        in_specs=[pl.BlockSpec(memory_space=space) for space in spaces],
        out_specs=[pl.BlockSpec(memory_space=VMEM) for _ in outs],
        scratch_shapes=list(scratch),
        compiler_params=params,
        cost_estimate=cost,
    )


def shards(points, right_sides, skeleton, lengthscale, far_length, signal, noise_var):
    probes, rows = right_sides.shape
    levels, rank = skeleton.shape
    half = levels // 2
    count = lax.axis_size("loc")
    far_scale = 1.0 / (rank * rank * levels)
    beside = [(i, i ^ 1) for i in range(count)]
    across = [(i, i + 1) for i in range(1, count - 1, 2)]
    across = across + [(j, i) for i, j in across]

    def partner(value, slot):
        pairs = [(i, i ^ (2 << (2 * slot + i % 2))) for i in range(count)]
        return lax.ppermute(value, "loc", pairs)

    def sibling(value):
        return lax.ppermute(value, "loc", beside)

    height = -(-(24 + levels) // 8) * 8
    given = jnp.pad(right_sides, ((0, height - probes), (0, 0)))
    given += jnp.pad(points, ((16, height - 19), (0, 0)))
    given += jnp.pad(skeleton, ((24, height - 24 - levels), (0, rows - rank))).astype(FULL)
    msg, target, basis, skel_target, numbers, keep, beside_msg = call(
        functools.partial(front_kernel, levels),
        [
            ((MSG_ROWS, rows), HALF),
            ((SRC_ROWS, rows), HALF),
            ((levels * rank, rows), HALF),
            ((levels, SRC_ROWS, rank), HALF),
            ((8, 128), FULL),
            ((half, 96, rank), HALF),
            ((MSG_ROWS, rows + 2 * half * rank), HALF),
        ],
        [SMEM, SMEM, VMEM],
        [
            VMEM((SRC_ROWS, rows), FULL),
            VMEM((2 * SRC_ROWS, rows), HALF),
            VMEM((levels * rank, SRC_ROWS), HALF),
        ],
    )(lengthscale, far_length, given)
    msg_a = sibling(beside_msg)
    msg_b = lax.ppermute(msg, "loc", across)
    near_outs = [((rows, rows), HALF), ((32, rows), FULL), ((probes, rows), FULL)]
    turned_buf = [VMEM((rows, SRC_ROWS), HALF)]
    packs = call(first_pack_kernel, [((2, 96, rank), HALF)] * half, [VMEM] * 2, micros=0.1)(keep, msg_a)
    msg, packs = lax.optimization_barrier((msg, packs))
    kept, image, slopes = call(own_kernel, near_outs, [VMEM] * 3, turned_buf)(numbers, msg, target)
    cross = [partner(pack, slot) for slot, pack in enumerate(packs)]
    kept_a, image, slopes = call(side_kernel, near_outs, [VMEM] * 5, turned_buf)(numbers, msg_a, target, image, slopes)
    kept_b, image, slopes = call(side_kernel, near_outs, [VMEM] * 5, turned_buf)(numbers, msg_b, target, image, slopes)
    image, cross = lax.optimization_barrier((image, cross))
    other = [sibling(value) for value in cross]
    couplings = [((half, rank, rank), HALF)]
    image, own_high = call(
        functools.partial(carried_kernel, half, far_scale), [((32, rows), FULL)] + couplings, [VMEM] * (4 + half), micros=1.0
    )(numbers, image, basis, skel_target, *cross)
    other_high, row_sum, first, wmsg, keep, beside_msg = call(
        functools.partial(far_kernel, half, far_scale),
        couplings
        + [
            ((1, rows), FULL),
            ((probes, rows), FULL),
            ((2 * probes, rows), HALF),
            ((2 * probes, half * rank), HALF),
            ((2 * probes, rows + half * rank), HALF),
        ],
        [VMEM] * (5 + half),
    )(numbers, image, given, basis, skel_target, *other)
    wmsg_a = sibling(beside_msg)
    wmsg_b = lax.ppermute(wmsg, "loc", across)
    packs = call(pack_kernel, [((2, 2 * probes, rank), HALF)] * half, [VMEM] * 2, micros=0.1)(keep, wmsg_a)
    cross = [partner(pack, slot) for slot, pack in enumerate(packs)]
    (near,) = call(near_kernel, [((2 * probes, rows), FULL)], [VMEM] * 6, micros=1.2)(wmsg, wmsg_a, wmsg_b, kept, kept_a, kept_b)
    other = [sibling(value) for value in cross]
    sums, first_rest, second_rest, shift = call(
        functools.partial(second_kernel, half, far_scale),
        [((count, 128), FULL), ((probes, rows), FULL), ((probes, rows), FULL), ((probes, 128), FULL)],
        [VMEM] * (8 + levels),
    )(near, basis, own_high, other_high, row_sum, first, given, slopes, *cross, *other)
    sums, signal, noise_var = lax.optimization_barrier((sums, signal, noise_var))
    table = lax.all_to_all(sums, "loc", 0, 0, tiled=True)
    (slope_image,) = call(slope_kernel, [((probes, rows), FULL)], [SMEM, VMEM, VMEM])(signal, numbers, slopes)
    solution, residual, trace = call(
        functools.partial(last_kernel, float(rows * count)),
        [((probes, rows), FULL), ((probes, rows), FULL), ((1, probes), FULL)],
        [SMEM, SMEM] + [VMEM] * 6,
    )(signal, noise_var, numbers, table, shift, first_rest, second_rest, given)
    return (solution, residual, slope_image, trace.reshape(probes))


def solution(mesh):
    placed = (P(None, "loc"), P(None, "loc"), P(None, "loc"), P(), P(), P(), P())
    return jax.shard_map(
        shards,
        mesh=mesh,
        in_specs=placed,
        out_specs=(P(None, "loc"), P(None, "loc"), P(None, "loc"), P()),
        check_vma=False,
    )
```
